32 devices in a mesh: rep: 8 (over z, y), grp: 4 (over x, core).
Axes of the slice: x: 2, y: 2, z: 4, core: 2. Of those that a mesh axis runs over, the one named last changes fastest.
Arguments:
- layer_input: bfloat16 [8, 1536, 1024], P('rep', 'grp'), may hold values from -4 to 4
- branch: int32 [8, 2], P('rep'), may hold values from 192 to 768, as said below
- attention_gain: bfloat16 [1024], P('grp'), may hold values from 0.5 to 1.5
- factor_weight: bfloat16 [1024, 800], P('grp'), may hold values from -0.3125 to 0.3125
- output_weight: bfloat16 [1024, 1024], P('grp'), may hold values from -0.375 to 0.375
- feed_gain: bfloat16 [1024], P('grp'), may hold values from 0.5 to 1.5
- gate_weight: bfloat16 [1024, 2816], P('grp'), may hold values from -0.1875 to 0.1875
- up_weight: bfloat16 [1024, 2816], P('grp'), may hold values from -0.1875 to 0.1875
- down_weight: bfloat16 [2816, 1024], P('grp'), may hold values from -0.109375 to 0.109375
- cotangent: bfloat16 [8, 1536, 1024], P('rep', 'grp'), may hold values from -4 to 4
Outputs:
- layer_output: bfloat16 [8, 1536, 1024], P('rep', 'grp')
- input_grad: float32 [8, 1536, 1024], P('rep', 'grp')
- attention_gain_grad: float32 [1024], P('grp')
- factor_weight_grad: float32 [1024, 800], P('grp')
- output_weight_grad: float32 [1024, 1024], P('grp')
- feed_gain_grad: float32 [1024], P('grp')
- gate_weight_grad: float32 [1024, 2816], P('grp')
- up_weight_grad: float32 [1024, 2816], P('grp')
- down_weight_grad: float32 [2816, 1024], P('grp')
The draws below stay inside these ranges and needn't reach their ends.
Inputs may be any that keep to these rules, and one draw needn't show every extreme that they name: Continuation c of group g follows the first branch[g, c] prompt tokens; in every group one continuation follows all 768.
All inputs are finite; a program needn't handle non-finite values.
Results may differ from the reference program's by a relative error of at most 0.024.
The reference program's roundings to bfloat16 on the way count: a program that leaves them out, or rounds other values in their place, can miss the bound.
Values may be sent and summed in bfloat16 or wider, within the bound.
No kernel may reach another device: no remote copies, remote signals or barrier semaphores. Data moves between devices by JAX's collectives and lax.ppermute only.
A program may use at most 128 MiB of HBM per device.

```python
import jax
import jax.numpy as jnp
from jax import lax

D = 1024
HEADS = 16
HDIM = 64
QRANK = 6
KRANK = 2
FF = 2816
TOK_DEV = 384
GROUPS = 8
GTOK = 1536
PLEN = 768
NCONT = 2
FAC = 800


def draw_branch(key, part):
    first_key, second_key = jax.random.split(jax.random.fold_in(key, 17))
    lengths = jax.random.randint(first_key, (GROUPS, NCONT), PLEN // 4, PLEN + 1)
    full_place = jax.random.randint(second_key, (GROUPS, 1), 0, NCONT)
    return jnp.where(jnp.arange(NCONT)[None, :] == full_place, PLEN, lengths).astype(jnp.int32)


def level_of(own_key, dims, cuts, smallest, high):
    loudness, own = 1.0, jax.random.fold_in(own_key, 6)
    for dim, shards_of in cuts:
        steps = jnp.exp(jax.random.uniform(jax.random.fold_in(own, dim), (shards_of,), jnp.float32, smallest / len(cuts), high / len(cuts)))
        loudness = loudness * jnp.repeat(steps, dims[dim] // shards_of).reshape([-1 if axis == dim else 1 for axis in range(len(dims))])
    return loudness


def bell_draw(rng, extent, width, most, cuts=(), kind=jnp.bfloat16):
    factor_of = level_of(rng, extent, cuts, -0.22, 0.18) if cuts else 1.0
    values = jax.random.normal(rng, extent, jnp.float32) * width * factor_of
    return jnp.minimum(jnp.maximum(values, -most), most).astype(kind)


def setup_inputs(seed: int = 0) -> dict:
    arg_keys = jax.random.split(jax.random.key(seed), 11)
    layer_input = bell_draw(arg_keys[0], (GROUPS, GTOK, D), 1.0, 4.0, ((0, 8), (1, 4)))
    branch = draw_branch(jax.random.fold_in(arg_keys[10], 71), 0)
    attention_gain = jnp.clip(1.0 + 0.1 * jax.random.normal(arg_keys[2], (D,), jnp.float32), 0.5, 1.5).astype(jnp.bfloat16)
    factor_weight = bell_draw(arg_keys[3], (D, FAC), (2 * D // 5) ** -0.5, 0.3125, ((0, 4),))
    output_weight = bell_draw(arg_keys[4], (HEADS * HDIM, D), (D // 4) ** -0.5, 0.375, ((0, 4),))
    feed_gain = jnp.clip(1.0 + 0.1 * jax.random.normal(arg_keys[5], (D,), jnp.float32), 0.5, 1.5).astype(jnp.bfloat16)
    gate_weight = bell_draw(arg_keys[6], (D, FF), D ** -0.5, 0.1875, ((0, 4),))
    up_weight = bell_draw(arg_keys[7], (D, FF), D ** -0.5, 0.1875, ((0, 4),))
    down_weight = bell_draw(arg_keys[8], (FF, D), FF ** -0.5, 0.109375, ((0, 4),))
    cotangent = bell_draw(arg_keys[9], (GROUPS, GTOK, D), 1.0, 4.0, ((0, 8), (1, 4)))
    return dict(layer_input=layer_input, branch=branch, attention_gain=attention_gain, factor_weight=factor_weight, output_weight=output_weight, feed_gain=feed_gain, gate_weight=gate_weight, up_weight=up_weight, down_weight=down_weight, cotangent=cotangent)


@jax.custom_vjp
def low(v):
    return lax.optimization_barrier(v.astype(jnp.bfloat16)).astype(jnp.float32)

@jax.custom_vjp
def low_back(v):
    return v

def low_keep(v):
    return (low(v), None)

def low_pass(kept, grad):
    return (grad,)

def back_keep(v):
    return (v, None)

def back_low(kept, grad):
    return (low(grad),)
low.defvjp(low_keep, low_pass)
low_back.defvjp(back_keep, back_low)
highest = lax.Precision.HIGHEST

def product(left_side, right_side):
    return jnp.dot(left_side, right_side, precision=highest, preferred_element_type=jnp.float32)

def rms_norm(values, gain_vector):
    return values * lax.rsqrt(lax.optimization_barrier(jnp.mean(values * values, axis=-1, keepdims=True)) + 1e-05) * gain_vector

def angles(positions, half_width):
    freqs = 10000.0 ** (-jnp.arange(half_width).astype(jnp.float32) / half_width)
    phase = positions.astype(jnp.float32)[:, None] * freqs[None, :]
    return (jnp.cos(phase), jnp.sin(phase))

def rotate(matrix, cosine, sine, ranks):
    half_cols = matrix.shape[1] // (2 * ranks)
    pieces = matrix.reshape(matrix.shape[0], ranks, 2, half_cols)
    first_half = pieces[:, :, 0]
    second_half = pieces[:, :, 1]
    cos_wide = cosine[:, None, :]
    sin_wide = sine[:, None, :]
    turned = jnp.stack([first_half * cos_wide - second_half * sin_wide, second_half * cos_wide + first_half * sin_wide], axis=2)
    return turned.reshape(matrix.shape)

def cut_points():
    first_cut = QRANK * HEADS
    second_cut = first_cut + QRANK * HDIM
    third_cut = second_cut + KRANK * HEADS
    fourth_cut = third_cut + KRANK * HDIM
    fifth_cut = fourth_cut + KRANK * HEADS
    return (first_cut, second_cut, third_cut, fourth_cut, fifth_cut)

def turn_factors(values, cosine, sine):
    cuts = cut_points()
    return jnp.concatenate([values[:, :cuts[0]], rotate(values[:, cuts[0]:cuts[1]], cosine, sine, QRANK), values[:, cuts[1]:cuts[2]], rotate(values[:, cuts[2]:cuts[3]], cosine, sine, KRANK), values[:, cuts[3]:]], axis=1)

def expand(head_part, dim_part, ranks):
    tokens_here = head_part.shape[0]
    left_factor = head_part.reshape(tokens_here, ranks, HEADS)
    right_factor = dim_part.reshape(tokens_here, ranks, HDIM)
    return jnp.einsum('nrh,nrd->nhd', left_factor, right_factor, precision=highest) / ranks

def geometry(table):
    index = jnp.arange(GTOK).astype(jnp.int32)
    inside = index < PLEN
    segment = jnp.where(inside, -1, (index - PLEN) // TOK_DEV).astype(jnp.int32)
    chosen = table[jnp.maximum(segment, 0)]
    position = jnp.where(inside, index, chosen + (index - PLEN) % TOK_DEV)
    limit = jnp.where(inside, 0, chosen)
    return (index, segment, position, limit)

def residual_block(inputs, attention_gain, factor_weight, output_weight, feed_gain, gate_weight, up_weight, down_weight, index, segment, position, limit):
    hidden_one = low(rms_norm(inputs, attention_gain))
    raw_factors = low_back(product(hidden_one, factor_weight))
    cosine, sine = angles(position, HDIM // 2)
    factors = low(turn_factors(raw_factors, cosine, sine))
    cuts = cut_points()
    queries = low(expand(factors[:, :cuts[0]], factors[:, cuts[0]:cuts[1]], QRANK))
    keys_all = low(expand(factors[:, cuts[1]:cuts[2]], factors[:, cuts[2]:cuts[3]], KRANK))
    values_all = low(expand(factors[:, cuts[3]:cuts[4]], factors[:, cuts[4]:], KRANK))
    block_rows = 512 if GTOK % 512 == 0 else GTOK
    block_count = GTOK // block_rows

    def attend(element):
        query_part, query_index, query_seg, query_lim = element
        logits = low_back(jnp.einsum('qhd,khd->hqk', query_part, keys_all, precision=highest) * HDIM ** (-0.5))
        same_line = (segment[None, :] == query_seg[:, None]) & (index[None, :] <= query_index[:, None])
        from_prompt = (segment[None, :] == -1) & (index[None, :] < query_lim[:, None])
        logits = jnp.where((same_line | from_prompt)[None], logits, -1e+30)
        highest_score = lax.optimization_barrier(jnp.max(logits, axis=-1, keepdims=True))
        weights_now = jnp.exp(logits - highest_score)
        probs = low(weights_now / lax.optimization_barrier(jnp.sum(weights_now, axis=-1, keepdims=True)))
        return jnp.einsum('hqk,khd->qhd', probs, values_all, precision=highest)
    mixed = lax.map(jax.checkpoint(attend), (queries.reshape(block_count, block_rows, HEADS, HDIM), index.reshape(block_count, block_rows), segment.reshape(block_count, block_rows), limit.reshape(block_count, block_rows)))
    attended = low(low_back(mixed.reshape(GTOK, HEADS * HDIM)))
    middle = inputs + low_back(product(attended, output_weight))
    hidden_two = low(rms_norm(middle, feed_gain))
    gate_values = low_back(product(hidden_two, gate_weight))
    up_values = low_back(product(hidden_two, up_weight))
    active = low(gate_values * jax.nn.sigmoid(gate_values) * up_values)
    return middle + low_back(product(active, down_weight))

def reference(layer_input, branch, attention_gain, factor_weight, output_weight, feed_gain, gate_weight, up_weight, down_weight, cotangent):
    weights_all = tuple((weight.astype(jnp.float32) for weight in (attention_gain, factor_weight, output_weight, feed_gain, gate_weight, up_weight, down_weight)))

    def one_group(totals, element):
        group_input, table, upstream = element
        index, segment, position, limit = geometry(table)

        def forward(values, *params):
            return residual_block(values, *params, index, segment, position, limit)
        result, pull = jax.vjp(forward, group_input.astype(jnp.float32), *weights_all)
        grads = pull(upstream.astype(jnp.float32))
        totals = tuple((running + grad for running, grad in zip(totals, grads[1:])))
        return (totals, (result.astype(jnp.bfloat16), grads[0]))
    start_totals = tuple((jnp.zeros(weight.shape, jnp.float32) for weight in weights_all))
    totals, (results, input_grads) = lax.scan(one_group, start_totals, (layer_input, branch, cotangent))
    return (results, input_grads, totals[0], totals[1], totals[2], totals[3], totals[4], totals[5], totals[6])
```

```python
import functools

import jax
import jax.numpy as jnp
import numpy as np
from jax import lax
from jax.experimental import pallas as pl
from jax.experimental.pallas import tpu as pltpu
from jax.sharding import PartitionSpec as P

HEADS = 16
HDIM = 64
QRANK = 6
KRANK = 2
HALF = HDIM // 2
QCOLS = QRANK * HEADS + QRANK * HDIM
KVCOLS = 2 * (KRANK * HEADS + KRANK * HDIM)
AQ, BQ = 0, QRANK * HEADS
AK, BK = 0, KRANK * HEADS
AV = BK + KRANK * HDIM
BV = AV + KRANK * HEADS
SCALE = HDIM**-0.5
EXP_SCALE = SCALE * float(np.log2(np.e))
NEG = -1e30
DEPTH = 128
EPS = 1e-05
VMEM_LIMIT = 60 * 2**20

f32 = jnp.float32
bf16 = jnp.bfloat16
NN = (((1,), (0,)), ((), ()))
NT = (((1,), (1,)), ((), ()))
TN = (((0,), (0,)), ((), ()))


def mm(left, right, dims=NN):
    return lax.dot_general(left, right, dims, preferred_element_type=f32)


def vmem():
    return pl.BlockSpec(memory_space=pltpu.VMEM)


def smem():
    return pl.BlockSpec(memory_space=pltpu.SMEM)


def params():
    return pltpu.CompilerParams(vmem_limit_bytes=VMEM_LIMIT)


def cost(flops, nbytes):
    return pl.CostEstimate(flops=int(flops), bytes_accessed=int(nbytes), transcendentals=0)


def turn(part, cosine, sine):
    first, second = part[:HALF], part[HALF:]
    return first * cosine - second * sine, second * cosine + first * sine


def front_kernel(x_ref, gain_ref, w_ref, cos_ref, sin_ref, fac_ref, hid_ref):
    xf = x_ref[...].astype(f32)
    scale = lax.rsqrt(jnp.mean(xf * xf, axis=-1, keepdims=True) + EPS)
    hidden = (xf * scale * gain_ref[...]).astype(bf16)
    hid_ref[...] = jnp.transpose(hidden)
    raw = jnp.transpose(mm(hidden, w_ref[...]))
    cosine, sine = cos_ref[...], sin_ref[...]
    fac_ref[...] = raw.astype(bf16)
    starts = [BQ + r * HDIM for r in range(QRANK)] + [QCOLS + BK + r * HDIM for r in range(KRANK)]
    for at in starts:
        one, two = turn(raw[at : at + HDIM], cosine, sine)
        fac_ref[at : at + HALF, :] = one.astype(bf16)
        fac_ref[at + HALF : at + HDIM, :] = two.astype(bf16)


def front(x, gain, weight, cosine, sine):
    rows, width = x.shape
    cols = weight.shape[1]
    return pl.pallas_call(
        front_kernel,
        out_shape=[
            jax.ShapeDtypeStruct((cols, rows), bf16),
            jax.ShapeDtypeStruct((width, rows), bf16),
        ],
        in_specs=[vmem()] * 5,
        out_specs=[vmem()] * 2,
        compiler_params=params(),
        cost_estimate=cost(2 * rows * width * cols, 4 * width * (cols + rows)),
        name="front",
    )(x, gain, weight, cosine, sine)


def load_factors(fac_ref, kv_ref, facf, kvf, qT, me, npc):
    facf[...] = fac_ref[...].astype(f32)

    def load(j, _):
        kvf[j] = kv_ref[j].astype(f32)
        return 0

    lax.fori_loop(0, npc, load, 0)
    load(me, 0)
    row = lax.broadcasted_iota(jnp.int32, (DEPTH - HDIM, qT.shape[1]), 0)
    qT[HDIM:DEPTH, :] = jnp.where(row == 0, 1.0, 0.0).astype(bf16)


def build_query(facf, qT, h):
    total = facf[pl.ds(AQ + h, 1), :] * facf[BQ : BQ + HDIM, :]
    for r in range(1, QRANK):
        total += facf[pl.ds(AQ + r * HEADS + h, 1), :] * facf[BQ + r * HDIM : BQ + (r + 1) * HDIM, :]
    qT[0:HDIM, :] = (total * (1.0 / QRANK)).astype(bf16)


def build_pair(kvf, j, h, a_at, b_at):
    total = kvf[j, pl.ds(a_at + h, 1), :] * kvf[j, b_at : b_at + HDIM, :]
    for r in range(1, KRANK):
        total += (
            kvf[j, pl.ds(a_at + r * HEADS + h, 1), :]
            * kvf[j, b_at + r * HDIM : b_at + (r + 1) * HDIM, :]
        )
    return (total * (1.0 / KRANK)).astype(bf16)


def build_key(kvf, kT, j, h, limit):
    span = kT.shape[1]
    kT[0:HDIM, :] = build_pair(kvf, j, h, AK, BK)
    if limit is None:
        kT[HDIM:DEPTH, :] = jnp.zeros((DEPTH - HDIM, span), bf16)
    else:
        row = lax.broadcasted_iota(jnp.int32, (DEPTH - HDIM, span), 0)
        key = j * span + lax.broadcasted_iota(jnp.int32, (DEPTH - HDIM, span), 1)
        kT[HDIM:DEPTH, :] = jnp.where((row == 0) & (key >= limit), NEG, 0.0).astype(bf16)


def causal(scores):
    key = lax.broadcasted_iota(jnp.int32, scores.shape, 0)
    query = lax.broadcasted_iota(jnp.int32, scores.shape, 1)
    return jnp.where(key <= query, scores, NEG)


def attend_kernel(info_ref, fac_ref, kv_ref, out_ref, lse_ref, facf, kvf, qT, kT, s_ref):
    me, npc, limit = info_ref[0], info_ref[1], info_ref[2]
    rows = fac_ref.shape[1]
    load_factors(fac_ref, kv_ref, facf, kvf, qT, me, npc)

    def head(h, _):
        build_query(facf, qT, h)

        def chunk(j, top):
            build_key(kvf, kT, j, h, limit)
            scores = mm(kT[...], qT[...], TN)
            s_ref[j] = scores
            return jnp.maximum(top, jnp.max(scores, axis=0, keepdims=True))

        top = lax.fori_loop(0, npc, chunk, jnp.full((1, rows), NEG, f32))
        build_key(kvf, kT, me, h, None)
        scores = causal(mm(kT[...], qT[...], TN))
        s_ref[npc] = scores
        top = jnp.maximum(top, jnp.max(scores, axis=0, keepdims=True)) * EXP_SCALE

        def weigh(j, mass):
            probs = jnp.exp2(s_ref[j] * EXP_SCALE - top)
            s_ref[j] = probs
            return mass + jnp.sum(probs, axis=0, keepdims=True)

        mass = lax.fori_loop(0, npc + 1, weigh, jnp.zeros((1, rows), f32))
        lse_ref[pl.ds(h, 1), :] = top + jnp.log2(mass)
        share = 1.0 / mass

        def gather(j, total):
            at = jnp.where(j == npc, me, j)
            return total + mm(build_pair(kvf, at, h, AV, BV), (s_ref[j] * share).astype(bf16))

        total = lax.fori_loop(0, npc + 1, gather, jnp.zeros((HDIM, rows), f32))
        out_ref[pl.ds(pl.multiple_of(h * HDIM, HDIM), HDIM), :] = total.astype(bf16)
        return 0

    lax.fori_loop(0, HEADS, head, 0)


def attend(info, fac, kv):
    parts, cols, rows = kv.shape
    seen = min(parts, parts // 2 + 1)
    return pl.pallas_call(
        attend_kernel,
        out_shape=[
            jax.ShapeDtypeStruct((HEADS * HDIM, rows), bf16),
            jax.ShapeDtypeStruct((HEADS, rows), f32),
        ],
        in_specs=[smem(), vmem(), vmem()],
        out_specs=[vmem()] * 2,
        scratch_shapes=[
            pltpu.VMEM((QCOLS, rows), f32),
            pltpu.VMEM((parts, cols, rows), f32),
            pltpu.VMEM((DEPTH, rows), bf16),
            pltpu.VMEM((DEPTH, rows), bf16),
            pltpu.VMEM((seen, rows, rows), f32),
        ],
        compiler_params=params(),
        cost_estimate=cost(16 * 2 * HEADS * 256 * rows * rows * seen, 4 * cols * rows * parts),
        name="attend",
    )(info, fac, kv)


def attend_back_kernel(
    info_ref, fac_ref, kv_ref, grad_ref, lse_ref, dq_ref, dkv_ref, facf, kvf, dkvf, qT, kTs, p_ref, dp_ref
):
    me, npc, limit = info_ref[0], info_ref[1], info_ref[2]
    parts, _, rows = kv_ref.shape
    load_factors(fac_ref, kv_ref, facf, kvf, qT, me, npc)

    def clear(j, _):
        dkvf[j] = jnp.zeros(dkvf.shape[1:], f32)
        return 0

    lax.fori_loop(0, parts, clear, 0)
    dq_ref[...] = jnp.zeros(dq_ref.shape, f32)

    def head(h, _):
        build_query(facf, qT, h)
        at_head = pl.ds(pl.multiple_of(h * HDIM, HDIM), HDIM)
        grad = grad_ref[at_head, :]
        lse = lse_ref[pl.ds(h, 1), :]

        def probe(slot, at, scores, delta):
            probs = jnp.exp2(scores * EXP_SCALE - lse)
            p_ref[slot] = probs
            prob_grad = mm(build_pair(kvf, at, h, AV, BV), grad, TN)
            dp_ref[slot] = prob_grad
            return delta + jnp.sum(probs * prob_grad, axis=0, keepdims=True)

        def chunk(j, delta):
            build_key(kvf, kTs.at[j], j, h, limit)
            return probe(j, j, mm(kTs[j], qT[...], TN), delta)

        delta = lax.fori_loop(0, npc, chunk, jnp.zeros((1, rows), f32))
        build_key(kvf, kTs.at[npc], me, h, None)
        delta = probe(npc, me, causal(mm(kTs[npc], qT[...], TN)), delta)

        def pull(j, total):
            at = jnp.where(j == npc, me, j)
            probs = p_ref[j]
            score_grad = (probs * (dp_ref[j] - delta)).astype(bf16)
            key_grad = mm(qT[0:HDIM, :], score_grad, NT) * (SCALE / KRANK)
            value_grad = mm(grad, probs.astype(bf16), NT) * (1.0 / KRANK)
            for a_at, b_at, got in ((AK, BK, key_grad), (AV, BV, value_grad)):
                for r in range(KRANK):
                    a_row = pl.ds(a_at + r * HEADS + h, 1)
                    b_rows = slice(b_at + r * HDIM, b_at + (r + 1) * HDIM)
                    dkvf[at, a_row, :] = jnp.sum(got * kvf[at, b_rows, :], axis=0, keepdims=True)
                    dkvf[at, b_rows, :] += got * kvf[at, a_row, :]
            return total + mm(kTs[j, 0:HDIM, :], score_grad)

        query_grad = lax.fori_loop(0, npc + 1, pull, jnp.zeros((HDIM, rows), f32)) * (SCALE / QRANK)
        for r in range(QRANK):
            a_row = pl.ds(AQ + r * HEADS + h, 1)
            b_rows = slice(BQ + r * HDIM, BQ + (r + 1) * HDIM)
            dq_ref[a_row, :] = jnp.sum(query_grad * facf[b_rows, :], axis=0, keepdims=True)
            dq_ref[b_rows, :] += query_grad * facf[a_row, :]
        return 0

    lax.fori_loop(0, HEADS, head, 0)

    def store(j, _):
        dkv_ref[j] = dkvf[j].astype(bf16)
        return 0

    lax.fori_loop(0, parts, store, 0)


def attend_back(info, fac, kv, grad, lse):
    parts, cols, rows = kv.shape
    seen = min(parts, parts // 2 + 1)
    return pl.pallas_call(
        attend_back_kernel,
        out_shape=[
            jax.ShapeDtypeStruct((QCOLS, rows), f32),
            jax.ShapeDtypeStruct((parts, cols, rows), bf16),
        ],
        in_specs=[smem()] + [vmem()] * 4,
        out_specs=[vmem()] * 2,
        scratch_shapes=[
            pltpu.VMEM((QCOLS, rows), f32),
            pltpu.VMEM((parts, cols, rows), f32),
            pltpu.VMEM((parts, cols, rows), f32),
            pltpu.VMEM((DEPTH, rows), bf16),
            pltpu.VMEM((seen, DEPTH, rows), bf16),
            pltpu.VMEM((seen, rows, rows), f32),
            pltpu.VMEM((seen, rows, rows), f32),
        ],
        compiler_params=params(),
        cost_estimate=cost(40 * 2 * HEADS * 256 * rows * rows * seen, 8 * cols * rows * parts),
        name="attend_back",
    )(info, fac, kv, grad, lse)


def rms_scale(values):
    return lax.rsqrt(jnp.mean(values * values, axis=-1, keepdims=True) + EPS)


def norm_back(grad_hidden, normed, scale, gain_vector):
    grad_normed = grad_hidden * gain_vector
    gain_grad = jnp.sum(grad_hidden * normed, axis=0)
    grad_values = scale * (
        grad_normed - normed * jnp.mean(grad_normed * normed, axis=-1, keepdims=True)
    )
    return gain_grad, grad_values


def turn_back(grads, cosine, sine):
    starts = [BQ + r * HDIM for r in range(QRANK)] + [QCOLS + BK + r * HDIM for r in range(KRANK)]
    pieces, at = [], 0
    for start in starts:
        pieces.append(grads[at:start])
        pieces.extend(turn(grads[start : start + HDIM], cosine, -sine))
        at = start + HDIM
    pieces.append(grads[at:])
    return jnp.concatenate(pieces, axis=0)


def local(
    layer_input,
    branch,
    attention_gain,
    factor_weight,
    output_weight,
    feed_gain,
    gate_weight,
    up_weight,
    down_weight,
    cotangent,
):
    def everywhere(values):
        return lax.all_gather(values, "grp", axis=0, tiled=True)

    rows = layer_input.shape[1]
    parts = lax.axis_size("grp")
    me = lax.axis_index("grp")
    prompt_parts = parts // 2
    follows = me >= prompt_parts
    chosen = branch[0, jnp.maximum(me - prompt_parts, 0)]
    limit = jnp.where(follows, chosen, me * rows)
    npc = (limit + rows - 1) // rows
    position = jnp.where(follows, chosen, me * rows) + jnp.arange(rows, dtype=jnp.int32)
    info = jnp.stack([me, npc, limit]).astype(jnp.int32)
    freqs = 10000.0 ** (-jnp.arange(HALF).astype(f32) / HALF)
    phase = freqs[:, None] * position.astype(f32)[None, :]
    cosine, sine = jnp.cos(phase), jnp.sin(phase)

    gain_one = everywhere(attention_gain).astype(f32)
    gain_two = everywhere(feed_gain).astype(f32)
    w_fac = everywhere(factor_weight)
    w_out = everywhere(output_weight)
    w_gate = everywhere(gate_weight)
    w_up = everywhere(up_weight)
    w_down = everywhere(down_weight)

    x = layer_input[0]
    upstream = cotangent[0]
    fac, hid_one = front(x, gain_one[None], w_fac, cosine, sine)
    kv = lax.all_gather(fac[QCOLS:], "grp", axis=0, tiled=False)
    fac_q = fac[:QCOLS]
    mixed, lse = attend(info, fac_q, kv)

    residual_in = x.astype(f32)
    middle = residual_in + mm(mixed, w_out, TN)
    scale_two = rms_scale(middle)
    normed_two = middle * scale_two
    hidden_two = (normed_two * gain_two).astype(bf16)
    gate_values = mm(hidden_two, w_gate)
    up_values = mm(hidden_two, w_up)
    sigmoid_gate = jax.nn.sigmoid(gate_values)
    active = (gate_values * sigmoid_gate * up_values).astype(bf16)
    result = middle + mm(active, w_down)
    down_grad = mm(active, upstream, TN)
    active_grad = mm(upstream, w_down, NT)
    gate_grad = (
        active_grad * up_values * sigmoid_gate * (1.0 + gate_values * (1.0 - sigmoid_gate))
    ).astype(bf16)
    up_grad = (active_grad * gate_values * sigmoid_gate).astype(bf16)
    gate_weight_grad = mm(hidden_two, gate_grad, TN)
    up_weight_grad = mm(hidden_two, up_grad, TN)
    hidden_two_grad = mm(gate_grad, w_gate, NT) + mm(up_grad, w_up, NT)
    feed_gain_grad, middle_grad = norm_back(hidden_two_grad, normed_two, scale_two, gain_two)
    middle_grad = middle_grad + upstream.astype(f32)
    branch_grad = middle_grad.astype(bf16)
    output_weight_grad = mm(mixed, branch_grad)
    mixed_grad = mm(w_out, branch_grad, NT).astype(bf16)

    dq, dkv = attend_back(info, fac_q, kv, mixed_grad, lse)
    own = lax.psum_scatter(dkv, "grp", scatter_dimension=0, tiled=False)
    draw = turn_back(jnp.concatenate([dq, own.astype(f32)], axis=0), cosine, sine).astype(bf16)
    factor_weight_grad = mm(hid_one, draw, NT)
    hidden_one_grad = mm(draw, w_fac, (((0,), (1,)), ((), ())))
    scale_one = rms_scale(residual_in)
    attention_gain_grad, input_part = norm_back(
        hidden_one_grad, residual_in * scale_one, scale_one, gain_one
    )
    input_grad = middle_grad + input_part

    def reduced(values):
        shard = lax.psum_scatter(values.astype(bf16), "grp", scatter_dimension=0, tiled=True)
        return lax.psum(shard, "rep").astype(f32)

    return (
        result.astype(bf16)[None],
        input_grad[None],
        reduced(attention_gain_grad),
        reduced(factor_weight_grad),
        reduced(output_weight_grad),
        reduced(feed_gain_grad),
        reduced(gate_weight_grad),
        reduced(up_weight_grad),
        reduced(down_grad),
    )


def solution(mesh):
    in_specs = (
        P("rep", "grp", None),
        P("rep", None),
        P("grp"),
        P("grp", None),
        P("grp", None),
        P("grp"),
        P("grp", None),
        P("grp", None),
        P("grp", None),
        P("rep", "grp", None),
    )
    out_specs = (
        P("rep", "grp", None),
        P("rep", "grp", None),
        P("grp"),
        P("grp", None),
        P("grp", None),
        P("grp"),
        P("grp", None),
        P("grp", None),
        P("grp", None),
    )
    return jax.shard_map(local, mesh=mesh, in_specs=in_specs, out_specs=out_specs, check_vma=False)
```

```python
import functools

import jax
import jax.numpy as jnp
import numpy as np
from jax import lax
from jax.experimental import pallas as pl
from jax.experimental.pallas import tpu as pltpu
from jax.sharding import PartitionSpec as P

HEADS = 16
HDIM = 64
QRANK = 6
KRANK = 2
HALF = HDIM // 2
QCOLS = QRANK * HEADS + QRANK * HDIM
KVCOLS = 2 * (KRANK * HEADS + KRANK * HDIM)
AQ, BQ = 0, QRANK * HEADS
AK, BK = 0, KRANK * HEADS
AV = BK + KRANK * HDIM
BV = AV + KRANK * HEADS
SCALE = HDIM**-0.5
EXP_SCALE = SCALE * float(np.log2(np.e))
NEG = -1e30
DEPTH = 128
EPS = 1e-05
VMEM_LIMIT = 60 * 2**20

f32 = jnp.float32
bf16 = jnp.bfloat16
NN = (((1,), (0,)), ((), ()))
NT = (((1,), (1,)), ((), ()))
TN = (((0,), (0,)), ((), ()))


def mm(left, right, dims=NN):
    return lax.dot_general(left, right, dims, preferred_element_type=f32)


def vmem():
    return pl.BlockSpec(memory_space=pltpu.VMEM)


def smem():
    return pl.BlockSpec(memory_space=pltpu.SMEM)


def params():
    return pltpu.CompilerParams(vmem_limit_bytes=VMEM_LIMIT)


def cost(flops, nbytes):
    return pl.CostEstimate(flops=int(flops), bytes_accessed=int(nbytes), transcendentals=0)


def turn(part, cosine, sine):
    first, second = part[:HALF], part[HALF:]
    return first * cosine - second * sine, second * cosine + first * sine


def front_kernel(count, cols, offs, x_ref, cos_ref, sin_ref, *refs):
    pieces = refs[:count]
    fac_ref, kv_ref, hid_ref, gains_ref, w, sems = refs[count:]
    w_in = Mover(sems).pieces(offs, pieces, w)
    xf = x_ref[...].astype(f32)
    normed = xf * lax.rsqrt(jnp.mean(xf * xf, axis=-1, keepdims=True) + EPS)
    wait(w_in)
    last = w.shape[1] - 128
    gains = jnp.transpose(w[:, last:])[cols - last : cols - last + 16].astype(f32)
    gains_ref[...] = gains[0:8]
    hidden = (normed * gains[0:1]).astype(bf16)
    hid_ref[...] = jnp.transpose(hidden)
    raw = jnp.transpose(mm(hidden, w[...]))
    cosine, sine = cos_ref[...], sin_ref[...]
    fac_ref[...] = raw[:QCOLS].astype(bf16)
    kv_ref[...] = raw[QCOLS:cols].astype(bf16)
    for ref, first, at in [(fac_ref, 0, BQ + r * HDIM) for r in range(QRANK)] + [
        (kv_ref, QCOLS, BK + r * HDIM) for r in range(KRANK)
    ]:
        one, two = turn(raw[first + at : first + at + HDIM], cosine, sine)
        ref[at : at + HALF, :] = one.astype(bf16)
        ref[at + HALF : at + HDIM, :] = two.astype(bf16)


def front(offs, x, cosine, sine, w_fac, cols):
    rows, width = x.shape
    wide = w_fac[0].shape[1]
    count = len(w_fac)
    return pl.pallas_call(
        functools.partial(front_kernel, count, cols),
        out_shape=[
            like(QCOLS, rows),
            like(cols - QCOLS, rows),
            like(width, rows),
            like(8, width, dtype=f32),
        ],
        in_specs=[smem()] + [vmem()] * 3 + [anywhere()] * count,
        out_specs=[vmem()] * 4,
        scratch_shapes=[scratch(width, wide), pltpu.SemaphoreType.DMA((count,))],
        compiler_params=params(),
        cost_estimate=cost(2 * rows * width * cols, 4 * width * (cols + rows)),
        name="front",
    )(offs, x, cosine, sine, *w_fac)


def load_factors(fac_ref, kv_refs, facf, kvf, qT, me):
    facf[...] = fac_ref[...].astype(f32)
    if len(kv_refs) == 1:

        def load(j, _):
            kvf[j] = kv_refs[0][j].astype(f32)
            return 0

        lax.fori_loop(0, kvf.shape[0], load, 0)
    else:
        for flip, ref in enumerate(kv_refs):
            kvf[me ^ flip] = ref[...].astype(f32)
    row = lax.broadcasted_iota(jnp.int32, (DEPTH - HDIM, qT.shape[1]), 0)
    qT[HDIM:DEPTH, :] = jnp.where(row == 0, 1.0, 0.0).astype(bf16)


def build_query(facf, qT, h):
    total = facf[pl.ds(AQ + h, 1), :] * facf[BQ : BQ + HDIM, :]
    for r in range(1, QRANK):
        total += facf[pl.ds(AQ + r * HEADS + h, 1), :] * facf[BQ + r * HDIM : BQ + (r + 1) * HDIM, :]
    qT[0:HDIM, :] = (total * (1.0 / QRANK)).astype(bf16)


def build_pair(kvf, j, h, a_at, b_at):
    total = kvf[j, pl.ds(a_at + h, 1), :] * kvf[j, b_at : b_at + HDIM, :]
    for r in range(1, KRANK):
        total += (
            kvf[j, pl.ds(a_at + r * HEADS + h, 1), :]
            * kvf[j, b_at + r * HDIM : b_at + (r + 1) * HDIM, :]
        )
    return (total * (1.0 / KRANK)).astype(bf16)


def build_key(kvf, kT, j, h, limit):
    span = kT.shape[1]
    kT[0:HDIM, :] = build_pair(kvf, j, h, AK, BK)
    if limit is None:
        kT[HDIM:DEPTH, :] = jnp.zeros((DEPTH - HDIM, span), bf16)
    else:
        row = lax.broadcasted_iota(jnp.int32, (DEPTH - HDIM, span), 0)
        key = j * span + lax.broadcasted_iota(jnp.int32, (DEPTH - HDIM, span), 1)
        kT[HDIM:DEPTH, :] = jnp.where((row == 0) & (key >= limit), NEG, 0.0).astype(bf16)


def causal(scores):
    key = lax.broadcasted_iota(jnp.int32, scores.shape, 0)
    query = lax.broadcasted_iota(jnp.int32, scores.shape, 1)
    return jnp.where(key <= query, scores, NEG)


def attend_kernel(first, heads, count, info_ref, fac_ref, *refs):
    kv_refs, (out_ref, lse_ref, facf, kvf, qT, kT, s_ref) = refs[:count], refs[count:]
    me, npc, limit = info_ref[0], info_ref[1], info_ref[2]
    rows = fac_ref.shape[1]
    load_factors(fac_ref, kv_refs, facf, kvf, qT, me)

    def head(step, _):
        h = first + step
        build_query(facf, qT, h)

        def chunk(j, top):
            build_key(kvf, kT, j, h, limit)
            scores = mm(kT[...], qT[...], TN)
            s_ref[j] = scores
            return jnp.maximum(top, jnp.max(scores, axis=0, keepdims=True))

        top = lax.fori_loop(0, npc, chunk, jnp.full((1, rows), NEG, f32))
        build_key(kvf, kT, me, h, None)
        scores = causal(mm(kT[...], qT[...], TN))
        s_ref[npc] = scores
        top = jnp.maximum(top, jnp.max(scores, axis=0, keepdims=True)) * EXP_SCALE

        def weigh(j, mass):
            probs = jnp.exp2(s_ref[j] * EXP_SCALE - top)
            s_ref[j] = probs
            return mass + jnp.sum(probs, axis=0, keepdims=True)

        mass = lax.fori_loop(0, npc + 1, weigh, jnp.zeros((1, rows), f32))
        lse_ref[pl.ds(step, 1), :] = top + jnp.log2(mass)
        share = 1.0 / mass

        def gather(j, total):
            at = jnp.where(j == npc, me, j)
            return total + mm(build_pair(kvf, at, h, AV, BV), (s_ref[j] * share).astype(bf16))

        total = lax.fori_loop(0, npc + 1, gather, jnp.zeros((HDIM, rows), f32))
        out_ref[pl.ds(pl.multiple_of(step * HDIM, HDIM), HDIM), :] = total.astype(bf16)
        return 0

    lax.fori_loop(0, heads, head, 0)


def kv_sizes(kv):
    return kv[0].shape if len(kv) == 1 else (len(kv),) + kv[0].shape


def attend(info, fac, kv, first, heads):
    parts, cols, rows = kv_sizes(kv)
    seen = min(parts, parts // 2 + 1)
    return pl.pallas_call(
        functools.partial(attend_kernel, first, heads, len(kv)),
        out_shape=[
            jax.ShapeDtypeStruct((heads * HDIM, rows), bf16),
            jax.ShapeDtypeStruct((heads, rows), f32),
        ],
        in_specs=[smem(), vmem()] + [vmem()] * len(kv),
        out_specs=[vmem()] * 2,
        scratch_shapes=[
            pltpu.VMEM((QCOLS, rows), f32),
            pltpu.VMEM((parts, cols, rows), f32),
            pltpu.VMEM((DEPTH, rows), bf16),
            pltpu.VMEM((DEPTH, rows), bf16),
            pltpu.VMEM((seen, rows, rows), f32),
        ],
        compiler_params=params(),
        cost_estimate=cost(16 * 2 * heads * 256 * rows * rows * seen, 4 * cols * rows * parts),
        name="attend",
    )(info, fac, *kv)


def attend_back_kernel(first, heads, final, count, info_ref, fac_ref, grad_ref, lse_ref, *refs):
    kv_refs, refs = refs[:count], refs[count:]
    if first:
        dq_in, dkv_in, *refs = refs
    dq_ref, *refs = refs
    if final:
        keep_ref, send_ref, *refs = refs
        *refs, dkvf = refs
    else:
        dkvf, *refs = refs
    facf, kvf, qT, kTs, p_ref, dp_ref = refs
    me, npc, limit = info_ref[0], info_ref[1], info_ref[2]
    parts, _, rows = kvf.shape
    load_factors(fac_ref, kv_refs, facf, kvf, qT, me)

    def begin(j, _):
        dkvf[j] = dkv_in[j] if first else jnp.zeros(dkvf.shape[1:], f32)
        return 0

    lax.fori_loop(0, parts, begin, 0)
    dq_ref[...] = dq_in[...] if first else jnp.zeros(dq_ref.shape, f32)

    def head(step, _):
        h = first + step
        build_query(facf, qT, h)
        grad = grad_ref[pl.ds(pl.multiple_of(h * HDIM, HDIM), HDIM), :]
        lse = lse_ref[pl.ds(h, 1), :]

        def probe(slot, at, scores, delta):
            probs = jnp.exp2(scores * EXP_SCALE - lse)
            p_ref[slot] = probs
            prob_grad = mm(build_pair(kvf, at, h, AV, BV), grad, TN)
            dp_ref[slot] = prob_grad
            return delta + jnp.sum(probs * prob_grad, axis=0, keepdims=True)

        def chunk(j, delta):
            build_key(kvf, kTs.at[j], j, h, limit)
            return probe(j, j, mm(kTs[j], qT[...], TN), delta)

        delta = lax.fori_loop(0, npc, chunk, jnp.zeros((1, rows), f32))
        build_key(kvf, kTs.at[npc], me, h, None)
        delta = probe(npc, me, causal(mm(kTs[npc], qT[...], TN)), delta)

        def pull(j, total):
            at = jnp.where(j == npc, me, j)
            probs = p_ref[j]
            score_grad = (probs * (dp_ref[j] - delta)).astype(bf16)
            key_grad = mm(qT[0:HDIM, :], score_grad, NT) * (SCALE / KRANK)
            value_grad = mm(grad, probs.astype(bf16), NT) * (1.0 / KRANK)
            for a_at, b_at, got in ((AK, BK, key_grad), (AV, BV, value_grad)):
                for r in range(KRANK):
                    a_row = pl.ds(a_at + r * HEADS + h, 1)
                    b_rows = slice(b_at + r * HDIM, b_at + (r + 1) * HDIM)
                    dkvf[at, a_row, :] = jnp.sum(got * kvf[at, b_rows, :], axis=0, keepdims=True)
                    dkvf[at, b_rows, :] += got * kvf[at, a_row, :]
            return total + mm(kTs[j, 0:HDIM, :], score_grad)

        query_grad = lax.fori_loop(0, npc + 1, pull, jnp.zeros((HDIM, rows), f32)) * (SCALE / QRANK)
        for r in range(QRANK):
            a_row = pl.ds(AQ + r * HEADS + h, 1)
            b_rows = slice(BQ + r * HDIM, BQ + (r + 1) * HDIM)
            dq_ref[a_row, :] = jnp.sum(query_grad * facf[b_rows, :], axis=0, keepdims=True)
            dq_ref[b_rows, :] += query_grad * facf[a_row, :]
        return 0

    lax.fori_loop(0, heads, head, 0)
    if final:
        for j in range(parts // 2):
            keep_ref[j] = dkvf[me ^ (2 * j)].astype(bf16)
            send_ref[j] = dkvf[me ^ (2 * j + 1)].astype(bf16)


def attend_back(info, fac, kv, grad, lse, first, heads, so_far):
    parts, cols, rows = kv_sizes(kv)
    seen = min(parts, parts // 2 + 1)
    final = first + heads == HEADS
    gathered = [like(parts // 2, cols, rows)] * 2 if final else [like(parts, cols, rows, dtype=f32)]
    return pl.pallas_call(
        functools.partial(attend_back_kernel, first, heads, final, len(kv)),
        out_shape=[like(QCOLS, rows, dtype=f32)] + gathered,
        in_specs=[smem()] + [vmem()] * (3 + len(kv) + len(so_far)),
        out_specs=[vmem()] * (1 + len(gathered)),
        scratch_shapes=[
            pltpu.VMEM((QCOLS, rows), f32),
            pltpu.VMEM((parts, cols, rows), f32),
            pltpu.VMEM((DEPTH, rows), bf16),
            pltpu.VMEM((seen, DEPTH, rows), bf16),
            pltpu.VMEM((seen, rows, rows), f32),
            pltpu.VMEM((seen, rows, rows), f32),
        ]
        + ([pltpu.VMEM((parts, cols, rows), f32)] if final else []),
        compiler_params=params(),
        cost_estimate=cost(40 * 2 * heads * 256 * rows * rows * seen, 8 * cols * rows * parts),
        name="attend_back",
    )(info, fac, grad, lse, *kv, *so_far)


class Mover:
    def __init__(self, sems):
        self.sems = sems
        self.used = 0

    def start(self, src, dst):
        copy = pltpu.make_async_copy(src, dst, self.sems.at[self.used])
        self.used += 1
        copy.start()
        return copy

    def pieces(self, offsets, refs, dst):
        copies = []
        for i, piece in enumerate(refs):
            rows, cols = piece.shape
            at = pl.ds(pl.multiple_of(offsets[2 * i], 16), rows)
            if cols == dst.shape[1]:
                where = dst.at[at]
            else:
                where = dst.at[at, pl.ds(pl.multiple_of(offsets[2 * i + 1], 128), cols)]
            copies.append(self.start(piece, where))
        return copies


def wait(copies):
    for copy in copies:
        copy.wait()


def anywhere():
    return pl.BlockSpec(memory_space=pl.ANY)


def like(*shape, dtype=bf16):
    return jax.ShapeDtypeStruct(shape, dtype)


def scratch(*shape, dtype=bf16):
    return pltpu.VMEM(shape, dtype)


TILE = 256


def norm_back(grad_hidden, normed, scale, gain):
    grad_normed = grad_hidden * gain
    gain_grad = jnp.sum(grad_hidden * normed, axis=0, keepdims=True)
    mean = jnp.mean(grad_normed * normed, axis=-1, keepdims=True)
    return gain_grad, scale * (grad_normed - normed * mean)


def shard_products(me, left, right, keep, send, mover, keep_out, send_out, cut=2816):
    copies = []
    count, rows, cols = keep.shape
    step = rows if rows <= 352 else rows // 2
    for odd, dst, out in ((1, send, send_out), (0, keep, keep_out)):
        for j in range(count):
            row = (me ^ (2 * j + odd)) * rows
            for low in range(0, rows, step):
                lhs = left[pl.ds(pl.multiple_of(row + low, 16), step), :]
                for at in range(0, cols, 1408 if cols % 1408 == 0 else cols):
                    width = 1408 if cols % 1408 == 0 else cols
                    dst[j, low : low + step, at : at + width] = mm(
                        lhs, right[:, at : at + width]
                    ).astype(bf16)
            copies.append(mover.start(dst.at[j], out.at[j]))
    return copies


def feed_kernel(count, offs, who, mix_ref, x_ref, gain_ref, up_ref, *refs):
    out_pieces, gate_pieces, lift_pieces = (refs[i * count : (i + 1) * count] for i in range(3))
    refs = refs[3 * count :]
    (mid_o, hid_o, act_o, slope_o, lin_o, keep_o, send_o) = refs[:7]
    (wo, wg, wu, mid, hid, hidT, act, slope, lin, actT, keep, send, sems) = refs[7:]
    mover = Mover(sems)
    wo_in = mover.pieces(offs, out_pieces, wo)
    wg_in = mover.pieces(offs, gate_pieces, wg)
    wu_in = mover.pieces(offs, lift_pieces, wu)
    mix = jnp.transpose(mix_ref[...])
    wait(wo_in)
    middle = x_ref[...].astype(f32) + mm(mix, wo[...])
    mid[...] = middle
    scale = lax.rsqrt(jnp.mean(middle * middle, axis=-1, keepdims=True) + EPS)
    hidden = (middle * scale * gain_ref[...]).astype(bf16)
    hid[...] = hidden
    hidT[...] = jnp.transpose(hidden)
    done = [mover.start(mid, mid_o), mover.start(hidT, hid_o)]
    wait(wg_in)
    wait(wu_in)

    def tile(j, _):
        cols = pl.ds(pl.multiple_of(j * TILE, TILE), TILE)
        gate = mm(hid[...], wg[:, cols])
        up = mm(hid[...], wu[:, cols])
        sig = jax.nn.sigmoid(gate)
        line = gate * sig
        active = (line * up).astype(bf16)
        act[:, cols] = active
        lin[:, cols] = line.astype(bf16)
        slope[:, cols] = (up * sig * (1.0 + gate * (1.0 - sig))).astype(bf16)
        actT[cols, :] = jnp.transpose(active)
        return 0

    lax.fori_loop(0, wg.shape[1] // TILE, tile, 0)
    done += [mover.start(act, act_o), mover.start(lin, lin_o), mover.start(slope, slope_o)]
    done += shard_products(who[0], actT, up_ref, keep, send, mover, keep_o, send_o)
    wait(done)


def feed(offs, who, mix, x, gain, upstream, w_out, w_gate, w_up, parts):
    rows, width = x.shape
    inner = w_gate[0].shape[1]
    count = len(w_gate)
    down = (parts // 2, inner // parts, width)
    return pl.pallas_call(
        functools.partial(feed_kernel, count),
        out_shape=[
            like(rows, width, dtype=f32),
            like(width, rows),
            like(rows, inner),
            like(rows, inner),
            like(rows, inner),
            like(*down),
            like(*down),
        ],
        in_specs=[smem(), smem()] + [vmem()] * 4 + [anywhere()] * (3 * count),
        out_specs=[anywhere()] * 7,
        scratch_shapes=[
            scratch(width, width),
            scratch(width, inner),
            scratch(width, inner),
            scratch(rows, width, dtype=f32),
            scratch(rows, width),
            scratch(width, rows),
            scratch(rows, inner),
            scratch(rows, inner),
            scratch(rows, inner),
            scratch(inner, rows),
            scratch(*down),
            scratch(*down),
            pltpu.SemaphoreType.DMA((3 * count + 5 + parts,)),
        ],
        compiler_params=params(),
        cost_estimate=cost(2 * rows * width * (width + 3 * inner), 2 * inner * (3 * width + 3 * rows)),
        name="feed",
    )(offs, who, mix, x, gain, upstream, *w_out, *w_gate, *w_up)


def slopes_kernel(c_ref, slope_ref, lin_ref, wd, dg, du):

    def tile(j, _):
        cols = pl.ds(pl.multiple_of(j * TILE, TILE), TILE)
        grad = mm(c_ref[...], wd[cols, :], NT)
        dg[:, cols] = (grad * slope_ref[:, cols].astype(f32)).astype(bf16)
        du[:, cols] = (grad * lin_ref[:, cols].astype(f32)).astype(bf16)
        return 0

    lax.fori_loop(0, wd.shape[0] // TILE, tile, 0)


def slopes(upstream, w_down, slope, lin):
    rows, width = upstream.shape
    inner = slope.shape[1]
    return pl.pallas_call(
        slopes_kernel,
        out_shape=[like(rows, inner)] * 2,
        in_specs=[vmem()] * 4,
        out_specs=[vmem()] * 2,
        compiler_params=params(),
        cost_estimate=cost(2 * rows * width * inner, 2 * inner * (width + 4 * rows)),
        name="slopes",
    )(upstream, slope, lin, w_down)


def widths_kernel(who, hid_ref, dg_ref, du_ref, gkeep_o, gsend_o, ukeep_o, usend_o, gkeep, gsend, ukeep, usend, sems):
    mover = Mover(sems)
    done = shard_products(who[0], hid_ref, dg_ref, gkeep, gsend, mover, gkeep_o, gsend_o)
    done += shard_products(who[0], hid_ref, du_ref, ukeep, usend, mover, ukeep_o, usend_o)
    wait(done)


def widths(who, hidT, dg, du, parts):
    width, rows = hidT.shape
    inner = dg.shape[1]
    shard = (parts // 2, width // parts, inner)
    return pl.pallas_call(
        widths_kernel,
        out_shape=[like(*shard)] * 4,
        in_specs=[smem()] + [vmem()] * 3,
        out_specs=[anywhere()] * 4,
        scratch_shapes=[scratch(*shard)] * 4 + [pltpu.SemaphoreType.DMA((2 * parts,))],
        compiler_params=params(),
        cost_estimate=cost(4 * rows * width * inner, 4 * inner * (width + rows)),
        name="widths",
    )(who, hidT, dg, du)


def settle_kernel(count, offs, who, c_ref, gain_ref, down_full, *refs):
    out_pieces, gate_pieces, lift_pieces = (refs[i * count : (i + 1) * count] for i in range(3))
    refs = refs[3 * count :]
    (act_i, mid_i, dg_i, du_i, mix_i) = refs[:5]
    (res_o, dmid_o, fgain_o, dmix_o, keep_o, send_o) = refs[5:11]
    (wd, wg, wu, wo, act, mid, dg, du, mix, dhid, res, fgain, dmix, keep, send, sems) = refs[11:]
    mover = Mover(sems)
    in_dg, in_du = mover.start(dg_i, dg), mover.start(du_i, du)
    in_wg = mover.pieces(offs, gate_pieces, wg)
    in_wu = mover.pieces(offs, lift_pieces, wu)
    in_mid, in_mix = mover.start(mid_i, mid), mover.start(mix_i, mix)
    in_wo = mover.pieces(offs, out_pieces, wo)
    in_act = mover.start(act_i, act)
    in_wd = [mover.start(down_full, wd)]
    width = wd.shape[1]

    wait([in_dg] + in_wg)

    def back(which, j):
        at = pl.ds(pl.multiple_of(j * TILE, TILE), TILE)
        if which == 0:
            dhid[:, at] = mm(dg[...], wg[at, :], NT)
        else:
            dhid[:, at] += mm(du[...], wu[at, :], NT)
        return 0

    lax.fori_loop(0, width // TILE, lambda j, _: back(0, j), 0)
    wait([in_du] + in_wu)
    lax.fori_loop(0, width // TILE, lambda j, _: back(1, j), 0)
    wait([in_mid, in_mix] + in_wo)
    middle = mid[...]
    scale = lax.rsqrt(jnp.mean(middle * middle, axis=-1, keepdims=True) + EPS)
    gain_grad, part = norm_back(dhid[...], middle * scale, scale, gain_ref[...])
    fgain[...] = jnp.broadcast_to(gain_grad, fgain.shape)
    total = c_ref[...].astype(f32) + part
    dhid[...] = total
    branch = total.astype(bf16)
    done = [mover.start(dhid, dmid_o), mover.start(fgain, fgain_o)]
    dmix[...] = mm(wo[...], branch, NT).astype(bf16)
    done += [mover.start(dmix, dmix_o)]
    done += shard_products(who[0], mix, branch, keep, send, mover, keep_o, send_o)
    wait([in_act] + in_wd)

    def forth(j, _):
        at = pl.ds(pl.multiple_of(j * TILE, TILE), TILE)
        res[:, at] = (mid[:, at] + mm(act[...], wd[:, at])).astype(bf16)
        return 0

    lax.fori_loop(0, width // TILE, forth, 0)
    done += [mover.start(res, res_o)]
    wait(done)


def settle(offs, who, upstream, gain, w_out, w_down, w_gate, w_up, act, mid, dg, du, mix, parts):
    rows, width = upstream.shape
    inner = act.shape[1]
    count = len(w_gate)
    shard = (parts // 2, width // parts, width)
    return pl.pallas_call(
        functools.partial(settle_kernel, count),
        out_shape=[
            like(rows, width),
            like(rows, width, dtype=f32),
            like(8, width, dtype=f32),
            like(width, rows),
            like(*shard),
            like(*shard),
        ],
        in_specs=[smem()] * 2 + [vmem()] * 2 + [anywhere()] * (3 * count + 6),
        out_specs=[anywhere()] * 6,
        scratch_shapes=[
            scratch(inner, width),
            scratch(width, inner),
            scratch(width, inner),
            scratch(width, width),
            scratch(rows, inner),
            scratch(rows, width, dtype=f32),
            scratch(rows, inner),
            scratch(rows, inner),
            scratch(width, rows),
            scratch(rows, width, dtype=f32),
            scratch(rows, width),
            scratch(8, width, dtype=f32),
            scratch(width, rows),
            scratch(*shard),
            scratch(*shard),
            pltpu.SemaphoreType.DMA((3 * count + 10 + parts,)),
        ],
        compiler_params=params(),
        cost_estimate=cost(2 * rows * width * (3 * inner + 2 * width), 2 * inner * (3 * width + 3 * rows)),
        name="settle",
    )(offs, who, upstream, gain, w_down, *w_out, *w_gate, *w_up, act, mid, dg, du, mix)


def tail_kernel(count, cols, offs, who, dq_ref, own_ref, cos_ref, sin_ref, hid_ref, x_ref, gain_ref, dmid_ref, fgain_ref, *refs):
    pieces = refs[:count]
    grad_ref, keep_o, send_o = refs[count : count + 3]
    w, raw, keep, send, sems = refs[count + 3 :]
    mover = Mover(sems)
    w_in = mover.pieces(offs, pieces, w)
    cosine, sine = cos_ref[...], -sin_ref[...]
    raw[0:QCOLS, :] = dq_ref[...].astype(bf16)
    raw[QCOLS:cols, :] = own_ref[...]
    raw[cols:, :] = jnp.zeros((raw.shape[0] - cols, raw.shape[1]), bf16)
    for r in range(QRANK):
        at = BQ + r * HDIM
        one, two = turn(dq_ref[at : at + HDIM, :], cosine, sine)
        raw[at : at + HALF, :] = one.astype(bf16)
        raw[at + HALF : at + HDIM, :] = two.astype(bf16)
    for r in range(KRANK):
        at = BK + r * HDIM
        one, two = turn(own_ref[at : at + HDIM, :].astype(f32), cosine, sine)
        raw[QCOLS + at : QCOLS + at + HALF, :] = one.astype(bf16)
        raw[QCOLS + at + HALF : QCOLS + at + HDIM, :] = two.astype(bf16)
    draw = jnp.transpose(raw[...])
    wait(w_in)
    xf = x_ref[...].astype(f32)
    scale = lax.rsqrt(jnp.mean(xf * xf, axis=-1, keepdims=True) + EPS)
    dhid = mm(draw, w[...], NT)
    gain_grad, part = norm_back(dhid, xf * scale, scale, gain_ref[...])
    grad_ref[...] = dmid_ref[...] + part
    width = raw.shape[0]
    line = lax.broadcasted_iota(jnp.int32, (128, gain_grad.shape[1]), 0) + (width - 128)
    both = jnp.where(line == cols, gain_grad, jnp.where(line == cols + 1, fgain_ref[0:1, :], 0.0))
    both = jnp.transpose(both)
    raw_gain = both.astype(bf16)
    w[:, 0:128] = raw_gain
    count_j, rows, _ = keep.shape
    done = []
    for odd, dst, out in ((1, send, send_o), (0, keep, keep_o)):
        for j in range(count_j):
            at = pl.ds(pl.multiple_of((who[0] ^ (2 * j + odd)) * rows, 16), rows)
            got = mm(hid_ref[at, :], draw)
            dst[j, :, 0 : width - 128] = got[:, 0 : width - 128].astype(bf16)
            dst[j, :, width - 128 :] = (got[:, width - 128 :] + w[at, 0:128].astype(f32)).astype(bf16)
            done.append(mover.start(dst.at[j], out.at[j]))
    wait(done)


def tail(offs, who, dq, own, cosine, sine, hidT, x, gain, dmid, fgain, w_fac, cols, parts):
    rows, width = x.shape
    wide = w_fac[0].shape[1]
    count = len(w_fac)
    shard = (parts // 2, width // parts, wide)
    return pl.pallas_call(
        functools.partial(tail_kernel, count, cols),
        out_shape=[like(rows, width, dtype=f32), like(*shard), like(*shard)],
        in_specs=[smem()] * 2 + [vmem()] * 9 + [anywhere()] * count,
        out_specs=[vmem()] + [anywhere()] * 2,
        scratch_shapes=[
            scratch(width, wide),
            scratch(wide, rows),
            scratch(*shard),
            scratch(*shard),
            pltpu.SemaphoreType.DMA((count + parts,)),
        ],
        compiler_params=params(),
        cost_estimate=cost(4 * rows * width * cols, 4 * width * (cols + 3 * rows)),
        name="tail",
    )(offs, who, dq, own, cosine, sine, hidT, x, gain, dmid, fgain, *w_fac)


def partner(values, axis, flip):
    size = lax.axis_size(axis)
    return lax.ppermute(values, axis, [(i, i ^ flip) for i in range(size)])


def finish_kernel(count, place_ref, *refs):
    near, far, out = refs[:count], refs[count], refs[count + 1]
    low, high = place_ref[0], place_ref[1]
    rows = near[0].shape[0]
    for j, piece in enumerate(near):
        at = (high ^ j) * 2 * rows
        out[pl.ds(pl.multiple_of(at + low * rows, 8), rows), :] = piece[...].astype(f32)
        out[pl.ds(pl.multiple_of(at + (1 - low) * rows, 8), rows), :] = far[j].astype(f32)


def finish(place, near, far):
    rows, cols = near[0].shape
    count = len(near)
    return pl.pallas_call(
        functools.partial(finish_kernel, count),
        out_shape=like(2 * count * rows, cols, dtype=f32),
        in_specs=[smem()] + [vmem()] * (count + 1),
        out_specs=vmem(),
        compiler_params=params(),
        cost_estimate=cost(0, 12 * count * rows * cols),
        name="finish",
    )(place, *near, far)


def after(value, *earlier):
    return lax.optimization_barrier((value, *earlier))[0]


def places(pieces, rows, half):
    me = lax.axis_index("grp")
    at = []
    for flip, which in pieces:
        row = (me ^ flip) * rows
        at += [row if which is None else row + which * half, 0]
    return jnp.stack([jnp.asarray(v, jnp.int32) for v in at])


def add(*terms):
    total = terms[0].astype(f32)
    for term in terms[1:]:
        total = total + term.astype(f32)
    return total.astype(bf16)


def scatter_all(keep, send):
    parts = lax.axis_size("grp")
    me = lax.axis_index("grp")
    both = jnp.stack([keep, send], axis=1).reshape((parts,) + keep.shape[1:])
    both = jnp.take(both, jnp.arange(parts) ^ me, axis=0)
    return lax.psum_scatter(both, "grp", scatter_dimension=0, tiled=False)


class Order:
    def __init__(self):
        self.last = None

    def __call__(self, value, *earlier):
        earlier = earlier if self.last is None else earlier + (self.last,)
        return after(value, *earlier) if earlier else value

    def ran(self, value):
        self.last = value
        return value


class Chunk:
    def __init__(self, order, keep, send):
        self.order, self.keep, self.send = order, keep, send

    def core(self, *earlier):
        self.got = partner(after(self.send, *earlier) if earlier else self.send, "grp", 1)

    def add_core(self):
        kept = self.order(self.keep)
        self.other = self.order.ran(add(kept[1], self.got[1]))
        self.mine = add(kept[0], self.got[0])

    def cross(self, *earlier):
        self.got = partner(after(self.other, *earlier) if earlier else self.other, "grp", 2)

    def add_cross(self):
        low = lax.axis_index("rep") % 2
        rows, cols = self.mine.shape
        cut = lambda v, i: lax.dynamic_index_in_dim(v.reshape(4, 2, rows // 8, cols), i, 1, False)
        mine = self.order(self.mine)
        self.other = self.order.ran(add(cut(mine, 1 - low), cut(self.got, 1 - low)))
        self.mine = add(cut(mine, low), cut(self.got, low))

    def side(self):
        self.got = partner(self.other, "rep", 1)

    def add_side(self):
        high = lax.axis_index("rep") // 2
        cut = lambda v, i: lax.dynamic_index_in_dim(v, i, 0, False)
        mine = self.order(self.mine)
        self.other = [add(cut(mine, high ^ j), cut(self.got, high ^ j)) for j in range(1, 4)]
        self.mine = self.order.ran(add(cut(mine, high), cut(self.got, high)))

    def line(self):
        self.got = [partner(value, "rep", 2 * (j + 1)) for j, value in enumerate(self.other)]

    def add_line(self):
        self.mine = self.order.ran(add(self.order(self.mine), *self.got))

    def gather(self):
        self.whole = lax.all_gather(self.mine, "rep", axis=0, tiled=True)
        return self.whole.astype(f32)

    def spread_line(self):
        self.near = [self.mine] + [partner(self.mine, "rep", 2 * j) for j in range(1, 4)]

    def spread_side(self):
        self.far = partner(self.order.ran(jnp.stack([self.order(self.mine)] + self.near[1:])), "rep", 1)

    def finish(self):
        place = jnp.stack([lax.axis_index("rep") % 2, lax.axis_index("rep") // 2])
        near = [self.order(self.mine)] + self.near[1:]
        return self.order.ran(finish(place.astype(jnp.int32), near, self.far))


def local(
    layer_input,
    branch,
    attention_gain,
    factor_weight,
    output_weight,
    feed_gain,
    gate_weight,
    up_weight,
    down_weight,
    cotangent,
):
    rows = layer_input.shape[1]
    parts = lax.axis_size("grp")
    me = lax.axis_index("grp")
    prompt_parts = parts // 2
    follows = me >= prompt_parts
    chosen = branch[0, jnp.maximum(me - prompt_parts, 0)]
    limit = jnp.where(follows, chosen, me * rows)
    npc = (limit + rows - 1) // rows
    position = jnp.where(follows, chosen, me * rows) + jnp.arange(rows, dtype=jnp.int32)
    info = jnp.stack([me, npc, limit]).astype(jnp.int32)
    freqs = 10000.0 ** (-jnp.arange(HALF).astype(f32) / HALF)
    phase = freqs[:, None] * position.astype(f32)[None, :]
    cosine, sine = jnp.cos(phase), jnp.sin(phase)

    x = layer_input[0]
    upstream = cotangent[0]
    shard_rows, cols = factor_weight.shape
    wide = (cols // 128 + 1) * 128
    factor_wide = jnp.concatenate(
        [
            factor_weight,
            attention_gain[:, None],
            feed_gain[:, None],
            jnp.zeros((shard_rows, wide - cols - 2), bf16),
        ],
        axis=1,
    )
    gather = lambda value: lax.all_gather(value, "grp", axis=0, tiled=True)

    if parts != 4 or lax.axis_size("rep") != 8:
        whole = jnp.zeros((2,), jnp.int32)
        w_fac, w_out, w_down = [gather(factor_wide)], [gather(output_weight)], gather(down_weight)
        w_gate, w_up = [gather(gate_weight)], [gather(up_weight)]
        fac, kv_own, hid_one, gains = front(whole, x, cosine, sine, w_fac, cols)
        kv = [lax.all_gather(kv_own, "grp", axis=0, tiled=False)]
        mixed, lse = attend(info, fac, kv, 0, HEADS)
        mid, hid_two, act, slope, lin, *down_terms = feed(
            whole, info, mixed, x, gains[1:2], upstream, w_out, w_gate, w_up, parts
        )
        dgate, dup = slopes(upstream, w_down, slope, lin)
        gk, gs, uk, us = widths(info, hid_two, dgate, dup, parts)
        result, dmid, fgain, dmix, *out_terms = settle(
            whole, info, upstream, gains[1:2], w_out, w_down, w_gate, w_up,
            act, mid, dgate, dup, mixed, parts,
        )
        dq, *dkv = attend_back(info, fac, kv, dmix, lse, 0, HEADS, ())
        input_grad, *fac_terms = tail(
            whole, info, dq, scatter_all(*dkv), cosine, sine, hid_one, x, gains[0:1], dmid, fgain,
            w_fac, cols, parts,
        )
        terms = (fac_terms, out_terms, (gk, gs), (uk, us), down_terms)
        sums = [lax.psum(scatter_all(*pair), "rep").astype(f32) for pair in terms]
        fac_grad, out_grad, gate_grad, up_grad, down_grad = sums
    else:
        order = Order()
        low = lax.axis_index("rep") % 2
        even = (lax.axis_index("rep") // 2) % 2
        half = shard_rows // 2
        take = lambda v, which: lax.dynamic_slice_in_dim(v, which * half, half, 0)
        quarter = places([(k, None) for k in range(4)], shard_rows, half)
        by_side = places(
            [(0, None), (1, None), (2, low), (2, 1 - low), (3, low), (3, 1 - low)], shard_rows, half
        )
        fac_x = partner(factor_wide, "grp", 2)
        fac_c = partner(factor_wide, "grp", 1)
        fac_xc = partner(fac_x, "grp", 1)
        gate_x = partner(after(take(gate_weight, low), fac_x), "grp", 2)
        gate_c = partner(after(gate_weight, fac_x), "grp", 1)
        w_fac = [factor_wide, fac_c, fac_x, fac_xc]
        fac, kv_own, hid_one, gains = front(quarter, x, cosine, sine, w_fac, cols)
        kv_x = partner(kv_own, "grp", 2)
        kv_c = partner(kv_own, "grp", 1)
        out_x = partner(after(take(output_weight, low), gate_x), "grp", 2)
        out_c = partner(after(output_weight, gate_x), "grp", 1)
        up_c = partner(after(up_weight, gate_x), "grp", 1)
        gate_y = partner(gate_x, "rep", 1)
        gate_xc = partner(gate_x, "grp", 1)
        up_x = partner(after(take(up_weight, low), gate_x, kv_x), "grp", 2)
        kv_xc = partner(kv_x, "grp", 1)
        kv = [kv_own, kv_c, kv_x, kv_xc]
        part = HEADS // 4
        heads = []
        heads.append(attend(info, after(fac, gate_x), kv, 0, part))
        order.ran(heads[-1][0])
        out_y = partner(order(out_x), "rep", 1)
        out_xc = partner(order(out_x), "grp", 1)
        heads.append(attend(info, order(fac, out_x), kv, part, part))
        order.ran(heads[-1][0])
        up_y = partner(order(up_x), "rep", 1)
        up_xc = partner(order(up_x), "grp", 1)
        gate_yc = partner(order(gate_y), "grp", 1)
        out_yc = partner(order(out_y), "grp", 1)
        heads.append(attend(info, order(fac, up_x, gate_y, out_y), kv, 2 * part, part))
        order.ran(heads[-1][0])
        w_down = gather(after(down_weight, up_x))
        heads.append(attend(info, order(fac), kv, 3 * part, part))
        order.ran(heads[-1][0])
        up_yc = partner(order(up_y), "grp", 1)
        mixed = jnp.concatenate([got for got, _ in heads], axis=0)
        lse = jnp.concatenate([got for _, got in heads], axis=0)
        w_out = [output_weight, out_c, out_x, out_y, out_xc, out_yc]
        w_gate = [gate_weight, gate_c, gate_x, gate_y, gate_xc, gate_yc]
        w_up = [up_weight, up_c, up_x, up_y, up_xc, up_yc]

        mid, hid_two, act, slope, lin, *terms = feed(
            by_side, info, mixed, x, gains[1:2], upstream, w_out, w_gate, w_up, parts
        )
        down = Chunk(order, *terms)
        down.core()
        dgate, dup = slopes(upstream, w_down, slope, lin)
        order.ran(dgate)
        down.add_core()
        down.cross()
        gk, gs, uk, us = widths(info, order(hid_two), dgate, dup, parts)
        order.ran(gk)
        gate, up = Chunk(order, gk, gs), Chunk(order, uk, us)
        gate.core()
        up.core(gate.got)
        result, dmid, fgain, dmix, *terms = settle(
            by_side, info, upstream, gains[1:2], w_out, w_down, w_gate, w_up,
            act, mid, dgate, order(dup), mixed, parts,
        )
        order.ran(dmix)
        out = Chunk(order, *terms)
        out.core()
        gate.add_core()
        gate.cross(down.got)
        down.add_cross()
        down.side()
        state = attend_back(info, fac, kv, order(dmix), lse, 0, part, ())
        order.ran(state[0])
        up.add_core()
        out.add_core()
        down.add_side()
        down.line()
        state = attend_back(info, fac, kv, order(dmix), lse, part, part, state)
        order.ran(state[0])
        gate.add_cross()
        gate.side()
        up.cross(gate.other)
        down.add_line()
        down_grad = down.gather()
        state = attend_back(info, fac, kv, order(dmix), lse, 2 * part, part, state)
        order.ran(state[0])
        gate.add_side()
        gate.line()
        dq, *terms = attend_back(info, fac, kv, order(dmix), lse, 3 * part, part, state)
        order.ran(dq)
        dkv = Chunk(order, *terms)
        dkv.core()
        gate.add_line()
        gate_grad = gate.gather()
        dkv.add_core()
        dkv.cross(up.got)
        up.add_cross()
        up.side()
        out.cross(dkv.got)
        own = order.ran(add(order(dkv.mine), dkv.got))
        input_grad, *terms = tail(
            quarter, info, dq, own, cosine, sine, hid_one, x, gains[0:1], dmid, fgain, w_fac, cols, parts
        )
        order.ran(input_grad)
        factor = Chunk(order, *terms)
        factor.core()
        up.add_side()
        up.line()
        factor.add_core()
        factor.cross()
        out.add_cross()
        out.side()
        up.add_line()
        up.spread_line()
        factor.add_cross()
        factor.side()
        out.add_side()
        out.line()
        up.spread_side()
        factor.add_side()
        factor.line()
        out.add_line()
        out.spread_line()
        factor.add_line()
        factor.spread_line()
        out.spread_side()
        up_grad = up.finish()
        factor.spread_side()
        out_grad = out.finish()
        fac_grad = factor.finish()
    return (
        result[None],
        input_grad[None],
        fac_grad[:, cols],
        fac_grad[:, :cols],
        out_grad,
        fac_grad[:, cols + 1],
        gate_grad,
        up_grad,
        down_grad,
    )


def solution(mesh):
    in_specs = (
        P("rep", "grp", None),
        P("rep", None),
        P("grp"),
        P("grp", None),
        P("grp", None),
        P("grp"),
        P("grp", None),
        P("grp", None),
        P("grp", None),
        P("rep", "grp", None),
    )
    out_specs = (
        P("rep", "grp", None),
        P("rep", "grp", None),
        P("grp"),
        P("grp", None),
        P("grp", None),
        P("grp"),
        P("grp", None),
        P("grp", None),
        P("grp", None),
    )
    return jax.shard_map(local, mesh=mesh, in_specs=in_specs, out_specs=out_specs, check_vma=False)
```

```python
import functools

import jax
import jax.numpy as jnp
import numpy as np
from jax import lax
from jax.experimental import pallas as pl
from jax.experimental.pallas import tpu as pltpu
from jax.sharding import PartitionSpec as P

HEADS = 16
HDIM = 64
QRANK = 6
KRANK = 2
HALF = HDIM // 2
QCOLS = QRANK * HEADS + QRANK * HDIM
KVCOLS = 2 * (KRANK * HEADS + KRANK * HDIM)
AQ, BQ = 0, QRANK * HEADS
AK, BK = 0, KRANK * HEADS
AV = BK + KRANK * HDIM
BV = AV + KRANK * HEADS
SCALE = HDIM**-0.5
EXP_SCALE = SCALE * float(np.log2(np.e))
NEG = -1e30
DEPTH = 128
EPS = 1e-05
VMEM_LIMIT = 60 * 2**20

f32 = jnp.float32
bf16 = jnp.bfloat16
NN = (((1,), (0,)), ((), ()))
NT = (((1,), (1,)), ((), ()))
TN = (((0,), (0,)), ((), ()))


def mm(left, right, dims=NN):
    return lax.dot_general(left, right, dims, preferred_element_type=f32)


def vmem():
    return pl.BlockSpec(memory_space=pltpu.VMEM)


def smem():
    return pl.BlockSpec(memory_space=pltpu.SMEM)


def params():
    return pltpu.CompilerParams(vmem_limit_bytes=VMEM_LIMIT)


def cost(flops, nbytes):
    return pl.CostEstimate(flops=int(flops) // 10**5, bytes_accessed=int(nbytes) // 10**5, transcendentals=0)


def weighty(micros):
    return pl.CostEstimate(flops=int(micros * 1.1e9), bytes_accessed=0, transcendentals=0)


def turn(part, cosine, sine):
    first, second = part[:HALF], part[HALF:]
    return first * cosine - second * sine, second * cosine + first * sine


def front_kernel(count, cols, offs, x_ref, cos_ref, sin_ref, *refs):
    pieces = refs[:count]
    fac_ref, kv_ref, hid_ref, gains_ref, w, sems = refs[count:]
    w_in = Mover(sems).pieces(offs, pieces, w)
    xf = x_ref[...].astype(f32)
    normed = xf * lax.rsqrt(jnp.mean(xf * xf, axis=-1, keepdims=True) + EPS)
    wait(w_in)
    last = w.shape[1] - 128
    gains = jnp.transpose(w[:, last:])[cols - last : cols - last + 16].astype(f32)
    gains_ref[...] = gains[0:8]
    hidden = (normed * gains[0:1]).astype(bf16)
    hid_ref[...] = jnp.transpose(hidden)
    raw = jnp.transpose(mm(hidden, w[...]))
    cosine, sine = cos_ref[...], sin_ref[...]
    fac_ref[...] = raw[:QCOLS].astype(bf16)
    kv_ref[...] = raw[QCOLS:cols].astype(bf16)
    for ref, first, at in [(fac_ref, 0, BQ + r * HDIM) for r in range(QRANK)] + [
        (kv_ref, QCOLS, BK + r * HDIM) for r in range(KRANK)
    ]:
        one, two = turn(raw[first + at : first + at + HDIM], cosine, sine)
        ref[at : at + HALF, :] = one.astype(bf16)
        ref[at + HALF : at + HDIM, :] = two.astype(bf16)


def front(offs, x, cosine, sine, w_fac, cols):
    rows, width = x.shape
    wide = w_fac[0].shape[1]
    count = len(w_fac)
    return pl.pallas_call(
        functools.partial(front_kernel, count, cols),
        out_shape=[
            like(QCOLS, rows),
            like(cols - QCOLS, rows),
            like(width, rows),
            like(8, width, dtype=f32),
        ],
        in_specs=[smem()] + [vmem()] * 3 + [anywhere()] * count,
        out_specs=[vmem()] * 4,
        scratch_shapes=[scratch(width, wide), pltpu.SemaphoreType.DMA((count,))],
        compiler_params=params(),
        cost_estimate=cost(2 * rows * width * cols, 4 * width * (cols + rows)),
        name="front",
    )(offs, x, cosine, sine, *w_fac)


def load_factors(fac_ref, kv_refs, facf, kvf, qT, me):
    facf[...] = fac_ref[...].astype(f32)
    if len(kv_refs) == 1:

        def load(j, _):
            kvf[j] = kv_refs[0][j].astype(f32)
            return 0

        lax.fori_loop(0, kvf.shape[0], load, 0)
    else:
        for flip, ref in enumerate(kv_refs):
            kvf[me ^ flip] = ref[...].astype(f32)
    row = lax.broadcasted_iota(jnp.int32, (DEPTH - HDIM, qT.shape[1]), 0)
    qT[HDIM:DEPTH, :] = jnp.where(row == 0, 1.0, 0.0).astype(bf16)


def build_query(facf, qT, h):
    total = facf[pl.ds(AQ + h, 1), :] * facf[BQ : BQ + HDIM, :]
    for r in range(1, QRANK):
        total += facf[pl.ds(AQ + r * HEADS + h, 1), :] * facf[BQ + r * HDIM : BQ + (r + 1) * HDIM, :]
    qT[0:HDIM, :] = (total * (1.0 / QRANK)).astype(bf16)


def build_pair(kvf, j, h, a_at, b_at):
    total = kvf[j, pl.ds(a_at + h, 1), :] * kvf[j, b_at : b_at + HDIM, :]
    for r in range(1, KRANK):
        total += (
            kvf[j, pl.ds(a_at + r * HEADS + h, 1), :]
            * kvf[j, b_at + r * HDIM : b_at + (r + 1) * HDIM, :]
        )
    return (total * (1.0 / KRANK)).astype(bf16)


def build_key(kvf, kT, j, h, limit):
    span = kT.shape[1]
    kT[0:HDIM, :] = build_pair(kvf, j, h, AK, BK)
    if limit is None:
        kT[HDIM:DEPTH, :] = jnp.zeros((DEPTH - HDIM, span), bf16)
    else:
        row = lax.broadcasted_iota(jnp.int32, (DEPTH - HDIM, span), 0)
        key = j * span + lax.broadcasted_iota(jnp.int32, (DEPTH - HDIM, span), 1)
        kT[HDIM:DEPTH, :] = jnp.where((row == 0) & (key >= limit), NEG, 0.0).astype(bf16)


def causal(scores):
    key = lax.broadcasted_iota(jnp.int32, scores.shape, 0)
    query = lax.broadcasted_iota(jnp.int32, scores.shape, 1)
    return jnp.where(key <= query, scores, NEG)


def attend_kernel(first, heads, count, info_ref, fac_ref, *refs):
    kv_refs, (out_ref, lse_ref, facf, kvf, qT, kT, s_ref) = refs[:count], refs[count:]
    me, npc, limit = info_ref[0], info_ref[1], info_ref[2]
    rows = fac_ref.shape[1]
    load_factors(fac_ref, kv_refs, facf, kvf, qT, me)

    def head(step, _):
        h = first + step
        build_query(facf, qT, h)

        def chunk(j, top):
            build_key(kvf, kT, j, h, limit)
            scores = mm(kT[...], qT[...], TN)
            s_ref[j] = scores
            return jnp.maximum(top, jnp.max(scores, axis=0, keepdims=True))

        top = lax.fori_loop(0, npc, chunk, jnp.full((1, rows), NEG, f32))
        build_key(kvf, kT, me, h, None)
        scores = causal(mm(kT[...], qT[...], TN))
        s_ref[npc] = scores
        top = jnp.maximum(top, jnp.max(scores, axis=0, keepdims=True)) * EXP_SCALE

        def weigh(j, mass):
            probs = jnp.exp2(s_ref[j] * EXP_SCALE - top)
            s_ref[j] = probs
            return mass + jnp.sum(probs, axis=0, keepdims=True)

        mass = lax.fori_loop(0, npc + 1, weigh, jnp.zeros((1, rows), f32))
        lse_ref[pl.ds(step, 1), :] = top + jnp.log2(mass)
        share = 1.0 / mass

        def gather(j, total):
            at = jnp.where(j == npc, me, j)
            return total + mm(build_pair(kvf, at, h, AV, BV), (s_ref[j] * share).astype(bf16))

        total = lax.fori_loop(0, npc + 1, gather, jnp.zeros((HDIM, rows), f32))
        out_ref[pl.ds(pl.multiple_of(step * HDIM, HDIM), HDIM), :] = total.astype(bf16)
        return 0

    lax.fori_loop(0, heads, head, 0)


def kv_sizes(kv):
    return kv[0].shape if len(kv) == 1 else (len(kv),) + kv[0].shape


def attend(info, fac, kv, first, heads):
    parts, cols, rows = kv_sizes(kv)
    seen = min(parts, parts // 2 + 1)
    return pl.pallas_call(
        functools.partial(attend_kernel, first, heads, len(kv)),
        out_shape=[
            jax.ShapeDtypeStruct((heads * HDIM, rows), bf16),
            jax.ShapeDtypeStruct((heads, rows), f32),
        ],
        in_specs=[smem(), vmem()] + [vmem()] * len(kv),
        out_specs=[vmem()] * 2,
        scratch_shapes=[
            pltpu.VMEM((QCOLS, rows), f32),
            pltpu.VMEM((parts, cols, rows), f32),
            pltpu.VMEM((DEPTH, rows), bf16),
            pltpu.VMEM((DEPTH, rows), bf16),
            pltpu.VMEM((seen, rows, rows), f32),
        ],
        compiler_params=params(),
        cost_estimate=cost(16 * 2 * heads * 256 * rows * rows * seen, 4 * cols * rows * parts),
        name="attend",
    )(info, fac, *kv)


def attend_back_kernel(
    first, heads, final, count, count_out, blocks, info_ref, fac_ref, grad_ref, *refs
):
    kv_refs, lse_refs, refs = refs[:count], refs[count : count + blocks], refs[count + blocks :]
    if first:
        dq_in, dkv_in, *refs = refs
    dq_ref, *refs = refs
    if final:
        outs, refs = refs[:count_out], refs[count_out:]
        dkvf, *refs = refs
    else:
        dkvf, *refs = refs
    facf, kvf, qT, kTs, p_ref, dp_ref, lse_ref = refs
    for i, ref in enumerate(lse_refs):
        lse_ref[i * ref.shape[0] : (i + 1) * ref.shape[0], :] = ref[...]
    me, npc, limit = info_ref[0], info_ref[1], info_ref[2]
    parts, _, rows = kvf.shape
    load_factors(fac_ref, kv_refs, facf, kvf, qT, me)

    def begin(j, _):
        dkvf[j] = dkv_in[j] if first else jnp.zeros(dkvf.shape[1:], f32)
        return 0

    lax.fori_loop(0, parts, begin, 0)
    dq_ref[...] = dq_in[...] if first else jnp.zeros(dq_ref.shape, f32)

    def head(step, _):
        h = first + step
        build_query(facf, qT, h)
        grad = grad_ref[pl.ds(pl.multiple_of(h * HDIM, HDIM), HDIM), :]
        lse = lse_ref[pl.ds(h, 1), :]

        def probe(slot, at, scores, delta):
            probs = jnp.exp2(scores * EXP_SCALE - lse)
            p_ref[slot] = probs
            prob_grad = mm(build_pair(kvf, at, h, AV, BV), grad, TN)
            dp_ref[slot] = prob_grad
            return delta + jnp.sum(probs * prob_grad, axis=0, keepdims=True)

        def chunk(j, delta):
            build_key(kvf, kTs.at[j], j, h, limit)
            return probe(j, j, mm(kTs[j], qT[...], TN), delta)

        delta = lax.fori_loop(0, npc, chunk, jnp.zeros((1, rows), f32))
        build_key(kvf, kTs.at[npc], me, h, None)
        delta = probe(npc, me, causal(mm(kTs[npc], qT[...], TN)), delta)

        def pull(j, total):
            at = jnp.where(j == npc, me, j)
            probs = p_ref[j]
            score_grad = (probs * (dp_ref[j] - delta)).astype(bf16)
            key_grad = mm(qT[0:HDIM, :], score_grad, NT) * (SCALE / KRANK)
            value_grad = mm(grad, probs.astype(bf16), NT) * (1.0 / KRANK)
            for a_at, b_at, got in ((AK, BK, key_grad), (AV, BV, value_grad)):
                for r in range(KRANK):
                    a_row = pl.ds(a_at + r * HEADS + h, 1)
                    b_rows = slice(b_at + r * HDIM, b_at + (r + 1) * HDIM)
                    dkvf[at, a_row, :] = jnp.sum(got * kvf[at, b_rows, :], axis=0, keepdims=True)
                    dkvf[at, b_rows, :] += got * kvf[at, a_row, :]
            return total + mm(kTs[j, 0:HDIM, :], score_grad)

        query_grad = lax.fori_loop(0, npc + 1, pull, jnp.zeros((HDIM, rows), f32)) * (SCALE / QRANK)
        for r in range(QRANK):
            a_row = pl.ds(AQ + r * HEADS + h, 1)
            b_rows = slice(BQ + r * HDIM, BQ + (r + 1) * HDIM)
            dq_ref[a_row, :] = jnp.sum(query_grad * facf[b_rows, :], axis=0, keepdims=True)
            dq_ref[b_rows, :] += query_grad * facf[a_row, :]
        return 0

    lax.fori_loop(0, heads, head, 0)
    if final:
        for flip in range(parts):
            outs[flip % 2][flip // 2] = dkvf[me ^ flip].astype(bf16)


def attend_back(info, fac, kv, grad, lse, first, heads, so_far, declared=None):
    parts, cols, rows = kv_sizes(kv)
    seen = min(parts, parts // 2 + 1)
    final = first + heads == HEADS
    gathered = [like(parts // 2, cols, rows)] * 2 if final else [like(parts, cols, rows, dtype=f32)]
    return pl.pallas_call(
        functools.partial(
            attend_back_kernel, first, heads, final, len(kv), len(gathered), len(lse)
        ),
        out_shape=[like(QCOLS, rows, dtype=f32)] + gathered,
        in_specs=[smem()] + [vmem()] * (2 + len(kv) + len(lse) + len(so_far)),
        out_specs=[vmem()] * (1 + len(gathered)),
        scratch_shapes=([pltpu.VMEM((parts, cols, rows), f32)] if final else [])
        + [
            pltpu.VMEM((QCOLS, rows), f32),
            pltpu.VMEM((parts, cols, rows), f32),
            pltpu.VMEM((DEPTH, rows), bf16),
            pltpu.VMEM((seen, DEPTH, rows), bf16),
            pltpu.VMEM((seen, rows, rows), f32),
            pltpu.VMEM((seen, rows, rows), f32),
            pltpu.VMEM((HEADS, rows), f32),
        ],
        compiler_params=params(),
        cost_estimate=declared or cost(heads * rows * rows, 8 * cols * rows * parts),
        name="attend_back",
    )(info, fac, grad, *kv, *lse, *so_far)


class Mover:
    def __init__(self, sems):
        self.sems = sems
        self.used = 0

    def start(self, src, dst):
        copy = pltpu.make_async_copy(src, dst, self.sems.at[self.used])
        self.used += 1
        copy.start()
        return copy

    def pieces(self, offsets, refs, dst, first=0):
        copies = []
        for i, piece in enumerate(refs):
            rows, cols = piece.shape
            at = pl.ds(pl.multiple_of(offsets[first + 2 * i], 16), rows)
            if cols == dst.shape[1]:
                where = dst.at[at]
            else:
                where = dst.at[at, pl.ds(pl.multiple_of(offsets[first + 2 * i + 1], 128), cols)]
            copies.append(self.start(piece, where))
        return copies


def wait(copies):
    for copy in copies:
        copy.wait()


def anywhere():
    return pl.BlockSpec(memory_space=pl.ANY)


def like(*shape, dtype=bf16):
    return jax.ShapeDtypeStruct(shape, dtype)


def scratch(*shape, dtype=bf16):
    return pltpu.VMEM(shape, dtype)


TILE = 256


def norm_back(grad_hidden, normed, scale, gain):
    grad_normed = grad_hidden * gain
    gain_grad = jnp.sum(grad_hidden * normed, axis=0, keepdims=True)
    mean = jnp.mean(grad_normed * normed, axis=-1, keepdims=True)
    return gain_grad, scale * (grad_normed - normed * mean)


def shard_products(me, left, right, pair, mover, pair_out):
    copies = []
    count, rows, cols = pair[0].shape
    step = rows if rows <= 352 else rows // 2
    width = cols // 2 if cols % 256 == 0 and cols > 2048 else cols
    for odd in (1, 0):
        for j in range(count):
            row = (me ^ (2 * j + odd)) * rows
            for low in range(0, rows, step):
                lhs = left[pl.ds(pl.multiple_of(row + low, 16), step), :]
                for at in range(0, cols, width):
                    pair[odd][j, low : low + step, at : at + width] = mm(
                        lhs, right[:, at : at + width]
                    ).astype(bf16)
            copies.append(mover.start(pair[odd].at[j], pair_out[odd].at[j]))
    return copies


def feed_kernel(count, blocks, offs, x_ref, gain_ref, *refs):
    mix_refs, refs = refs[:blocks], refs[blocks:]
    out_pieces, gate_pieces, lift_pieces = (refs[i * count : (i + 1) * count] for i in range(3))
    refs = refs[3 * count :]
    (mid_o, hid_o, act_o, slope_o, lin_o, actT_o) = refs[:6]
    (wo, wg, wu, mid, hid, hidT, act, slope, lin, actT, sems) = refs[6:]
    mover = Mover(sems)
    wo_in = mover.pieces(offs, out_pieces, wo)
    wg_in = mover.pieces(offs, gate_pieces, wg)
    wu_in = mover.pieces(offs, lift_pieces, wu, 2 * count)
    mix = jnp.concatenate([jnp.transpose(ref[...]) for ref in mix_refs], axis=1)
    wait(wo_in)
    middle = x_ref[...].astype(f32) + mm(mix, wo[...])
    mid[...] = middle
    scale = lax.rsqrt(jnp.mean(middle * middle, axis=-1, keepdims=True) + EPS)
    hidden = (middle * scale * gain_ref[...]).astype(bf16)
    hid[...] = hidden
    hidT[...] = jnp.transpose(hidden)
    done = [mover.start(mid, mid_o), mover.start(hidT, hid_o)]
    wait(wg_in)
    wait(wu_in)

    def tile(j, _):
        cols = pl.ds(pl.multiple_of(j * TILE, TILE), TILE)
        gate = mm(hid[...], wg[:, cols])
        up = mm(hid[...], wu[:, cols])
        sig = jax.nn.sigmoid(gate)
        line = gate * sig
        active = (line * up).astype(bf16)
        act[:, cols] = active
        lin[:, cols] = line.astype(bf16)
        slope[:, cols] = (up * sig * (1.0 + gate * (1.0 - sig))).astype(bf16)
        actT[cols, :] = jnp.transpose(active)
        return 0

    lax.fori_loop(0, wg.shape[1] // TILE, tile, 0, unroll=True)
    done += [mover.start(act, act_o), mover.start(lin, lin_o), mover.start(slope, slope_o)]
    done.append(mover.start(actT, actT_o))
    wait(done)


def feed(offs, mix, x, gain, w_out, w_gate, w_up):
    rows, width = x.shape
    inner = w_gate[0].shape[1]
    count = len(w_gate)
    return pl.pallas_call(
        functools.partial(feed_kernel, count, len(mix)),
        out_shape=[
            like(rows, width, dtype=f32),
            like(width, rows),
            like(rows, inner),
            like(rows, inner),
            like(rows, inner),
        ]
        + [like(inner, rows)],
        in_specs=[smem()] + [vmem()] * (2 + len(mix)) + [anywhere()] * (3 * count),
        out_specs=[anywhere()] * 6,
        scratch_shapes=[
            scratch(width, width),
            scratch(width, inner),
            scratch(width, inner),
            scratch(rows, width, dtype=f32),
            scratch(rows, width),
            scratch(width, rows),
            scratch(rows, inner),
            scratch(rows, inner),
            scratch(rows, inner),
            scratch(inner, rows),
            pltpu.SemaphoreType.DMA((3 * count + 6,)),
        ],
        compiler_params=params(),
        cost_estimate=cost(2 * rows * width * (width + 3 * inner), 2 * inner * (3 * width + 3 * rows)),
        name="feed",
    )(offs, x, gain, *mix, *w_out, *w_gate, *w_up)


def slopes_kernel(count, offs, slope_ref, lin_ref, c_ref, *refs):
    pieces, (dg_o, du_o, wd, dg, du, sems) = refs[:count], refs[count:]
    mover = Mover(sems)
    wait(mover.pieces(offs, pieces, wd))

    def tile(j, _):
        cols = pl.ds(pl.multiple_of(j * TILE, 128), TILE)
        grad = mm(c_ref[...], wd[cols, :], NT)
        dg[:, cols] = (grad * slope_ref[:, cols].astype(f32)).astype(bf16)
        du[:, cols] = (grad * lin_ref[:, cols].astype(f32)).astype(bf16)
        return 0

    lax.fori_loop(0, wd.shape[0] // TILE, tile, 0, unroll=True)
    wait([mover.start(dg, dg_o), mover.start(du, du_o)])


def slopes(offs, upstream, w_down, slope, lin):
    rows, width = upstream.shape
    inner = slope.shape[1]
    count = len(w_down)
    return pl.pallas_call(
        functools.partial(slopes_kernel, count),
        out_shape=[like(rows, inner)] * 2,
        in_specs=[smem()] + [vmem()] * 3 + [anywhere()] * count,
        out_specs=[anywhere()] * 2,
        scratch_shapes=[
            scratch(inner, width),
            scratch(rows, inner),
            scratch(rows, inner),
            pltpu.SemaphoreType.DMA((count + 2,)),
        ],
        compiler_params=params(),
        cost_estimate=cost(2 * rows * width * inner, 2 * inner * (width + 4 * rows)),
        name="slopes",
    )(offs, slope, lin, upstream, *w_down)


def products_kernel(who, left, right, *refs):
    outs, pair, sems = refs[0:2], refs[2:4], refs[4]
    wait(shard_products(who[0], left, right, pair, Mover(sems), outs))


def products(who, left, right, parts):
    width, rows = left.shape
    inner = right.shape[1]
    pair = (parts // 2, width // parts, inner)
    return pl.pallas_call(
        products_kernel,
        out_shape=[like(*pair)] * 2,
        in_specs=[smem()] + [vmem()] * 2,
        out_specs=[anywhere()] * 2,
        scratch_shapes=[scratch(*pair)] * 2 + [pltpu.SemaphoreType.DMA((parts,))],
        compiler_params=params(),
        cost_estimate=cost(2 * rows * width * inner, 2 * inner * (width + rows)),
        name="products",
    )(who, left, right)


def middle_kernel(count, blocks, offs, who, c_ref, gain_ref, *refs):
    out_pieces, gate_pieces, lift_pieces = (refs[i * count : (i + 1) * count] for i in range(3))
    mix_refs, refs = refs[3 * count : 3 * count + blocks], refs[3 * count + blocks :]
    dg_i, du_i, mid_i, dmid_o, fgain, dmix, *refs = refs
    outs, (wg, wu, wo, dg, du, mid, dhid, branch, mix), pair, sems = refs[:2], refs[2:11], refs[11:13], refs[13]
    mover = Mover(sems)
    in_dg = [mover.start(dg_i, dg)]
    in_wg = mover.pieces(offs, gate_pieces, wg)
    in_du = [mover.start(du_i, du)]
    in_wu = mover.pieces(offs, lift_pieces, wu, 2 * count)
    in_mid = [mover.start(mid_i, mid)]
    in_wo = mover.pieces(offs, out_pieces, wo)
    width = wg.shape[0]

    def back(which, j):
        at = pl.ds(pl.multiple_of(j * TILE, TILE), TILE)
        if which == 0:
            dhid[:, at] = mm(dg[...], wg[at, :], NT)
        else:
            dhid[:, at] += mm(du[...], wu[at, :], NT)
        return 0

    wait(in_dg + in_wg)
    lax.fori_loop(0, width // TILE, lambda j, _: back(0, j), 0, unroll=True)
    wait(in_du + in_wu)
    lax.fori_loop(0, width // TILE, lambda j, _: back(1, j), 0, unroll=True)
    wait(in_mid + in_wo)
    middle = mid[...]
    scale = lax.rsqrt(jnp.mean(middle * middle, axis=-1, keepdims=True) + EPS)
    gain_grad, part = norm_back(dhid[...], middle * scale, scale, gain_ref[...])
    fgain[...] = jnp.broadcast_to(gain_grad, fgain.shape)
    total = c_ref[...].astype(f32) + part
    dhid[...] = total
    branch[...] = total.astype(bf16)
    done = [mover.start(dhid, dmid_o)]
    for i, ref in enumerate(mix_refs):
        size = ref.shape[0]
        mix[i * size : (i + 1) * size, :] = ref[...]
    done += shard_products(who[0], mix, branch, pair, mover, outs)
    dmix[...] = mm(wo[...], branch[...], NT).astype(bf16)
    wait(done)


def middle_grads(offs, who, upstream, gain, mix, w_out, w_gate, w_up, dg, du, mid, parts):
    rows, width = upstream.shape
    pair = (parts // 2, width // parts, width)
    inner = dg.shape[1]
    count = len(w_gate)
    return pl.pallas_call(
        functools.partial(middle_kernel, count, len(mix)),
        out_shape=[
            like(rows, width, dtype=f32),
            like(8, width, dtype=f32),
            like(width, rows),
            like(*pair),
            like(*pair),
        ],
        in_specs=[smem()] * 2
        + [vmem()] * 2
        + [anywhere()] * (3 * count)
        + [vmem()] * len(mix)
        + [anywhere()] * 3,
        out_specs=[anywhere()] + [vmem()] * 2 + [anywhere()] * 2,
        scratch_shapes=[
            scratch(width, inner),
            scratch(width, inner),
            scratch(width, width),
            scratch(rows, inner),
            scratch(rows, inner),
            scratch(rows, width, dtype=f32),
            scratch(rows, width, dtype=f32),
            scratch(rows, width),
            scratch(width, rows),
            scratch(*pair),
            scratch(*pair),
            pltpu.SemaphoreType.DMA((3 * count + 4 + parts,)),
        ],
        compiler_params=params(),
        cost_estimate=cost(2 * rows * width * (2 * inner + width), 4 * inner * (width + rows)),
        name="middle_grads",
    )(offs, who, upstream, gain, *w_out, *w_gate, *w_up, *mix, dg, du, mid)


def settle_kernel(count, offs, who, hid_ref, dg_ref, act_i, mid_i, *refs):
    pieces, (res, *outs, wd, act, mid, keep, send, sems) = refs[:count], refs[count:]
    mover = Mover(sems)
    later = [mover.start(act_i, act), mover.start(mid_i, mid)] + mover.pieces(offs, pieces, wd)
    done = shard_products(who[0], hid_ref, dg_ref, (keep, send), mover, outs)
    wait(later)

    def forth(j, _):
        at = pl.ds(pl.multiple_of(j * TILE, TILE), TILE)
        res[:, at] = (mid[:, at] + mm(act[...], wd[:, at])).astype(bf16)
        return 0

    lax.fori_loop(0, wd.shape[1] // TILE, forth, 0, unroll=True)
    wait(done)


def settle(offs, who, hidT, dg, act, mid, w_down, parts):
    rows, width = mid.shape
    count = len(w_down)
    inner = act.shape[1]
    pair = (parts // 2, width // parts, inner)
    return pl.pallas_call(
        functools.partial(settle_kernel, count),
        out_shape=[like(rows, width), like(*pair), like(*pair)],
        in_specs=[smem()] * 2 + [vmem()] * 2 + [anywhere()] * (2 + count),
        out_specs=[vmem()] + [anywhere()] * 2,
        scratch_shapes=[
            scratch(inner, width),
            scratch(rows, inner),
            scratch(rows, width, dtype=f32),
            scratch(*pair),
            scratch(*pair),
            pltpu.SemaphoreType.DMA((2 + count + parts,)),
        ],
        compiler_params=params(),
        cost_estimate=cost(2 * rows * width * (2 * inner + width), 2 * inner * (3 * width + rows)),
        name="settle",
    )(offs, who, hidT, dg, act, mid, *w_down)


def tail_kernel(count, cols, offs, who, dq_ref, own_ref, cos_ref, sin_ref, hid_ref, x_ref, gain_ref, dmid_ref, fgain_ref, *refs):
    pieces = refs[:count]
    grad_ref, *outs = refs[count:]
    *outs, w, raw, sems = outs
    mover = Mover(sems)
    w_in = mover.pieces(offs, pieces, w)
    cosine, sine = cos_ref[...], -sin_ref[...]
    raw[0:QCOLS, :] = dq_ref[...].astype(bf16)
    raw[QCOLS:cols, :] = own_ref[...]
    raw[cols:, :] = jnp.zeros((raw.shape[0] - cols, raw.shape[1]), bf16)
    for r in range(QRANK):
        at = BQ + r * HDIM
        one, two = turn(dq_ref[at : at + HDIM, :], cosine, sine)
        raw[at : at + HALF, :] = one.astype(bf16)
        raw[at + HALF : at + HDIM, :] = two.astype(bf16)
    for r in range(KRANK):
        at = BK + r * HDIM
        one, two = turn(own_ref[at : at + HDIM, :].astype(f32), cosine, sine)
        raw[QCOLS + at : QCOLS + at + HALF, :] = one.astype(bf16)
        raw[QCOLS + at + HALF : QCOLS + at + HDIM, :] = two.astype(bf16)
    draw = jnp.transpose(raw[...])
    wait(w_in)
    xf = x_ref[...].astype(f32)
    scale = lax.rsqrt(jnp.mean(xf * xf, axis=-1, keepdims=True) + EPS)
    dhid = mm(draw, w[...], NT)
    gain_grad, part = norm_back(dhid, xf * scale, scale, gain_ref[...])
    grad_ref[...] = dmid_ref[...] + part
    width = raw.shape[0]
    line = lax.broadcasted_iota(jnp.int32, (128, gain_grad.shape[1]), 0) + (width - 128)
    both = jnp.where(line == cols, gain_grad, jnp.where(line == cols + 1, fgain_ref[0:1, :], 0.0))
    both = jnp.transpose(both)
    raw_gain = both.astype(bf16)
    w[:, 0:128] = raw_gain
    count_out, rows, _ = outs[0].shape
    for flip in range(2 * count_out):
        at = pl.ds(pl.multiple_of((who[0] ^ flip) * rows, 16), rows)
        got = mm(hid_ref[at, :], draw)
        out = outs[flip % 2]
        out[flip // 2, :, 0 : width - 128] = got[:, 0 : width - 128].astype(bf16)
        out[flip // 2, :, width - 128 :] = (got[:, width - 128 :] + w[at, 0:128].astype(f32)).astype(bf16)


def tail(offs, who, dq, own, cosine, sine, hidT, x, gain, dmid, fgain, w_fac, cols, parts):
    rows, width = x.shape
    wide = w_fac[0].shape[1]
    count = len(w_fac)
    shard = (parts // 2, width // parts, wide)
    return pl.pallas_call(
        functools.partial(tail_kernel, count, cols),
        out_shape=[like(rows, width, dtype=f32)] + [like(*shard)] * 2,
        in_specs=[smem()] * 2 + [vmem()] * 9 + [anywhere()] * count,
        out_specs=[vmem()] * 3,
        scratch_shapes=[
            scratch(width, wide),
            scratch(wide, rows),
            pltpu.SemaphoreType.DMA((count,)),
        ],
        compiler_params=params(),
        cost_estimate=cost(4 * rows * width * cols, 4 * width * (cols + 3 * rows)),
        name="tail",
    )(offs, who, dq, own, cosine, sine, hidT, x, gain, dmid, fgain, *w_fac)


def partner(values, axis, flip):
    size = lax.axis_size(axis)
    return lax.ppermute(values, axis, [(i, i ^ flip) for i in range(size)])


def after(value, *earlier):
    if not earlier:
        return value
    return lax.optimization_barrier((value, *earlier))[0]


def places(pieces, rows, half):
    me = lax.axis_index("grp")
    at = []
    for flip, which in pieces:
        row = (me ^ flip) * rows
        at += [row if which is None else row + which * half, 0]
    return jnp.stack([jnp.asarray(v, jnp.int32) for v in at])


def total(*terms):
    got = terms[0].astype(f32)
    for term in terms[1:]:
        got = got + term.astype(f32)
    return got.astype(bf16)


def add_pairs_kernel(*refs):
    mine, other = refs[-2:]
    at = 0
    for keep, got in zip(refs[:-2:2], refs[1:-2:2]):
        cols = slice(at, at + keep.shape[2])
        mine[:, cols] = total(keep[0], got[0])
        other[:, cols] = total(keep[1], got[1])
        at += keep.shape[2]


def add_pairs(groups):
    rows = groups[0][0].shape[1]
    wide = sum(keep.shape[2] for keep, _ in groups)
    steps = next(n for n in (4, 2, 1) if n == 1 or (rows % (16 * n) == 0 and rows * wide > 2**19))
    out = pl.BlockSpec((rows // steps, wide), lambda i: (i, 0))
    terms = [term for group in groups for term in group]
    return pl.pallas_call(
        add_pairs_kernel,
        grid=(steps,),
        out_shape=[like(rows, wide)] * 2,
        in_specs=[pl.BlockSpec((2, rows // steps, v.shape[2]), lambda i: (0, i, 0)) for v in terms],
        out_specs=[out] * 2,
        compiler_params=params(),
        cost_estimate=cost(1, 1),
        name="add_pairs",
    )(*terms)


def halve_kernel(place, keep_one, keep_two, send_one, send_two, keep, send):
    keep[...] = total(keep_one[...], keep_two[...])
    send[...] = total(send_one[...], send_two[...])


def halve(place, one, two):
    rows, cols = one.shape[0] // 8, one.shape[1]
    one, two = (v.reshape(8, rows, cols) for v in (one, two))

    def piece(flip):
        def index(i, place):
            at = place[0] ^ ((i >> 1) * place[2]) ^ ((i & 1) * place[3])
            return (at ^ place[1] if flip else at, 0, 0)

        return pl.BlockSpec((1, rows, cols), index)

    out = pl.BlockSpec((1, rows, cols), lambda i, place: (i, 0, 0))
    return pl.pallas_call(
        halve_kernel,
        grid_spec=pltpu.PrefetchScalarGridSpec(
            num_scalar_prefetch=1,
            grid=(4,),
            in_specs=[piece(False)] * 2 + [piece(True)] * 2,
            out_specs=[out] * 2,
        ),
        out_shape=[like(4, rows, cols)] * 2,
        compiler_params=params(),
        cost_estimate=cost(1, 1),
        name="halve",
    )(place, one, two, one, two)


def batch_kernel(tasks, *refs):
    ins, outs = refs[: 2 * len(tasks)], list(refs[2 * len(tasks) :])
    for i, (kind, flip) in enumerate(tasks):
        one, two = ins[2 * i : 2 * i + 2]
        out = outs.pop(0)
        if kind == "split":
            half = out.shape[0]
            out[...] = total(one[:half], two[:half])
            outs.pop(0)[...] = total(one[half:], two[half:])
        elif kind == "pair":
            out[...] = total(one[0], two[0])
            outs.pop(0)[...] = total(one[1], two[1])
        elif kind == "join":
            half = one.shape[0]
            out[:half] = one[...]
            out[half:] = two[...]
        elif flip:
            for k in range(out.shape[0]):
                out[k] = total(one[k], two[k ^ flip])
        else:
            out[...] = total(one[...], two[...])


def batch(tasks):
    shapes, counts = [], []
    for kind, _, one, _ in tasks:
        first, rest = one.shape[0], one.shape[1:]
        got = {
            "split": [(first // 2,) + rest] * 2,
            "pair": [rest] * 2,
            "join": [(2 * first,) + rest],
            "sum": [one.shape],
        }[kind]
        shapes += got
        counts.append(len(got))
    outs = pl.pallas_call(
        functools.partial(batch_kernel, [task[:2] for task in tasks]),
        out_shape=[like(*shape) for shape in shapes],
        in_specs=[vmem()] * (2 * len(tasks)),
        out_specs=[vmem()] * len(shapes),
        compiler_params=params(),
        cost_estimate=cost(1, 1),
        name="batch",
    )(*[value for task in tasks for value in task[2:]])
    groups = []
    for count in counts:
        groups.append(outs[:count])
        outs = outs[count:]
    return groups


def finish_kernel(widths, place, near, far, *outs):
    _, rows, wide = near.shape
    last = wide - 128
    for side, value in ((0, near), (1, far)):
        for k in range(4):
            at = place[0] ^ (side * place[1]) ^ ((k >> 1) * place[2]) ^ ((k & 1) * place[3])
            row = pl.ds(pl.multiple_of(at * rows, 8), rows)
            col = 0
            for out, cols in zip(outs, widths):
                out[row, :] = value[k, :, col : col + cols].astype(f32)
                col += cols
            if col < wide:
                outs[-1][row, :] = value[k, :, last:].astype(f32)
    if sum(widths) < wide:
        outs[-2][...] = jnp.transpose(outs[-1][...])[sum(widths) - last : sum(widths) - last + 8]


def finish(place, near, far, widths):
    _, rows, wide = near.shape
    shapes = [like(8 * rows, cols, dtype=f32) for cols in widths]
    more = sum(widths) < wide
    return pl.pallas_call(
        functools.partial(finish_kernel, widths),
        out_shape=shapes + ([like(8, 8 * rows, dtype=f32)] if more else []),
        in_specs=[smem()] + [vmem()] * 2,
        out_specs=[vmem()] * (len(shapes) + more),
        scratch_shapes=[scratch(8 * rows, 128, dtype=f32)] if more else [],
        compiler_params=params(),
        cost_estimate=cost(1, 1),
        name="finish",
    )(place, near, far)


def scatter_all(keep, send):
    me = lax.axis_index("grp")
    both = jnp.stack([keep, send], axis=1)
    both = both.reshape((-1,) + both.shape[2:])
    both = jnp.take(both, jnp.arange(both.shape[0]) ^ me, axis=0)
    return lax.psum_scatter(both, "grp", scatter_dimension=0, tiled=False)


class Order:
    def __init__(self):
        self.last = None
        self.before = ()
        self.tasks = []

    def add(self, kind, flip, one, two, then):
        self.tasks.append(((kind, flip, self.free(one), two), then))

    def flush(self):
        groups = batch([task for task, _ in self.tasks])
        for (_, then), group in zip(self.tasks, groups):
            then(*group)
        self.tasks = []

    def __call__(self, value, *earlier):
        earlier = earlier if self.last is None else earlier + (self.last,)
        return after(value, *earlier) if earlier else value

    def phase(self, *results):
        self.before = results
        self.last = None

    def now(self, value, *earlier):
        last = () if self.last is None else (self.last,)
        return after(value, *self.before, *earlier, *last)

    def free(self, value):
        return after(value, *self.before)

    def ran(self, value):
        self.last = value
        return value


BITS = ((1, 2, 4), (2, 1, 4))


def along(values, step):
    reps, parts = lax.axis_size("rep"), lax.axis_size("grp")
    pairs = [
        (r * parts + g, (r ^ BITS[g % 2][step]) * parts + g)
        for r in range(reps)
        for g in range(parts)
    ]
    return lax.ppermute(values, ("rep", "grp"), pairs)


class Chunk:
    def __init__(self, order, place, *pairs):
        self.order, self.place, self.pairs = order, place, pairs

    def core(self):
        send = [after(pair[1], *self.order.before) for pair in self.pairs]
        self.got = [partner(value, "grp", 1) for value in send]

    def add_core(self):
        keep = [self.order.now(self.pairs[0][0])] + [pair[0] for pair in self.pairs[1:]]
        self.mine, self.other = add_pairs(list(zip(keep, self.got)))
        self.order.ran(self.other)

    def cross(self):
        self.got = partner(self.other, "grp", 2)

    def fold(self, step):
        def then(mine, other):
            self.mine, self.other = mine, other
            self.got = along(other, step)

        if step == 0:
            then(*halve(self.place, self.order.now(self.mine), self.got))
            self.order.ran(self.other)
        else:
            self.order.add("split", 0, self.mine, self.got, then)

    def pair(self):
        def then(mine, other):
            self.mine = mine
            self.got = partner(other, "grp", 2)

        self.order.add("pair", 0, self.pairs[0][0], self.got[0], then)

    def swap(self, step):
        def then(mine):
            self.mine = mine
            self.got = along(mine, step % 3)

        self.order.add("sum", (0, 0, 2, 1)[step] if self.mine.shape[0] > 1 else 0, self.mine, self.got, then)

    def open(self, step):
        def then(mine):
            self.mine = mine
            self.got = along(mine, step)

        self.order.add("join", 0, self.mine, self.got, then)

    def finish(self, *widths):
        got = finish(self.place, self.order.now(self.mine), self.got, widths)
        self.order.ran(got[0])
        return got


def local(
    layer_input,
    branch,
    attention_gain,
    factor_weight,
    output_weight,
    feed_gain,
    gate_weight,
    up_weight,
    down_weight,
    cotangent,
):
    rows = layer_input.shape[1]
    parts = lax.axis_size("grp")
    me = lax.axis_index("grp")
    prompt_parts = parts // 2
    follows = me >= prompt_parts
    chosen = branch[0, jnp.maximum(me - prompt_parts, 0)]
    limit = jnp.where(follows, chosen, me * rows)
    npc = (limit + rows - 1) // rows
    position = jnp.where(follows, chosen, me * rows) + jnp.arange(rows, dtype=jnp.int32)
    info = jnp.stack([me, npc, limit]).astype(jnp.int32)
    freqs = 10000.0 ** (-jnp.arange(HALF).astype(f32) / HALF)
    phase = freqs[:, None] * position.astype(f32)[None, :]
    cosine, sine = jnp.cos(phase), jnp.sin(phase)

    x = layer_input[0]
    upstream = cotangent[0]
    shard_rows, cols = factor_weight.shape
    wide = (cols // 128 + 1) * 128
    factor_wide = jnp.concatenate(
        [
            factor_weight,
            attention_gain[:, None],
            feed_gain[:, None],
            jnp.zeros((shard_rows, wide - cols - 2), bf16),
        ],
        axis=1,
    )
    gather = lambda value: lax.all_gather(value, "grp", axis=0, tiled=True)

    if parts != 4 or lax.axis_size("rep") != 8:
        whole = jnp.zeros((4,), jnp.int32)
        w_fac, w_out, w_down = ([gather(v)] for v in (factor_wide, output_weight, down_weight))
        w_gate, w_up = [gather(gate_weight)], [gather(up_weight)]
        fac, kv_own, hid_one, gains = front(whole, x, cosine, sine, w_fac, cols)
        kv = [lax.all_gather(kv_own, "grp", axis=0, tiled=False)]
        mixed, lse = ([got] for got in attend(info, fac, kv, 0, HEADS))
        mid, hid_two, act, slope, lin, act_rows = feed(
            whole, mixed, x, gains[1:2], w_out, w_gate, w_up
        )
        down_pair = products(info, act_rows, upstream, parts)
        dgate, dup = slopes(whole, upstream, w_down, slope, lin)
        up_pair = products(info, hid_two, dup, parts)
        dmid, fgain, dmix, *out_pair = middle_grads(
            whole, info, upstream, gains[1:2], mixed, w_out, w_gate, w_up, dgate, dup, mid, parts
        )
        result, *gate_pair = settle(whole, info, hid_two, dgate, act, mid, w_down, parts)
        dq, *dkv = attend_back(info, fac, kv, dmix, lse, 0, HEADS, ())
        input_grad, *fac_pair = tail(
            whole, info, dq, scatter_all(*dkv), cosine, sine, hid_one, x, gains[0:1], dmid, fgain,
            w_fac, cols, parts,
        )
        pairs = (fac_pair, out_pair, gate_pair, up_pair, down_pair)
        shards = [scatter_all(*pair) for pair in pairs]
        sums = [lax.psum(shard, "rep").astype(f32) for shard in shards]
        fac_grad, out_grad, gate_grad, up_grad, down_grad = sums
        fac_grad, gain_grads = fac_grad[:, :cols], fac_grad[:, cols : cols + 2].T
    else:
        order = Order()
        low = lax.axis_index("rep") % 2
        even = (lax.axis_index("rep") // 2) % 2
        take = lambda v, which: lax.dynamic_slice_in_dim(v, which * (v.shape[0] // 2), v.shape[0] // 2, 0)
        quarter = places([(k, None) for k in range(4)], shard_rows, 0)
        halves = lambda v, rows: places(
            [(0, None), (1, None), (2, v), (2, 1 - v), (3, v), (3, 1 - v)], rows, rows // 2
        )
        by_side, by_line = halves(low, shard_rows), halves(even, shard_rows)
        by_down = halves(low, down_weight.shape[0])
        grp = lambda value, flip: partner(order.free(value), "grp", flip)
        rep = lambda value, flip: partner(order.free(value), "rep", flip)
        fac_x = partner(factor_wide, "grp", 2)
        fac_c = partner(factor_wide, "grp", 1)
        gate_c = partner(gate_weight, "grp", 1)
        up_c = partner(up_weight, "grp", 1)
        out_c = partner(output_weight, "grp", 1)
        gate_half, up_half = take(gate_weight, low), take(up_weight, even)
        out_half, down_half = take(output_weight, low), take(down_weight, low)
        order.phase(fac_x, fac_c, gate_c, up_c, out_c, gate_half, up_half, out_half, down_half)
        fac_xc = grp(fac_x, 1)
        gate_x = grp(gate_half, 2)
        w_fac = [factor_wide, fac_c, fac_x, fac_xc]
        fac, kv_own, hid_one, gains = front(quarter, order.now(x), cosine, sine, w_fac, cols)
        kv_x = partner(kv_own, "grp", 2)
        kv_c = partner(kv_own, "grp", 1)
        kv_xc = partner(kv_x, "grp", 1)
        kv = [kv_own, kv_c, kv_x, kv_xc]

        order.phase(gate_x, kv_x, kv_c, kv_xc)
        up_x = grp(up_half, 2)
        out_x = grp(out_half, 2)
        gate_y = rep(gate_x, 1)
        gate_xc = grp(gate_x, 1)
        down_c = grp(down_weight, 1)
        part = HEADS // 2
        heads = [attend(info, order.now(fac), kv, 0, part)]

        order.phase(up_x, out_x, gate_y, gate_xc, down_c, heads[0][0])
        down_x = grp(down_half, 2)
        up_z = rep(up_x, 2)
        up_xc = grp(up_x, 1)
        out_y = rep(out_x, 1)
        gate_yc = grp(gate_y, 1)
        heads.append(attend(info, order.now(fac), kv, part, part))
        mixed, lse = ([got[i] for got in heads] for i in range(2))

        order.phase(down_x, up_z, up_xc, out_y, gate_yc, heads[1][0])
        up_zc = grp(up_z, 1)
        out_xc = grp(out_x, 1)
        out_yc = grp(out_y, 1)
        w_out = [output_weight, out_c, out_x, out_y, out_xc, out_yc]
        w_gate = [gate_weight, gate_c, gate_x, gate_y, gate_xc, gate_yc]
        w_up = [up_weight, up_c, up_x, up_z, up_xc, up_zc]
        offs_feed = jnp.concatenate([by_side, by_line])

        order.phase(up_zc, out_xc, out_yc)
        odd = me % 2
        place = jnp.stack([lax.axis_index("rep"), 1 + odd, 2 - odd, jnp.full_like(odd, 4)])
        place = place.astype(jnp.int32)
        chunk = functools.partial(Chunk, order, place)
        down_y = rep(down_x, 1)
        down_xc = grp(down_x, 1)
        mid, hid_two, act, slope, lin, act_rows = feed(
            offs_feed, mixed, order.now(x), gains[1:2], w_out, w_gate, w_up
        )

        order.phase(down_y, down_xc, mid)
        down_yc = grp(down_y, 1)
        w_down = [down_weight, down_c, down_x, down_y, down_xc, down_yc]
        down = chunk(products(info, order.now(act_rows), upstream, parts))

        order.phase(down_yc, down.pairs[0][0])
        down.core()
        dgate, dup = slopes(by_down, order.now(upstream), w_down, slope, lin)
        up = chunk(products(info, hid_two, dup, parts))

        order.phase(*down.got, up.pairs[0][0])
        down.add_core()
        down.cross()
        up.core()
        dmid, fgain, dmix, *out_pair = middle_grads(
            offs_feed, info, order.free(upstream), gains[1:2], mixed, w_out, w_gate, w_up,
            dgate, dup, mid, parts,
        )
        out = chunk(out_pair)
        out.core()
        result, *terms = settle(
            by_down, info, after(hid_two, dmix), dgate, act, mid, w_down, parts
        )
        gate = chunk(terms)

        order.phase(down.got, *up.got, *out.got, result)
        both = chunk(*up.pairs, *out.pairs)
        both.got = up.got + out.got
        both.add_core()
        both.cross()
        down.fold(0)
        gate.core()
        part = 3 * HEADS // 4
        state = attend_back(info, fac, kv, order.free(dmix), lse, 0, part, ())

        order.phase(both.got, down.got, *gate.got, state[0])
        gate.add_core()
        gate.cross()
        both.fold(0)
        down.fold(1)
        order.flush()
        dq, *terms = attend_back(info, fac, kv, order.free(dmix), lse, part, HEADS - part, state)

        order.phase(both.got, down.got, dq)
        dkv = chunk(terms)
        dkv.core()
        both.fold(1)
        down.fold(2)
        order.flush()

        order.phase(*dkv.got, both.got, down.got, gate.got)
        dkv.pair()
        both.fold(2)
        order.flush()
        gate.fold(0)

        order.phase(dkv.got, both.got, gate.got)
        sums = []
        order.add("sum", 0, dkv.mine, dkv.got, sums.append)
        both.swap(2)
        gate.fold(1)
        order.flush()
        input_grad, *terms = tail(
            quarter, info, dq, sums[0], cosine, sine, hid_one, x, gains[0:1], dmid, fgain,
            w_fac, cols, parts,
        )

        order.phase(both.got, gate.got, input_grad)
        factor = chunk(terms)
        factor.core()
        both.open(1)
        gate.fold(2)
        down.swap(2)
        order.flush()

        order.phase(*factor.got, both.got, gate.got, down.got)
        factor.pair()
        both.open(0)
        gate.swap(2)
        down.open(1)
        order.flush()

        order.phase(factor.got, both.got, gate.got, down.got)
        factor.fold(0)
        gate.open(1)
        down.open(0)
        order.flush()
        up_grad, out_grad = both.finish(up_weight.shape[1], output_weight.shape[1])

        order.phase(factor.got, gate.got, down.got, up_grad)
        factor.swap(1)
        gate.open(0)
        order.flush()
        (down_grad,) = down.finish(down_weight.shape[1])

        order.phase(factor.got, gate.got, down_grad)
        factor.swap(2)
        order.flush()
        (gate_grad,) = gate.finish(gate_weight.shape[1])

        order.phase(factor.got, gate_grad)
        factor.swap(3)
        order.flush()

        order.phase(factor.got)
        fac_grad, gain_grads = factor.finish(cols)
    return (
        result[None],
        input_grad[None],
        gain_grads[0],
        fac_grad,
        out_grad,
        gain_grads[1],
        gate_grad,
        up_grad,
        down_grad,
    )


def solution(mesh):
    in_specs = (
        P("rep", "grp", None),
        P("rep", None),
        P("grp"),
        P("grp", None),
        P("grp", None),
        P("grp"),
        P("grp", None),
        P("grp", None),
        P("grp", None),
        P("rep", "grp", None),
    )
    out_specs = (
        P("rep", "grp", None),
        P("rep", "grp", None),
        P("grp"),
        P("grp", None),
        P("grp", None),
        P("grp"),
        P("grp", None),
        P("grp", None),
        P("grp", None),
    )
    return jax.shard_map(local, mesh=mesh, in_specs=in_specs, out_specs=out_specs, check_vma=False)
```

```python
import functools

import jax
import jax.numpy as jnp
import numpy as np
from jax import lax
from jax.experimental import pallas as pl
from jax.experimental.pallas import tpu as pltpu
from jax.sharding import PartitionSpec as P

HEADS = 16
HDIM = 64
QRANK = 6
KRANK = 2
HALF = HDIM // 2
QCOLS = QRANK * HEADS + QRANK * HDIM
KVCOLS = 2 * (KRANK * HEADS + KRANK * HDIM)
AQ, BQ = 0, QRANK * HEADS
AK, BK = 0, KRANK * HEADS
AV = BK + KRANK * HDIM
BV = AV + KRANK * HEADS
SCALE = HDIM**-0.5
EXP_SCALE = SCALE * float(np.log2(np.e))
NEG = -1e30
DEPTH = 128
EPS = 1e-05
VMEM_LIMIT = 60 * 2**20

f32 = jnp.float32
bf16 = jnp.bfloat16
NN = (((1,), (0,)), ((), ()))
NT = (((1,), (1,)), ((), ()))
TN = (((0,), (0,)), ((), ()))


def mm(left, right, dims=NN):
    return lax.dot_general(left, right, dims, preferred_element_type=f32)


def vmem():
    return pl.BlockSpec(memory_space=pltpu.VMEM)


def smem():
    return pl.BlockSpec(memory_space=pltpu.SMEM)


def params():
    return pltpu.CompilerParams(vmem_limit_bytes=VMEM_LIMIT)


def cost(flops, nbytes):
    return pl.CostEstimate(flops=int(flops) // 10**5, bytes_accessed=int(nbytes) // 10**5, transcendentals=0)


def weighty(micros):
    return pl.CostEstimate(flops=int(micros * 1.1e9), bytes_accessed=0, transcendentals=0)


def turn(part, cosine, sine):
    first, second = part[:HALF], part[HALF:]
    return first * cosine - second * sine, second * cosine + first * sine


def front_kernel(count, offs, x_ref, cos_ref, sin_ref, *refs):
    pieces, gain_refs = refs[:count], refs[count : 2 * count]
    fac_ref, kv_ref, hid_ref, gains_ref, w, sems = refs[2 * count :]
    w_in = Mover(sems).columns(offs, pieces, w)
    for i, ref in enumerate(gain_refs):
        size = ref.shape[1]
        at = offs[2 * i] if size % 128 == 0 else 0
        gains_ref[0:2, pl.ds(pl.multiple_of(at, 128), size)] = ref[...].astype(f32)
    xf = x_ref[...].astype(f32)
    normed = xf * lax.rsqrt(jnp.mean(xf * xf, axis=-1, keepdims=True) + EPS)
    hidden = (normed * gains_ref[0:1, :]).astype(bf16)
    turned = jnp.transpose(hidden)
    hid_ref[...] = turned
    wait(w_in)
    raw = mm(w[...], turned)
    cosine, sine = cos_ref[...], sin_ref[...]
    fac_ref[...] = raw[:QCOLS].astype(bf16)
    kv_ref[...] = raw[QCOLS:].astype(bf16)
    for ref, first, at in [(fac_ref, 0, BQ + r * HDIM) for r in range(QRANK)] + [
        (kv_ref, QCOLS, BK + r * HDIM) for r in range(KRANK)
    ]:
        one, two = turn(raw[first + at : first + at + HDIM], cosine, sine)
        ref[at : at + HALF, :] = one.astype(bf16)
        ref[at + HALF : at + HDIM, :] = two.astype(bf16)


def front(offs, x, cosine, sine, w_fac, gains):
    rows, width = x.shape
    cols = w_fac[0].shape[0]
    count = len(w_fac)
    return pl.pallas_call(
        functools.partial(front_kernel, count),
        out_shape=[
            like(QCOLS, rows),
            like(cols - QCOLS, rows),
            like(width, rows),
            like(8, width, dtype=f32),
        ],
        in_specs=[smem()] + [vmem()] * 3 + [anywhere()] * count + [vmem()] * count,
        out_specs=[vmem()] * 4,
        scratch_shapes=[scratch(cols, width), pltpu.SemaphoreType.DMA((count,))],
        compiler_params=params(),
        cost_estimate=cost(2 * rows * width * cols, 4 * width * (cols + rows)),
        name="front",
    )(offs, x, cosine, sine, *w_fac, *gains)


def load_factors(fac_ref, kv_refs, facf, kvf, qT, me):
    facf[...] = fac_ref[...].astype(f32)
    if len(kv_refs) == 1:

        def load(j, _):
            kvf[j] = kv_refs[0][j].astype(f32)
            return 0

        lax.fori_loop(0, kvf.shape[0], load, 0)
    else:
        for flip, ref in enumerate(kv_refs):
            kvf[me ^ flip] = ref[...].astype(f32)
    row = lax.broadcasted_iota(jnp.int32, (DEPTH - HDIM, qT.shape[1]), 0)
    qT[HDIM:DEPTH, :] = jnp.where(row == 0, 1.0, 0.0).astype(bf16)


def build_query(facf, qT, h):
    total = facf[pl.ds(AQ + h, 1), :] * facf[BQ : BQ + HDIM, :]
    for r in range(1, QRANK):
        total += facf[pl.ds(AQ + r * HEADS + h, 1), :] * facf[BQ + r * HDIM : BQ + (r + 1) * HDIM, :]
    qT[0:HDIM, :] = (total * (1.0 / QRANK)).astype(bf16)


def build_pair(kvf, j, h, a_at, b_at):
    total = kvf[j, pl.ds(a_at + h, 1), :] * kvf[j, b_at : b_at + HDIM, :]
    for r in range(1, KRANK):
        total += (
            kvf[j, pl.ds(a_at + r * HEADS + h, 1), :]
            * kvf[j, b_at + r * HDIM : b_at + (r + 1) * HDIM, :]
        )
    return (total * (1.0 / KRANK)).astype(bf16)


def build_key(kvf, kT, j, h, limit):
    span = kT.shape[1]
    kT[0:HDIM, :] = build_pair(kvf, j, h, AK, BK)
    if limit is None:
        kT[HDIM:DEPTH, :] = jnp.zeros((DEPTH - HDIM, span), bf16)
    else:
        row = lax.broadcasted_iota(jnp.int32, (DEPTH - HDIM, span), 0)
        key = j * span + lax.broadcasted_iota(jnp.int32, (DEPTH - HDIM, span), 1)
        kT[HDIM:DEPTH, :] = jnp.where((row == 0) & (key >= limit), NEG, 0.0).astype(bf16)


def causal(scores):
    key = lax.broadcasted_iota(jnp.int32, scores.shape, 0)
    query = lax.broadcasted_iota(jnp.int32, scores.shape, 1)
    return jnp.where(key <= query, scores, NEG)


def attend_kernel(first, heads, count, info_ref, fac_ref, *refs):
    kv_refs, (out_ref, lse_ref, facf, kvf, qT, kT, s_ref) = refs[:count], refs[count:]
    me, npc, limit = info_ref[0], info_ref[1], info_ref[2]
    rows = fac_ref.shape[1]
    load_factors(fac_ref, kv_refs, facf, kvf, qT, me)

    def head(step, _):
        h = first + step
        build_query(facf, qT, h)

        def chunk(j, top):
            build_key(kvf, kT, j, h, limit)
            scores = mm(kT[...], qT[...], TN)
            s_ref[j] = scores
            return jnp.maximum(top, jnp.max(scores, axis=0, keepdims=True))

        top = lax.fori_loop(0, npc, chunk, jnp.full((1, rows), NEG, f32))
        build_key(kvf, kT, me, h, None)
        scores = causal(mm(kT[...], qT[...], TN))
        s_ref[npc] = scores
        top = jnp.maximum(top, jnp.max(scores, axis=0, keepdims=True)) * EXP_SCALE

        def weigh(j, mass):
            probs = jnp.exp2(s_ref[j] * EXP_SCALE - top)
            s_ref[j] = probs
            return mass + jnp.sum(probs, axis=0, keepdims=True)

        mass = lax.fori_loop(0, npc + 1, weigh, jnp.zeros((1, rows), f32))
        lse_ref[pl.ds(step, 1), :] = top + jnp.log2(mass)
        share = 1.0 / mass

        def gather(j, total):
            at = jnp.where(j == npc, me, j)
            return total + mm(build_pair(kvf, at, h, AV, BV), (s_ref[j] * share).astype(bf16))

        total = lax.fori_loop(0, npc + 1, gather, jnp.zeros((HDIM, rows), f32))
        out_ref[pl.ds(pl.multiple_of(step * HDIM, HDIM), HDIM), :] = total.astype(bf16)
        return 0

    lax.fori_loop(0, heads, head, 0)


def kv_sizes(kv):
    return kv[0].shape if len(kv) == 1 else (len(kv),) + kv[0].shape


def attend(info, fac, kv, first, heads):
    parts, cols, rows = kv_sizes(kv)
    seen = min(parts, parts // 2 + 1)
    return pl.pallas_call(
        functools.partial(attend_kernel, first, heads, len(kv)),
        out_shape=[
            jax.ShapeDtypeStruct((heads * HDIM, rows), bf16),
            jax.ShapeDtypeStruct((heads, rows), f32),
        ],
        in_specs=[smem(), vmem()] + [vmem()] * len(kv),
        out_specs=[vmem()] * 2,
        scratch_shapes=[
            pltpu.VMEM((QCOLS, rows), f32),
            pltpu.VMEM((parts, cols, rows), f32),
            pltpu.VMEM((DEPTH, rows), bf16),
            pltpu.VMEM((DEPTH, rows), bf16),
            pltpu.VMEM((seen, rows, rows), f32),
        ],
        compiler_params=params(),
        cost_estimate=cost(16 * 2 * heads * 256 * rows * rows * seen, 4 * cols * rows * parts),
        name="attend",
    )(info, fac, *kv)


def attend_back_kernel(
    first, heads, final, count, count_out, blocks, info_ref, fac_ref, grad_ref, *refs
):
    kv_refs, lse_refs, refs = refs[:count], refs[count : count + blocks], refs[count + blocks :]
    if first:
        dq_in, dkv_in, *refs = refs
    dq_ref, *refs = refs
    if final:
        outs, refs = refs[:count_out], refs[count_out:]
        dkvf, *refs = refs
    else:
        dkvf, *refs = refs
    facf, kvf, qT, kTs, p_ref, dp_ref, lse_ref = refs
    for i, ref in enumerate(lse_refs):
        lse_ref[i * ref.shape[0] : (i + 1) * ref.shape[0], :] = ref[...]
    me, npc, limit = info_ref[0], info_ref[1], info_ref[2]
    parts, _, rows = kvf.shape
    load_factors(fac_ref, kv_refs, facf, kvf, qT, me)

    def begin(j, _):
        dkvf[j] = dkv_in[j] if first else jnp.zeros(dkvf.shape[1:], f32)
        return 0

    lax.fori_loop(0, parts, begin, 0)
    dq_ref[...] = dq_in[...] if first else jnp.zeros(dq_ref.shape, f32)

    def head(step, _):
        h = first + step
        build_query(facf, qT, h)
        grad = grad_ref[pl.ds(pl.multiple_of(h * HDIM, HDIM), HDIM), :]
        lse = lse_ref[pl.ds(h, 1), :]

        def probe(slot, at, scores, delta):
            probs = jnp.exp2(scores * EXP_SCALE - lse)
            p_ref[slot] = probs
            prob_grad = mm(build_pair(kvf, at, h, AV, BV), grad, TN)
            dp_ref[slot] = prob_grad
            return delta + jnp.sum(probs * prob_grad, axis=0, keepdims=True)

        def chunk(j, delta):
            build_key(kvf, kTs.at[j], j, h, limit)
            return probe(j, j, mm(kTs[j], qT[...], TN), delta)

        delta = lax.fori_loop(0, npc, chunk, jnp.zeros((1, rows), f32))
        build_key(kvf, kTs.at[npc], me, h, None)
        delta = probe(npc, me, causal(mm(kTs[npc], qT[...], TN)), delta)

        def pull(j, total):
            at = jnp.where(j == npc, me, j)
            probs = p_ref[j]
            score_grad = (probs * (dp_ref[j] - delta)).astype(bf16)
            key_grad = mm(qT[0:HDIM, :], score_grad, NT) * (SCALE / KRANK)
            value_grad = mm(grad, probs.astype(bf16), NT) * (1.0 / KRANK)
            for a_at, b_at, got in ((AK, BK, key_grad), (AV, BV, value_grad)):
                for r in range(KRANK):
                    a_row = pl.ds(a_at + r * HEADS + h, 1)
                    b_rows = slice(b_at + r * HDIM, b_at + (r + 1) * HDIM)
                    dkvf[at, a_row, :] = jnp.sum(got * kvf[at, b_rows, :], axis=0, keepdims=True)
                    dkvf[at, b_rows, :] += got * kvf[at, a_row, :]
            return total + mm(kTs[j, 0:HDIM, :], score_grad)

        query_grad = lax.fori_loop(0, npc + 1, pull, jnp.zeros((HDIM, rows), f32)) * (SCALE / QRANK)
        for r in range(QRANK):
            a_row = pl.ds(AQ + r * HEADS + h, 1)
            b_rows = slice(BQ + r * HDIM, BQ + (r + 1) * HDIM)
            dq_ref[a_row, :] = jnp.sum(query_grad * facf[b_rows, :], axis=0, keepdims=True)
            dq_ref[b_rows, :] += query_grad * facf[a_row, :]
        return 0

    lax.fori_loop(0, heads, head, 0)
    if final:
        for flip in range(parts):
            outs[flip % 2][flip // 2] = dkvf[me ^ flip].astype(bf16)


def attend_back(info, fac, kv, grad, lse, first, heads, so_far, declared=None):
    parts, cols, rows = kv_sizes(kv)
    seen = min(parts, parts // 2 + 1)
    final = first + heads == HEADS
    gathered = [like(parts // 2, cols, rows)] * 2 if final else [like(parts, cols, rows, dtype=f32)]
    return pl.pallas_call(
        functools.partial(
            attend_back_kernel, first, heads, final, len(kv), len(gathered), len(lse)
        ),
        out_shape=[like(QCOLS, rows, dtype=f32)] + gathered,
        in_specs=[smem()] + [vmem()] * (2 + len(kv) + len(lse) + len(so_far)),
        out_specs=[vmem()] * (1 + len(gathered)),
        scratch_shapes=([pltpu.VMEM((parts, cols, rows), f32)] if final else [])
        + [
            pltpu.VMEM((QCOLS, rows), f32),
            pltpu.VMEM((parts, cols, rows), f32),
            pltpu.VMEM((DEPTH, rows), bf16),
            pltpu.VMEM((seen, DEPTH, rows), bf16),
            pltpu.VMEM((seen, rows, rows), f32),
            pltpu.VMEM((seen, rows, rows), f32),
            pltpu.VMEM((HEADS, rows), f32),
        ],
        compiler_params=params(),
        cost_estimate=declared or cost(heads * rows * rows, 8 * cols * rows * parts),
        name="attend_back",
    )(info, fac, grad, *kv, *lse, *so_far)


class Mover:
    def __init__(self, sems):
        self.sems = sems
        self.used = 0

    def start(self, src, dst):
        copy = pltpu.make_async_copy(src, dst, self.sems.at[self.used])
        self.used += 1
        copy.start()
        return copy

    def pieces(self, offsets, refs, dst, first=0):
        copies = []
        for i, piece in enumerate(refs):
            rows, cols = piece.shape
            at = pl.ds(pl.multiple_of(offsets[first + 2 * i], 16), rows)
            if cols == dst.shape[1]:
                where = dst.at[at]
            else:
                where = dst.at[at, pl.ds(pl.multiple_of(offsets[first + 2 * i + 1], 128), cols)]
            copies.append(self.start(piece, where))
        return copies


    def columns(self, offsets, refs, dst):
        copies = []
        for i, piece in enumerate(refs):
            cols = piece.shape[1]
            if cols == dst.shape[1]:
                copies.append(self.start(piece, dst))
            else:
                at = pl.ds(pl.multiple_of(offsets[2 * i], 128), cols)
                copies.append(self.start(piece, dst.at[:, at]))
        return copies


def wait(copies):
    for copy in copies:
        copy.wait()


def anywhere():
    return pl.BlockSpec(memory_space=pl.ANY)


def like(*shape, dtype=bf16):
    return jax.ShapeDtypeStruct(shape, dtype)


def scratch(*shape, dtype=bf16):
    return pltpu.VMEM(shape, dtype)


TILE = 256


def norm_back(grad_hidden, normed, scale, gain):
    grad_normed = grad_hidden * gain
    gain_grad = jnp.sum(grad_hidden * normed, axis=0, keepdims=True)
    mean = jnp.mean(grad_normed * normed, axis=-1, keepdims=True)
    return gain_grad, scale * (grad_normed - normed * mean)


def shard_products(me, left, right, pair, mover, pair_out):
    copies = []
    count, rows, cols = pair[0].shape
    step = rows if rows <= 352 else rows // 2
    width = cols // 2 if cols % 256 == 0 and cols > 2048 else cols
    for odd in (1, 0):
        for j in range(count):
            row = (me ^ (2 * j + odd)) * rows
            for low in range(0, rows, step):
                lhs = left[pl.ds(pl.multiple_of(row + low, 16), step), :]
                for at in range(0, cols, width):
                    pair[odd][j, low : low + step, at : at + width] = mm(
                        lhs, right[:, at : at + width]
                    ).astype(bf16)
            copies.append(mover.start(pair[odd].at[j], pair_out[odd].at[j]))
    return copies


def feed_kernel(count, blocks, offs, x_ref, gain_ref, *refs):
    mix_refs, refs = refs[:blocks], refs[blocks:]
    out_pieces, gate_pieces, lift_pieces = (refs[i * count : (i + 1) * count] for i in range(3))
    refs = refs[3 * count :]
    (mid_o, hid_o, act_o, slope_o, lin_o, actT_o) = refs[:6]
    (wo, wg, wu, mid, hid, hidT, act, slope, lin, actT, sems) = refs[6:]
    mover = Mover(sems)
    wo_in = mover.pieces(offs, out_pieces, wo)
    wg_in = mover.pieces(offs, gate_pieces, wg)
    wu_in = mover.pieces(offs, lift_pieces, wu, 2 * count)
    mix = jnp.concatenate([jnp.transpose(ref[...]) for ref in mix_refs], axis=1)
    wait(wo_in)
    middle = x_ref[...].astype(f32) + mm(mix, wo[...])
    mid[...] = middle
    scale = lax.rsqrt(jnp.mean(middle * middle, axis=-1, keepdims=True) + EPS)
    hidden = (middle * scale * gain_ref[...]).astype(bf16)
    hid[...] = hidden
    hidT[...] = jnp.transpose(hidden)
    done = [mover.start(mid, mid_o), mover.start(hidT, hid_o)]
    wait(wg_in)
    wait(wu_in)

    def tile(j, _):
        cols = pl.ds(pl.multiple_of(j * TILE, TILE), TILE)
        gate = mm(hid[...], wg[:, cols])
        up = mm(hid[...], wu[:, cols])
        sig = jax.nn.sigmoid(gate)
        line = gate * sig
        active = (line * up).astype(bf16)
        act[:, cols] = active
        lin[:, cols] = line.astype(bf16)
        slope[:, cols] = (up * sig * (1.0 + gate * (1.0 - sig))).astype(bf16)
        actT[cols, :] = jnp.transpose(active)
        return 0

    lax.fori_loop(0, wg.shape[1] // TILE, tile, 0, unroll=True)
    done += [mover.start(act, act_o), mover.start(lin, lin_o), mover.start(slope, slope_o)]
    done.append(mover.start(actT, actT_o))
    wait(done)


def feed(offs, mix, x, gain, w_out, w_gate, w_up):
    rows, width = x.shape
    inner = w_gate[0].shape[1]
    count = len(w_gate)
    return pl.pallas_call(
        functools.partial(feed_kernel, count, len(mix)),
        out_shape=[
            like(rows, width, dtype=f32),
            like(width, rows),
            like(rows, inner),
            like(rows, inner),
            like(rows, inner),
        ]
        + [like(inner, rows)],
        in_specs=[smem()] + [vmem()] * (2 + len(mix)) + [anywhere()] * (3 * count),
        out_specs=[anywhere()] * 6,
        scratch_shapes=[
            scratch(width, width),
            scratch(width, inner),
            scratch(width, inner),
            scratch(rows, width, dtype=f32),
            scratch(rows, width),
            scratch(width, rows),
            scratch(rows, inner),
            scratch(rows, inner),
            scratch(rows, inner),
            scratch(inner, rows),
            pltpu.SemaphoreType.DMA((3 * count + 6,)),
        ],
        compiler_params=params(),
        cost_estimate=cost(2 * rows * width * (width + 3 * inner), 2 * inner * (3 * width + 3 * rows)),
        name="feed",
    )(offs, x, gain, *mix, *w_out, *w_gate, *w_up)


def slopes_kernel(count, offs, slope_ref, lin_ref, c_ref, *refs):
    pieces, (dg_o, du_o, wd, dg, du, sems) = refs[:count], refs[count:]
    mover = Mover(sems)
    wait(mover.pieces(offs, pieces, wd))

    def tile(j, _):
        cols = pl.ds(pl.multiple_of(j * TILE, 128), TILE)
        grad = mm(c_ref[...], wd[cols, :], NT)
        dg[:, cols] = (grad * slope_ref[:, cols].astype(f32)).astype(bf16)
        du[:, cols] = (grad * lin_ref[:, cols].astype(f32)).astype(bf16)
        return 0

    lax.fori_loop(0, wd.shape[0] // TILE, tile, 0, unroll=True)
    wait([mover.start(dg, dg_o), mover.start(du, du_o)])


def slopes(offs, upstream, w_down, slope, lin):
    rows, width = upstream.shape
    inner = slope.shape[1]
    count = len(w_down)
    return pl.pallas_call(
        functools.partial(slopes_kernel, count),
        out_shape=[like(rows, inner)] * 2,
        in_specs=[smem()] + [vmem()] * 3 + [anywhere()] * count,
        out_specs=[anywhere()] * 2,
        scratch_shapes=[
            scratch(inner, width),
            scratch(rows, inner),
            scratch(rows, inner),
            pltpu.SemaphoreType.DMA((count + 2,)),
        ],
        compiler_params=params(),
        cost_estimate=cost(2 * rows * width * inner, 2 * inner * (width + 4 * rows)),
        name="slopes",
    )(offs, slope, lin, upstream, *w_down)


def products_kernel(who, left, right, *refs):
    outs, pair, sems = refs[0:2], refs[2:4], refs[4]
    wait(shard_products(who[0], left, right, pair, Mover(sems), outs))


def products(who, left, right, parts):
    width, rows = left.shape
    inner = right.shape[1]
    pair = (parts // 2, width // parts, inner)
    return pl.pallas_call(
        products_kernel,
        out_shape=[like(*pair)] * 2,
        in_specs=[smem()] + [vmem()] * 2,
        out_specs=[anywhere()] * 2,
        scratch_shapes=[scratch(*pair)] * 2 + [pltpu.SemaphoreType.DMA((parts,))],
        compiler_params=params(),
        cost_estimate=cost(2 * rows * width * inner, 2 * inner * (width + rows)),
        name="products",
    )(who, left, right)


def middle_kernel(count, blocks, offs, who, c_ref, gain_ref, *refs):
    out_pieces, gate_pieces, lift_pieces = (refs[i * count : (i + 1) * count] for i in range(3))
    mix_refs, refs = refs[3 * count : 3 * count + blocks], refs[3 * count + blocks :]
    dg_i, du_i, mid_i, dmid_o, fgain, dmix, *refs = refs
    outs, (wg, wu, wo, dg, du, mid, dhid, branch, mix), pair, sems = refs[:2], refs[2:11], refs[11:13], refs[13]
    mover = Mover(sems)
    in_dg = [mover.start(dg_i, dg)]
    in_wg = mover.pieces(offs, gate_pieces, wg)
    in_du = [mover.start(du_i, du)]
    in_wu = mover.pieces(offs, lift_pieces, wu, 2 * count)
    in_mid = [mover.start(mid_i, mid)]
    in_wo = mover.pieces(offs, out_pieces, wo)
    width = wg.shape[0]

    def back(which, j):
        at = pl.ds(pl.multiple_of(j * TILE, TILE), TILE)
        if which == 0:
            dhid[:, at] = mm(dg[...], wg[at, :], NT)
        else:
            dhid[:, at] += mm(du[...], wu[at, :], NT)
        return 0

    wait(in_dg + in_wg)
    lax.fori_loop(0, width // TILE, lambda j, _: back(0, j), 0, unroll=True)
    wait(in_du + in_wu)
    lax.fori_loop(0, width // TILE, lambda j, _: back(1, j), 0, unroll=True)
    wait(in_mid + in_wo)
    middle = mid[...]
    scale = lax.rsqrt(jnp.mean(middle * middle, axis=-1, keepdims=True) + EPS)
    gain_grad, part = norm_back(dhid[...], middle * scale, scale, gain_ref[...])
    fgain[...] = jnp.broadcast_to(gain_grad, fgain.shape)
    total = c_ref[...].astype(f32) + part
    dhid[...] = total
    branch[...] = total.astype(bf16)
    done = [mover.start(dhid, dmid_o)]
    for i, ref in enumerate(mix_refs):
        size = ref.shape[0]
        mix[i * size : (i + 1) * size, :] = ref[...]
    done += shard_products(who[0], mix, branch, pair, mover, outs)
    dmix[...] = mm(wo[...], branch[...], NT).astype(bf16)
    wait(done)


def middle_grads(offs, who, upstream, gain, mix, w_out, w_gate, w_up, dg, du, mid, parts):
    rows, width = upstream.shape
    pair = (parts // 2, width // parts, width)
    inner = dg.shape[1]
    count = len(w_gate)
    return pl.pallas_call(
        functools.partial(middle_kernel, count, len(mix)),
        out_shape=[
            like(rows, width, dtype=f32),
            like(8, width, dtype=f32),
            like(width, rows),
            like(*pair),
            like(*pair),
        ],
        in_specs=[smem()] * 2
        + [vmem()] * 2
        + [anywhere()] * (3 * count)
        + [vmem()] * len(mix)
        + [anywhere()] * 3,
        out_specs=[anywhere()] + [vmem()] * 2 + [anywhere()] * 2,
        scratch_shapes=[
            scratch(width, inner),
            scratch(width, inner),
            scratch(width, width),
            scratch(rows, inner),
            scratch(rows, inner),
            scratch(rows, width, dtype=f32),
            scratch(rows, width, dtype=f32),
            scratch(rows, width),
            scratch(width, rows),
            scratch(*pair),
            scratch(*pair),
            pltpu.SemaphoreType.DMA((3 * count + 4 + parts,)),
        ],
        compiler_params=params(),
        cost_estimate=cost(2 * rows * width * (2 * inner + width), 4 * inner * (width + rows)),
        name="middle_grads",
    )(offs, who, upstream, gain, *w_out, *w_gate, *w_up, *mix, dg, du, mid)


def output_kernel(count, offs, act_ref, mid_ref, *refs):
    pieces, (res, wd, sems) = refs[:count], refs[count:]
    wait(Mover(sems).pieces(offs, pieces, wd))

    def forth(j, _):
        at = pl.ds(pl.multiple_of(j * TILE, TILE), TILE)
        res[:, at] = (mid_ref[:, at] + mm(act_ref[...], wd[:, at])).astype(bf16)
        return 0

    lax.fori_loop(0, wd.shape[1] // TILE, forth, 0, unroll=True)


def output(offs, act, mid, w_down):
    rows, width = mid.shape
    count = len(w_down)
    inner = act.shape[1]
    return pl.pallas_call(
        functools.partial(output_kernel, count),
        out_shape=like(rows, width),
        in_specs=[smem()] + [vmem()] * 2 + [anywhere()] * count,
        out_specs=vmem(),
        scratch_shapes=[scratch(inner, width), pltpu.SemaphoreType.DMA((count,))],
        compiler_params=params(),
        cost_estimate=cost(2 * rows * width * inner, 2 * inner * (width + rows)),
        name="output",
    )(offs, act, mid, *w_down)


def tail_kernel(count, cols, offs, who, dq_ref, own_ref, cos_ref, sin_ref, hid_ref, x_ref, gain_ref, dmid_ref, fgain_ref, *refs):
    pieces = refs[:count]
    grad_ref, *outs = refs[count:]
    *outs, w, raw, gain_cols, sems = outs
    mover = Mover(sems)
    w_in = mover.columns(offs, pieces, w)
    cosine, sine = cos_ref[...], -sin_ref[...]
    raw[0:QCOLS, :] = dq_ref[...].astype(bf16)
    raw[QCOLS:cols, :] = own_ref[...]
    raw[cols:, :] = jnp.zeros((raw.shape[0] - cols, raw.shape[1]), bf16)
    for r in range(QRANK):
        at = BQ + r * HDIM
        one, two = turn(dq_ref[at : at + HDIM, :], cosine, sine)
        raw[at : at + HALF, :] = one.astype(bf16)
        raw[at + HALF : at + HDIM, :] = two.astype(bf16)
    for r in range(KRANK):
        at = BK + r * HDIM
        one, two = turn(own_ref[at : at + HDIM, :].astype(f32), cosine, sine)
        raw[QCOLS + at : QCOLS + at + HALF, :] = one.astype(bf16)
        raw[QCOLS + at + HALF : QCOLS + at + HDIM, :] = two.astype(bf16)
    draw = jnp.transpose(raw[...])
    wait(w_in)
    xf = x_ref[...].astype(f32)
    scale = lax.rsqrt(jnp.mean(xf * xf, axis=-1, keepdims=True) + EPS)
    dhid = mm(draw[:, 0:cols], w[...])
    gain_grad, part = norm_back(dhid, xf * scale, scale, gain_ref[...])
    grad_ref[...] = dmid_ref[...] + part
    line = lax.broadcasted_iota(jnp.int32, (128, gain_grad.shape[1]), 0)
    both = jnp.where(line == 0, gain_grad, jnp.where(line == 1, fgain_ref[0:1, :], 0.0))
    gain_cols[...] = jnp.transpose(both)
    count_out, wide, rows = outs[0].shape
    for flip in range(2 * count_out):
        at = pl.ds(pl.multiple_of((who[0] ^ flip) * rows, 16), rows)
        out = outs[flip % 2]
        out[flip // 2, 0:cols, :] = mm(raw[0:cols, :], hid_ref[at, :], NT).astype(bf16)
        out[flip // 2, cols:wide, :] = jnp.transpose(gain_cols[at, :])[0 : wide - cols].astype(bf16)


def tail(offs, who, dq, own, cosine, sine, hidT, x, gain, dmid, fgain, w_fac, cols, parts):
    rows, width = x.shape
    wide = (cols // 128 + 1) * 128
    count = len(w_fac)
    shard = (parts // 2, wide, width // parts)
    return pl.pallas_call(
        functools.partial(tail_kernel, count, cols),
        out_shape=[like(rows, width, dtype=f32)] + [like(*shard)] * 2,
        in_specs=[smem()] * 2 + [vmem()] * 9 + [anywhere()] * count,
        out_specs=[vmem()] * 3,
        scratch_shapes=[
            scratch(cols, width),
            scratch(wide, rows),
            scratch(width, 128, dtype=f32),
            pltpu.SemaphoreType.DMA((count,)),
        ],
        compiler_params=params(),
        cost_estimate=cost(4 * rows * width * cols, 4 * width * (cols + 3 * rows)),
        name="tail",
    )(offs, who, dq, own, cosine, sine, hidT, x, gain, dmid, fgain, *w_fac)


def partner(values, axis, flip):
    size = lax.axis_size(axis)
    return lax.ppermute(values, axis, [(i, i ^ flip) for i in range(size)])


def after(value, *earlier):
    if not earlier:
        return value
    return lax.optimization_barrier((value, *earlier))[0]


def places(pieces, rows, half):
    me = lax.axis_index("grp")
    at = []
    for flip, which in pieces:
        row = (me ^ flip) * rows
        at += [row if which is None else row + which * half, 0]
    return jnp.stack([jnp.asarray(v, jnp.int32) for v in at])


def total(*terms):
    got = terms[0].astype(f32)
    for term in terms[1:]:
        got = got + term.astype(f32)
    return got.astype(bf16)


def add_pairs_kernel(*refs):
    mine, other = refs[-2:]
    at = 0
    for keep, got in zip(refs[:-2:2], refs[1:-2:2]):
        cols = slice(at, at + keep.shape[2])
        mine[:, cols] = total(keep[0], got[0])
        other[:, cols] = total(keep[1], got[1])
        at += keep.shape[2]


def add_pairs(groups):
    rows = groups[0][0].shape[1]
    wide = sum(keep.shape[2] for keep, _ in groups)
    steps = next(n for n in (4, 2, 1) if n == 1 or (rows % (16 * n) == 0 and rows * wide > 2**19))
    out = pl.BlockSpec((rows // steps, wide), lambda i: (i, 0))
    terms = [term for group in groups for term in group]
    return pl.pallas_call(
        add_pairs_kernel,
        grid=(steps,),
        out_shape=[like(rows, wide)] * 2,
        in_specs=[pl.BlockSpec((2, rows // steps, v.shape[2]), lambda i: (0, i, 0)) for v in terms],
        out_specs=[out] * 2,
        compiler_params=params(),
        cost_estimate=cost(1, 1),
        name="add_pairs",
    )(*terms)


def halve_kernel(place, keep_one, keep_two, send_one, send_two, keep, send):
    keep[...] = total(keep_one[...], keep_two[...])
    send[...] = total(send_one[...], send_two[...])


def halve(place, one, two):
    rows, cols = one.shape[0] // 8, one.shape[1]
    one, two = (v.reshape(8, rows, cols) for v in (one, two))

    def piece(flip):
        def index(i, place):
            at = place[0] ^ ((i >> 1) * place[2]) ^ ((i & 1) * place[3])
            return (at ^ place[1] if flip else at, 0, 0)

        return pl.BlockSpec((1, rows, cols), index)

    out = pl.BlockSpec((1, rows, cols), lambda i, place: (i, 0, 0))
    return pl.pallas_call(
        halve_kernel,
        grid_spec=pltpu.PrefetchScalarGridSpec(
            num_scalar_prefetch=1,
            grid=(4,),
            in_specs=[piece(False)] * 2 + [piece(True)] * 2,
            out_specs=[out] * 2,
        ),
        out_shape=[like(4, rows, cols)] * 2,
        compiler_params=params(),
        cost_estimate=cost(1, 1),
        name="halve",
    )(place, one, two, one, two)


def batch_kernel(tasks, *refs):
    ins, outs = refs[: 2 * len(tasks)], list(refs[2 * len(tasks) :])
    for i, (kind, flip) in enumerate(tasks):
        one, two = ins[2 * i : 2 * i + 2]
        out = outs.pop(0)
        if kind == "split":
            half = out.shape[0]
            out[...] = total(one[:half], two[:half])
            outs.pop(0)[...] = total(one[half:], two[half:])
        elif kind == "pair":
            out[...] = total(one[0], two[0])
            outs.pop(0)[...] = total(one[1], two[1])
        elif kind == "join":
            half = one.shape[0]
            out[:half] = one[...]
            out[half:] = two[...]
        elif flip:
            for k in range(out.shape[0]):
                out[k] = total(one[k], two[k ^ flip])
        else:
            out[...] = total(one[...], two[...])


def batch(tasks):
    shapes, counts = [], []
    for kind, _, one, _ in tasks:
        first, rest = one.shape[0], one.shape[1:]
        got = {
            "split": [(first // 2,) + rest] * 2,
            "pair": [rest] * 2,
            "join": [(2 * first,) + rest],
            "sum": [one.shape],
        }[kind]
        shapes += got
        counts.append(len(got))
    outs = pl.pallas_call(
        functools.partial(batch_kernel, [task[:2] for task in tasks]),
        out_shape=[like(*shape) for shape in shapes],
        in_specs=[vmem()] * (2 * len(tasks)),
        out_specs=[vmem()] * len(shapes),
        compiler_params=params(),
        cost_estimate=cost(1, 1),
        name="batch",
    )(*[value for task in tasks for value in task[2:]])
    groups = []
    for count in counts:
        groups.append(outs[:count])
        outs = outs[count:]
    return groups


def finish_kernel(widths, place, near, far, *outs):
    _, rows, wide = near.shape
    for side, value in ((0, near), (1, far)):
        for k in range(4):
            at = place[0] ^ (side * place[1]) ^ ((k >> 1) * place[2]) ^ ((k & 1) * place[3])
            row = pl.ds(pl.multiple_of(at * rows, 8), rows)
            col = 0
            for out, cols in zip(outs, widths):
                out[row, :] = value[k, :, col : col + cols].astype(f32)
                col += cols


def finish(place, near, far, widths):
    rows = near.shape[1]
    return pl.pallas_call(
        functools.partial(finish_kernel, widths),
        out_shape=[like(8 * rows, cols, dtype=f32) for cols in widths],
        in_specs=[smem()] + [vmem()] * 2,
        out_specs=[vmem()] * len(widths),
        compiler_params=params(),
        cost_estimate=cost(1, 1),
        name="finish",
    )(place, near, far)


def scatter_all(keep, send):
    me = lax.axis_index("grp")
    both = jnp.stack([keep, send], axis=1)
    both = both.reshape((-1,) + both.shape[2:])
    both = jnp.take(both, jnp.arange(both.shape[0]) ^ me, axis=0)
    return lax.psum_scatter(both, "grp", scatter_dimension=0, tiled=False)


class Order:
    def __init__(self):
        self.last = None
        self.before = ()
        self.tasks = []

    def add(self, kind, flip, one, two, then):
        self.tasks.append(((kind, flip, self.free(one), two), then))

    def flush(self):
        groups = batch([task for task, _ in self.tasks])
        for (_, then), group in zip(self.tasks, groups):
            then(*group)
        self.tasks = []

    def __call__(self, value, *earlier):
        earlier = earlier if self.last is None else earlier + (self.last,)
        return after(value, *earlier) if earlier else value

    def phase(self, *results):
        self.before = results
        self.last = None

    def now(self, value, *earlier):
        last = () if self.last is None else (self.last,)
        return after(value, *self.before, *earlier, *last)

    def free(self, value):
        return after(value, *self.before)

    def ran(self, value):
        self.last = value
        return value


BITS = ((1, 2, 4), (2, 1, 4))


def along(values, step):
    reps, parts = lax.axis_size("rep"), lax.axis_size("grp")
    pairs = [
        (r * parts + g, (r ^ BITS[g % 2][step]) * parts + g)
        for r in range(reps)
        for g in range(parts)
    ]
    return lax.ppermute(values, ("rep", "grp"), pairs)


class Chunk:
    def __init__(self, order, place, *pairs):
        self.order, self.place, self.pairs = order, place, pairs

    def core(self):
        send = [after(pair[1], *self.order.before) for pair in self.pairs]
        self.got = [partner(value, "grp", 1) for value in send]

    def add_core(self):
        keep = [self.order.now(self.pairs[0][0])] + [pair[0] for pair in self.pairs[1:]]
        self.mine, self.other = add_pairs(list(zip(keep, self.got)))
        self.order.ran(self.other)

    def cross(self):
        self.got = partner(self.order.free(self.other), "grp", 2)

    def go(self, step):
        self.got = along(self.order.free(self.other), step)

    def fold(self, step, start=True):
        def then(mine, other):
            self.mine, self.other = mine, other
            if start:
                self.got = along(other, step)

        if step == 0:
            then(*halve(self.place, self.order.now(self.mine), self.got))
            self.order.ran(self.other)
        else:
            self.order.add("split", 0, self.mine, self.got, then)

    def pair(self):
        def then(mine, other):
            self.mine = mine
            self.got = partner(other, "grp", 2)

        self.order.add("pair", 0, self.pairs[0][0], self.got[0], then)

    def swap(self, step, flip=0):
        def then(mine):
            self.mine = mine
            self.got = along(mine, step)

        self.order.add("sum", flip, self.mine, self.got, then)

    def open(self, step):
        def then(mine):
            self.mine = mine
            self.got = along(mine, step)

        self.order.add("join", 0, self.mine, self.got, then)

    def finish(self, *widths):
        got = finish(self.place, self.order.now(self.mine), self.got, widths)
        self.order.ran(got[0])
        return got


def local(
    layer_input,
    branch,
    attention_gain,
    factor_weight,
    output_weight,
    feed_gain,
    gate_weight,
    up_weight,
    down_weight,
    cotangent,
):
    rows = layer_input.shape[1]
    parts = lax.axis_size("grp")
    me = lax.axis_index("grp")
    prompt_parts = parts // 2
    follows = me >= prompt_parts
    chosen = branch[0, jnp.maximum(me - prompt_parts, 0)]
    limit = jnp.where(follows, chosen, me * rows)
    npc = (limit + rows - 1) // rows
    position = jnp.where(follows, chosen, me * rows) + jnp.arange(rows, dtype=jnp.int32)
    info = jnp.stack([me, npc, limit]).astype(jnp.int32)
    freqs = 10000.0 ** (-jnp.arange(HALF).astype(f32) / HALF)
    phase = freqs[:, None] * position.astype(f32)[None, :]
    cosine, sine = jnp.cos(phase), jnp.sin(phase)

    x = layer_input[0]
    upstream = cotangent[0]
    shard_rows, cols = factor_weight.shape
    own_gains = jnp.stack([attention_gain, feed_gain])
    factor_turned = factor_weight.T
    gather = lambda value: lax.all_gather(value, "grp", axis=0, tiled=True)

    if parts != 4 or lax.axis_size("rep") != 8:
        whole = jnp.zeros((4,), jnp.int32)
        w_out, w_down = [gather(output_weight)], [gather(down_weight)]
        w_fac = [lax.all_gather(factor_turned, "grp", axis=1, tiled=True)]
        w_gate, w_up = [gather(gate_weight)], [gather(up_weight)]
        all_gains = lax.all_gather(own_gains, "grp", axis=1, tiled=True)
        fac, kv_own, hid_one, gains = front(whole, x, cosine, sine, w_fac, [all_gains])
        kv = [lax.all_gather(kv_own, "grp", axis=0, tiled=False)]
        mixed, lse = ([got] for got in attend(info, fac, kv, 0, HEADS))
        mid, hid_two, act, slope, lin, act_rows = feed(
            whole, mixed, x, gains[1:2], w_out, w_gate, w_up
        )
        down_pair = products(info, act_rows, upstream, parts)
        dgate, dup = slopes(whole, upstream, w_down, slope, lin)
        up_pair = products(info, hid_two, dup, parts)
        dmid, fgain, dmix, *out_pair = middle_grads(
            whole, info, upstream, gains[1:2], mixed, w_out, w_gate, w_up, dgate, dup, mid, parts
        )
        gate_pair = products(info, hid_two, dgate, parts)
        result = output(whole, act, mid, w_down)
        dq, *dkv = attend_back(info, fac, kv, dmix, lse, 0, HEADS, ())
        input_grad, *fac_pair = tail(
            whole, info, dq, scatter_all(*dkv), cosine, sine, hid_one, x, gains[0:1], dmid, fgain,
            w_fac, cols, parts,
        )
        pairs = (fac_pair, out_pair, gate_pair, up_pair, down_pair)
        shards = [scatter_all(*pair) for pair in pairs]
        sums = [lax.psum(shard, "rep").astype(f32) for shard in shards]
        fac_grad, out_grad, gate_grad, up_grad, down_grad = sums
    else:
        order = Order()
        low = lax.axis_index("rep") % 2
        even = (lax.axis_index("rep") // 2) % 2
        take = lambda v, which: lax.dynamic_slice_in_dim(v, which * (v.shape[0] // 2), v.shape[0] // 2, 0)
        quarter = places([(k, None) for k in range(4)], shard_rows, 0)
        halves = lambda v, rows: places(
            [(0, None), (1, None), (2, v), (2, 1 - v), (3, v), (3, 1 - v)], rows, rows // 2
        )
        by_side, by_line = halves(low, shard_rows), halves(even, shard_rows)
        by_down = halves(low, down_weight.shape[0])
        grp = lambda value, flip: partner(order.free(value), "grp", flip)
        rep = lambda value, flip: partner(order.free(value), "rep", flip)
        fac_x = partner(factor_turned, "grp", 2)
        fac_c = partner(factor_turned, "grp", 1)
        gains_x = partner(own_gains, "grp", 2)
        gains_c = partner(own_gains, "grp", 1)
        gate_c = partner(gate_weight, "grp", 1)
        gate_half, up_half = take(gate_weight, low), take(up_weight, even)
        out_half, down_half = take(output_weight, low), take(down_weight, low)
        order.phase(
            fac_x, fac_c, gains_x, gains_c, gate_c, gate_half, up_half, out_half, down_half
        )
        fac_xc = grp(fac_x, 1)
        gains_xc = grp(gains_x, 1)
        gate_x = grp(gate_half, 2)
        up_c = grp(up_weight, 1)
        out_c = grp(output_weight, 1)
        w_fac = [factor_turned, fac_c, fac_x, fac_xc]
        all_gains = [own_gains, gains_c, gains_x, gains_xc]
        fac, kv_own, hid_one, gains = front(
            quarter, order.now(x), cosine, sine, w_fac, all_gains
        )
        kv_x = partner(kv_own, "grp", 2)
        kv_c = partner(kv_own, "grp", 1)
        kv_xc = partner(kv_x, "grp", 1)
        kv = [kv_own, kv_c, kv_x, kv_xc]

        order.phase(gate_x, kv_x, kv_c, kv_xc, up_c, out_c)
        up_x = grp(up_half, 2)
        out_x = grp(out_half, 2)
        gate_y = rep(gate_x, 1)
        gate_xc = grp(gate_x, 1)
        down_c = grp(down_weight, 1)
        part = HEADS // 2
        heads = [attend(info, order.now(fac), kv, 0, part)]

        order.phase(up_x, out_x, gate_y, gate_xc, down_c, heads[0][0])
        down_x = grp(down_half, 2)
        up_z = rep(up_x, 2)
        up_xc = grp(up_x, 1)
        out_y = rep(out_x, 1)
        gate_yc = grp(gate_y, 1)
        heads.append(attend(info, order.now(fac), kv, part, part))
        mixed, lse = ([got[i] for got in heads] for i in range(2))

        order.phase(down_x, up_z, up_xc, out_y, gate_yc, heads[1][0])
        up_zc = grp(up_z, 1)
        out_xc = grp(out_x, 1)
        out_yc = grp(out_y, 1)
        w_out = [output_weight, out_c, out_x, out_y, out_xc, out_yc]
        w_gate = [gate_weight, gate_c, gate_x, gate_y, gate_xc, gate_yc]
        w_up = [up_weight, up_c, up_x, up_z, up_xc, up_zc]
        offs_feed = jnp.concatenate([by_side, by_line])

        order.phase(up_zc, out_xc, out_yc)
        odd = me % 2
        place = jnp.stack([lax.axis_index("rep"), 1 + odd, 2 - odd, jnp.full_like(odd, 4)])
        place = place.astype(jnp.int32)
        chunk = functools.partial(Chunk, order, place)
        down_y = rep(down_x, 1)
        down_xc = grp(down_x, 1)
        mid, hid_two, act, slope, lin, act_rows = feed(
            offs_feed, mixed, order.now(x), gains[1:2], w_out, w_gate, w_up
        )

        order.phase(down_y, down_xc, mid)
        down_yc = grp(down_y, 1)
        w_down = [down_weight, down_c, down_x, down_y, down_xc, down_yc]
        down = chunk(products(info, order.now(act_rows), upstream, parts))

        order.phase(down_yc, down.pairs[0][0])
        down.core()
        dgate, dup = slopes(by_down, order.now(upstream), w_down, slope, lin)
        up = chunk(products(info, hid_two, dup, parts))

        order.phase(*down.got, up.pairs[0][0])
        down.add_core()
        down.cross()
        up.core()
        dmid, fgain, dmix, *out_pair = middle_grads(
            offs_feed, info, order.free(upstream), gains[1:2], mixed, w_out, w_gate, w_up,
            dgate, dup, mid, parts,
        )
        out = chunk(out_pair)
        out.core()
        gate = chunk(products(info, after(hid_two, dmix), dgate, parts))
        part = 4
        state = attend_back(info, fac, kv, after(dmix, gate.pairs[0][0]), lse, 0, part, ())

        order.phase(down.got, *up.got, *out.got, state[0])
        both = chunk(*up.pairs, *out.pairs)
        both.got = up.got + out.got
        both.add_core()
        both.cross()
        down.fold(0)
        gate.core()
        dq, *terms = attend_back(info, fac, kv, order.free(dmix), lse, part, HEADS - part, state)

        order.phase(both.got, down.got, *gate.got, dq)
        dkv = chunk(terms)
        dkv.core()
        down.fold(1)
        order.flush()
        both.fold(0, start=False)

        order.phase(*dkv.got, down.got, both.other)
        both.go(0)
        dkv.pair()
        down.fold(2)
        order.flush()
        gate.add_core()

        order.phase(dkv.got, down.got, gate.other)
        gate.cross()
        sums = []
        order.add("sum", 0, dkv.mine, dkv.got, sums.append)
        down.swap(2)
        order.flush()
        input_grad, *terms = tail(
            quarter, info, dq, sums[0], cosine, sine, hid_one, x, gains[0:1], dmid, fgain,
            w_fac, cols, parts,
        )

        order.phase(both.got, down.got, input_grad)
        factor = chunk(terms)
        factor.core()
        both.fold(1)
        down.open(1)
        order.flush()

        order.phase(*factor.got, both.got, down.got)
        factor.pair()
        both.fold(2)
        down.open(0)
        order.flush()
        gate.got = after(gate.got, factor.mine)
        gate.fold(0)

        order.phase(factor.got, both.got, down.got, gate.got)
        factor.fold(0)
        gate.fold(1)
        both.swap(2)
        order.flush()
        (down_grad,) = down.finish(down_weight.shape[1])

        order.phase(factor.got, both.got, gate.got, down_grad)
        factor.swap(1)
        gate.fold(2)
        both.open(1)
        order.flush()

        order.phase(factor.got, both.got, gate.got)
        gate.swap(2)
        both.open(0)
        order.flush()
        result = output(by_down, order.free(act), mid, w_down)

        order.phase(both.got, gate.got, result)
        factor.swap(2, 2)
        gate.open(1)
        order.flush()
        up_grad, out_grad = both.finish(up_weight.shape[1], output_weight.shape[1])

        order.phase(factor.got, gate.got, up_grad)
        factor.swap(0, 1)
        gate.open(0)
        order.flush()

        order.phase(factor.got, gate.got)
        (fac_grad,) = factor.finish(shard_rows)
        (gate_grad,) = gate.finish(gate_weight.shape[1])
    return (
        result[None],
        input_grad[None],
        fac_grad[cols],
        fac_grad[:cols].T,
        out_grad,
        fac_grad[cols + 1],
        gate_grad,
        up_grad,
        down_grad,
    )


def solution(mesh):
    in_specs = (
        P("rep", "grp", None),
        P("rep", None),
        P("grp"),
        P("grp", None),
        P("grp", None),
        P("grp"),
        P("grp", None),
        P("grp", None),
        P("grp", None),
        P("rep", "grp", None),
    )
    out_specs = (
        P("rep", "grp", None),
        P("rep", "grp", None),
        P("grp"),
        P("grp", None),
        P("grp", None),
        P("grp"),
        P("grp", None),
        P("grp", None),
        P("grp", None),
    )
    return jax.shard_map(local, mesh=mesh, in_specs=in_specs, out_specs=out_specs, check_vma=False)
```

```python
import functools

import jax
import jax.numpy as jnp
import numpy as np
from jax import lax
from jax.experimental import pallas as pl
from jax.experimental.pallas import tpu as pltpu
from jax.sharding import PartitionSpec as P

HEADS = 16
HDIM = 64
QRANK = 6
KRANK = 2
HALF = HDIM // 2
QCOLS = QRANK * HEADS + QRANK * HDIM
KVCOLS = 2 * (KRANK * HEADS + KRANK * HDIM)
AQ, BQ = 0, QRANK * HEADS
AK, BK = 0, KRANK * HEADS
AV = BK + KRANK * HDIM
BV = AV + KRANK * HEADS
SCALE = HDIM**-0.5
EXP_SCALE = SCALE * float(np.log2(np.e))
NEG = -1e30
DEPTH = 128
EPS = 1e-05
VMEM_LIMIT = 60 * 2**20

f32 = jnp.float32
bf16 = jnp.bfloat16
NN = (((1,), (0,)), ((), ()))
NT = (((1,), (1,)), ((), ()))
TN = (((0,), (0,)), ((), ()))


def mm(left, right, dims=NN):
    return lax.dot_general(left, right, dims, preferred_element_type=f32)


def vmem():
    return pl.BlockSpec(memory_space=pltpu.VMEM)


def smem():
    return pl.BlockSpec(memory_space=pltpu.SMEM)


def params():
    return pltpu.CompilerParams(vmem_limit_bytes=VMEM_LIMIT)


def cost(flops, nbytes):
    return pl.CostEstimate(flops=int(flops) // 10**5, bytes_accessed=int(nbytes) // 10**5, transcendentals=0)


def weighty(micros):
    return pl.CostEstimate(flops=int(micros * 1.1e9), bytes_accessed=0, transcendentals=0)


def turn(part, cosine, sine):
    first, second = part[:HALF], part[HALF:]
    return first * cosine - second * sine, second * cosine + first * sine


def front_kernel(count, offs, x_ref, cos_ref, sin_ref, *refs):
    pieces, gain_refs = refs[:count], refs[count : 2 * count]
    fac_ref, kv_ref, hid_ref, gains_ref, w, sems = refs[2 * count :]
    w_in = Mover(sems).columns(offs, pieces, w)
    for i, ref in enumerate(gain_refs):
        size = ref.shape[1]
        at = offs[2 * i] if size % 128 == 0 else 0
        gains_ref[0:2, pl.ds(pl.multiple_of(at, 128), size)] = ref[...].astype(f32)
    xf = x_ref[...].astype(f32)
    normed = xf * lax.rsqrt(jnp.mean(xf * xf, axis=-1, keepdims=True) + EPS)
    hidden = (normed * gains_ref[0:1, :]).astype(bf16)
    turned = jnp.transpose(hidden)
    hid_ref[...] = turned
    wait(w_in)
    raw = mm(w[...], turned)
    cosine, sine = cos_ref[...], sin_ref[...]
    fac_ref[...] = raw[:QCOLS].astype(bf16)
    kv_ref[...] = raw[QCOLS:].astype(bf16)
    for ref, first, at in [(fac_ref, 0, BQ + r * HDIM) for r in range(QRANK)] + [
        (kv_ref, QCOLS, BK + r * HDIM) for r in range(KRANK)
    ]:
        one, two = turn(raw[first + at : first + at + HDIM], cosine, sine)
        ref[at : at + HALF, :] = one.astype(bf16)
        ref[at + HALF : at + HDIM, :] = two.astype(bf16)


def front(offs, x, cosine, sine, w_fac, gains):
    rows, width = x.shape
    cols = w_fac[0].shape[0]
    count = len(w_fac)
    return pl.pallas_call(
        functools.partial(front_kernel, count),
        out_shape=[
            like(QCOLS, rows),
            like(cols - QCOLS, rows),
            like(width, rows),
            like(8, width, dtype=f32),
        ],
        in_specs=[smem()] + [vmem()] * 3 + [anywhere()] * count + [vmem()] * count,
        out_specs=[vmem()] * 4,
        scratch_shapes=[scratch(cols, width), pltpu.SemaphoreType.DMA((count,))],
        compiler_params=params(),
        cost_estimate=cost(2 * rows * width * cols, 4 * width * (cols + rows)),
        name="front",
    )(offs, x, cosine, sine, *w_fac, *gains)


def load_factors(fac_ref, kv_refs, facf, kvf, qT, me):
    facf[...] = fac_ref[...].astype(f32)
    if len(kv_refs) == 1:

        def load(j, _):
            kvf[j] = kv_refs[0][j].astype(f32)
            return 0

        lax.fori_loop(0, kvf.shape[0], load, 0)
    else:
        for flip, ref in enumerate(kv_refs):
            kvf[me ^ flip] = ref[...].astype(f32)
    row = lax.broadcasted_iota(jnp.int32, (DEPTH - HDIM, qT.shape[1]), 0)
    qT[HDIM:DEPTH, :] = jnp.where(row == 0, 1.0, 0.0).astype(bf16)


def build_query(facf, qT, h):
    total = facf[pl.ds(AQ + h, 1), :] * facf[BQ : BQ + HDIM, :]
    for r in range(1, QRANK):
        total += facf[pl.ds(AQ + r * HEADS + h, 1), :] * facf[BQ + r * HDIM : BQ + (r + 1) * HDIM, :]
    qT[0:HDIM, :] = (total * (1.0 / QRANK)).astype(bf16)


def build_pair(kvf, j, h, a_at, b_at):
    total = kvf[j, pl.ds(a_at + h, 1), :] * kvf[j, b_at : b_at + HDIM, :]
    for r in range(1, KRANK):
        total += (
            kvf[j, pl.ds(a_at + r * HEADS + h, 1), :]
            * kvf[j, b_at + r * HDIM : b_at + (r + 1) * HDIM, :]
        )
    return (total * (1.0 / KRANK)).astype(bf16)


def build_key(kvf, kT, j, h, limit):
    span = kT.shape[1]
    kT[0:HDIM, :] = build_pair(kvf, j, h, AK, BK)
    if limit is None:
        kT[HDIM:DEPTH, :] = jnp.zeros((DEPTH - HDIM, span), bf16)
    else:
        row = lax.broadcasted_iota(jnp.int32, (DEPTH - HDIM, span), 0)
        key = j * span + lax.broadcasted_iota(jnp.int32, (DEPTH - HDIM, span), 1)
        kT[HDIM:DEPTH, :] = jnp.where((row == 0) & (key >= limit), NEG, 0.0).astype(bf16)


def causal(scores):
    key = lax.broadcasted_iota(jnp.int32, scores.shape, 0)
    query = lax.broadcasted_iota(jnp.int32, scores.shape, 1)
    return jnp.where(key <= query, scores, NEG)


def attend_kernel(first, heads, count, info_ref, fac_ref, *refs):
    kv_refs, (out_ref, lse_ref, facf, kvf, qT, kT, s_ref) = refs[:count], refs[count:]
    me, npc, limit = info_ref[0], info_ref[1], info_ref[2]
    rows = fac_ref.shape[1]
    load_factors(fac_ref, kv_refs, facf, kvf, qT, me)

    def head(step, _):
        h = first + step
        build_query(facf, qT, h)

        def chunk(j, top):
            build_key(kvf, kT, j, h, limit)
            scores = mm(kT[...], qT[...], TN)
            s_ref[j] = scores
            return jnp.maximum(top, jnp.max(scores, axis=0, keepdims=True))

        top = lax.fori_loop(0, npc, chunk, jnp.full((1, rows), NEG, f32))
        build_key(kvf, kT, me, h, None)
        scores = causal(mm(kT[...], qT[...], TN))
        s_ref[npc] = scores
        top = jnp.maximum(top, jnp.max(scores, axis=0, keepdims=True)) * EXP_SCALE

        def weigh(j, mass):
            probs = jnp.exp2(s_ref[j] * EXP_SCALE - top)
            s_ref[j] = probs
            return mass + jnp.sum(probs, axis=0, keepdims=True)

        mass = lax.fori_loop(0, npc + 1, weigh, jnp.zeros((1, rows), f32))
        lse_ref[pl.ds(step, 1), :] = top + jnp.log2(mass)
        share = 1.0 / mass

        def gather(j, total):
            at = jnp.where(j == npc, me, j)
            return total + mm(build_pair(kvf, at, h, AV, BV), (s_ref[j] * share).astype(bf16))

        total = lax.fori_loop(0, npc + 1, gather, jnp.zeros((HDIM, rows), f32))
        out_ref[pl.ds(pl.multiple_of(step * HDIM, HDIM), HDIM), :] = total.astype(bf16)
        return 0

    lax.fori_loop(0, heads, head, 0)


def kv_sizes(kv):
    return kv[0].shape if len(kv) == 1 else (len(kv),) + kv[0].shape


def attend(info, fac, kv, first, heads):
    parts, cols, rows = kv_sizes(kv)
    seen = min(parts, parts // 2 + 1)
    return pl.pallas_call(
        functools.partial(attend_kernel, first, heads, len(kv)),
        out_shape=[
            jax.ShapeDtypeStruct((heads * HDIM, rows), bf16),
            jax.ShapeDtypeStruct((heads, rows), f32),
        ],
        in_specs=[smem(), vmem()] + [vmem()] * len(kv),
        out_specs=[vmem()] * 2,
        scratch_shapes=[
            pltpu.VMEM((QCOLS, rows), f32),
            pltpu.VMEM((parts, cols, rows), f32),
            pltpu.VMEM((DEPTH, rows), bf16),
            pltpu.VMEM((DEPTH, rows), bf16),
            pltpu.VMEM((seen, rows, rows), f32),
        ],
        compiler_params=params(),
        cost_estimate=cost(16 * 2 * heads * 256 * rows * rows * seen, 4 * cols * rows * parts),
        name="attend",
    )(info, fac, *kv)


def attend_back_kernel(
    first, heads, final, count, count_out, blocks, info_ref, fac_ref, grad_ref, *refs
):
    kv_refs, lse_refs, refs = refs[:count], refs[count : count + blocks], refs[count + blocks :]
    if first:
        dq_in, dkv_in, *refs = refs
    dq_ref, *refs = refs
    if final:
        outs, refs = refs[:count_out], refs[count_out:]
        dkvf, *refs = refs
    else:
        dkvf, *refs = refs
    facf, kvf, qT, kTs, p_ref, dp_ref, lse_ref = refs
    for i, ref in enumerate(lse_refs):
        lse_ref[i * ref.shape[0] : (i + 1) * ref.shape[0], :] = ref[...]
    me, npc, limit = info_ref[0], info_ref[1], info_ref[2]
    parts, _, rows = kvf.shape
    load_factors(fac_ref, kv_refs, facf, kvf, qT, me)

    def begin(j, _):
        dkvf[j] = dkv_in[j] if first else jnp.zeros(dkvf.shape[1:], f32)
        return 0

    lax.fori_loop(0, parts, begin, 0)
    dq_ref[...] = dq_in[...] if first else jnp.zeros(dq_ref.shape, f32)

    def head(step, _):
        h = first + step
        build_query(facf, qT, h)
        grad = grad_ref[pl.ds(pl.multiple_of(h * HDIM, HDIM), HDIM), :]
        lse = lse_ref[pl.ds(h, 1), :]

        def probe(slot, at, scores, delta):
            probs = jnp.exp2(scores * EXP_SCALE - lse)
            p_ref[slot] = probs
            prob_grad = mm(build_pair(kvf, at, h, AV, BV), grad, TN)
            dp_ref[slot] = prob_grad
            return delta + jnp.sum(probs * prob_grad, axis=0, keepdims=True)

        def chunk(j, delta):
            build_key(kvf, kTs.at[j], j, h, limit)
            return probe(j, j, mm(kTs[j], qT[...], TN), delta)

        delta = lax.fori_loop(0, npc, chunk, jnp.zeros((1, rows), f32))
        build_key(kvf, kTs.at[npc], me, h, None)
        delta = probe(npc, me, causal(mm(kTs[npc], qT[...], TN)), delta)

        def pull(j, total):
            at = jnp.where(j == npc, me, j)
            probs = p_ref[j]
            score_grad = (probs * (dp_ref[j] - delta)).astype(bf16)
            key_grad = mm(qT[0:HDIM, :], score_grad, NT) * (SCALE / KRANK)
            value_grad = mm(grad, probs.astype(bf16), NT) * (1.0 / KRANK)
            for a_at, b_at, got in ((AK, BK, key_grad), (AV, BV, value_grad)):
                for r in range(KRANK):
                    a_row = pl.ds(a_at + r * HEADS + h, 1)
                    b_rows = slice(b_at + r * HDIM, b_at + (r + 1) * HDIM)
                    dkvf[at, a_row, :] = jnp.sum(got * kvf[at, b_rows, :], axis=0, keepdims=True)
                    dkvf[at, b_rows, :] += got * kvf[at, a_row, :]
            return total + mm(kTs[j, 0:HDIM, :], score_grad)

        query_grad = lax.fori_loop(0, npc + 1, pull, jnp.zeros((HDIM, rows), f32)) * (SCALE / QRANK)
        for r in range(QRANK):
            a_row = pl.ds(AQ + r * HEADS + h, 1)
            b_rows = slice(BQ + r * HDIM, BQ + (r + 1) * HDIM)
            dq_ref[a_row, :] = jnp.sum(query_grad * facf[b_rows, :], axis=0, keepdims=True)
            dq_ref[b_rows, :] += query_grad * facf[a_row, :]
        return 0

    lax.fori_loop(0, heads, head, 0)
    if final:
        for flip in range(parts):
            outs[flip % 2][flip // 2] = dkvf[me ^ flip].astype(bf16)


def attend_back(info, fac, kv, grad, lse, first, heads, so_far, declared=None):
    parts, cols, rows = kv_sizes(kv)
    seen = min(parts, parts // 2 + 1)
    final = first + heads == HEADS
    gathered = [like(parts // 2, cols, rows)] * 2 if final else [like(parts, cols, rows, dtype=f32)]
    return pl.pallas_call(
        functools.partial(
            attend_back_kernel, first, heads, final, len(kv), len(gathered), len(lse)
        ),
        out_shape=[like(QCOLS, rows, dtype=f32)] + gathered,
        in_specs=[smem()] + [vmem()] * (2 + len(kv) + len(lse) + len(so_far)),
        out_specs=[vmem()] * (1 + len(gathered)),
        scratch_shapes=([pltpu.VMEM((parts, cols, rows), f32)] if final else [])
        + [
            pltpu.VMEM((QCOLS, rows), f32),
            pltpu.VMEM((parts, cols, rows), f32),
            pltpu.VMEM((DEPTH, rows), bf16),
            pltpu.VMEM((seen, DEPTH, rows), bf16),
            pltpu.VMEM((seen, rows, rows), f32),
            pltpu.VMEM((seen, rows, rows), f32),
            pltpu.VMEM((HEADS, rows), f32),
        ],
        compiler_params=params(),
        cost_estimate=declared or cost(heads * rows * rows, 8 * cols * rows * parts),
        name="attend_back",
    )(info, fac, grad, *kv, *lse, *so_far)


class Mover:
    def __init__(self, sems):
        self.sems = sems
        self.used = 0

    def start(self, src, dst):
        copy = pltpu.make_async_copy(src, dst, self.sems.at[self.used])
        self.used += 1
        copy.start()
        return copy

    def pieces(self, offsets, refs, dst, first=0):
        copies = []
        for i, piece in enumerate(refs):
            rows, cols = piece.shape
            at = pl.ds(pl.multiple_of(offsets[first + 2 * i], 16), rows)
            if cols == dst.shape[1]:
                where = dst.at[at]
            else:
                where = dst.at[at, pl.ds(pl.multiple_of(offsets[first + 2 * i + 1], 128), cols)]
            copies.append(self.start(piece, where))
        return copies


    def columns(self, offsets, refs, dst):
        copies = []
        for i, piece in enumerate(refs):
            cols = piece.shape[1]
            if cols == dst.shape[1]:
                copies.append(self.start(piece, dst))
            else:
                at = pl.ds(pl.multiple_of(offsets[2 * i], 128), cols)
                copies.append(self.start(piece, dst.at[:, at]))
        return copies


def wait(copies):
    for copy in copies:
        copy.wait()


def anywhere():
    return pl.BlockSpec(memory_space=pl.ANY)


def like(*shape, dtype=bf16):
    return jax.ShapeDtypeStruct(shape, dtype)


def scratch(*shape, dtype=bf16):
    return pltpu.VMEM(shape, dtype)


TILE = 256


def norm_back(grad_hidden, normed, scale, gain):
    grad_normed = grad_hidden * gain
    gain_grad = jnp.sum(grad_hidden * normed, axis=0, keepdims=True)
    mean = jnp.mean(grad_normed * normed, axis=-1, keepdims=True)
    return gain_grad, scale * (grad_normed - normed * mean)


def shard_products(me, left, right, pair, mover, pair_out):
    copies = []
    count, rows, cols = pair[0].shape
    step = rows if rows <= 352 else rows // 2
    width = cols // 2 if cols % 256 == 0 and cols > 2048 else cols
    for odd in (1, 0):
        for j in range(count):
            row = (me ^ (2 * j + odd)) * rows
            for low in range(0, rows, step):
                lhs = left[pl.ds(pl.multiple_of(row + low, 16), step), :]
                for at in range(0, cols, width):
                    pair[odd][j, low : low + step, at : at + width] = mm(
                        lhs, right[:, at : at + width]
                    ).astype(bf16)
            copies.append(mover.start(pair[odd].at[j], pair_out[odd].at[j]))
    return copies


def feed_kernel(count, blocks, offs, x_ref, gain_ref, *refs):
    mix_refs, refs = refs[:blocks], refs[blocks:]
    out_pieces, gate_pieces, lift_pieces = (refs[i * count : (i + 1) * count] for i in range(3))
    refs = refs[3 * count :]
    (mid_o, hid_o, act_o, slope_o, lin_o, actT_o) = refs[:6]
    (wo, wg, wu, mid, hid, hidT, act, slope, lin, actT, sems) = refs[6:]
    mover = Mover(sems)
    wo_in = mover.pieces(offs, out_pieces, wo)
    wg_in = mover.pieces(offs, gate_pieces, wg)
    wu_in = mover.pieces(offs, lift_pieces, wu, 2 * count)
    mix = jnp.concatenate([jnp.transpose(ref[...]) for ref in mix_refs], axis=1)
    wait(wo_in)
    middle = x_ref[...].astype(f32) + mm(mix, wo[...])
    mid[...] = middle
    scale = lax.rsqrt(jnp.mean(middle * middle, axis=-1, keepdims=True) + EPS)
    hidden = (middle * scale * gain_ref[...]).astype(bf16)
    hid[...] = hidden
    hidT[...] = jnp.transpose(hidden)
    done = [mover.start(mid, mid_o), mover.start(hidT, hid_o)]
    wait(wg_in)
    wait(wu_in)

    def tile(j, _):
        cols = pl.ds(pl.multiple_of(j * TILE, TILE), TILE)
        gate = mm(hid[...], wg[:, cols])
        up = mm(hid[...], wu[:, cols])
        sig = jax.nn.sigmoid(gate)
        line = gate * sig
        active = (line * up).astype(bf16)
        act[:, cols] = active
        lin[:, cols] = line.astype(bf16)
        slope[:, cols] = (up * sig * (1.0 + gate * (1.0 - sig))).astype(bf16)
        actT[cols, :] = jnp.transpose(active)
        return 0

    lax.fori_loop(0, wg.shape[1] // TILE, tile, 0, unroll=True)
    done += [mover.start(act, act_o), mover.start(lin, lin_o), mover.start(slope, slope_o)]
    done.append(mover.start(actT, actT_o))
    wait(done)


def feed(offs, mix, x, gain, w_out, w_gate, w_up):
    rows, width = x.shape
    inner = w_gate[0].shape[1]
    count = len(w_gate)
    return pl.pallas_call(
        functools.partial(feed_kernel, count, len(mix)),
        out_shape=[
            like(rows, width, dtype=f32),
            like(width, rows),
            like(rows, inner),
            like(rows, inner),
            like(rows, inner),
        ]
        + [like(inner, rows)],
        in_specs=[smem()] + [vmem()] * (2 + len(mix)) + [anywhere()] * (3 * count),
        out_specs=[anywhere()] * 6,
        scratch_shapes=[
            scratch(width, width),
            scratch(width, inner),
            scratch(width, inner),
            scratch(rows, width, dtype=f32),
            scratch(rows, width),
            scratch(width, rows),
            scratch(rows, inner),
            scratch(rows, inner),
            scratch(rows, inner),
            scratch(inner, rows),
            pltpu.SemaphoreType.DMA((3 * count + 6,)),
        ],
        compiler_params=params(),
        cost_estimate=cost(2 * rows * width * (width + 3 * inner), 2 * inner * (3 * width + 3 * rows)),
        name="feed",
    )(offs, x, gain, *mix, *w_out, *w_gate, *w_up)


def slopes_kernel(count, offs, slope_ref, lin_ref, c_ref, *refs):
    pieces, (dg_o, du_o, wd, dg, du, sems) = refs[:count], refs[count:]
    mover = Mover(sems)
    wait(mover.pieces(offs, pieces, wd))

    def tile(j, _):
        cols = pl.ds(pl.multiple_of(j * TILE, 128), TILE)
        grad = mm(c_ref[...], wd[cols, :], NT)
        dg[:, cols] = (grad * slope_ref[:, cols].astype(f32)).astype(bf16)
        du[:, cols] = (grad * lin_ref[:, cols].astype(f32)).astype(bf16)
        return 0

    lax.fori_loop(0, wd.shape[0] // TILE, tile, 0, unroll=True)
    wait([mover.start(dg, dg_o), mover.start(du, du_o)])


def slopes(offs, upstream, w_down, slope, lin):
    rows, width = upstream.shape
    inner = slope.shape[1]
    count = len(w_down)
    return pl.pallas_call(
        functools.partial(slopes_kernel, count),
        out_shape=[like(rows, inner)] * 2,
        in_specs=[smem()] + [vmem()] * 3 + [anywhere()] * count,
        out_specs=[anywhere()] * 2,
        scratch_shapes=[
            scratch(inner, width),
            scratch(rows, inner),
            scratch(rows, inner),
            pltpu.SemaphoreType.DMA((count + 2,)),
        ],
        compiler_params=params(),
        cost_estimate=cost(2 * rows * width * inner, 2 * inner * (width + 4 * rows)),
        name="slopes",
    )(offs, slope, lin, upstream, *w_down)


def products_kernel(who, left, right, *refs):
    outs, pair, sems = refs[0:2], refs[2:4], refs[4]
    wait(shard_products(who[0], left, right, pair, Mover(sems), outs))


def products(who, left, right, parts):
    width, rows = left.shape
    inner = right.shape[1]
    pair = (parts // 2, width // parts, inner)
    return pl.pallas_call(
        products_kernel,
        out_shape=[like(*pair)] * 2,
        in_specs=[smem()] + [vmem()] * 2,
        out_specs=[anywhere()] * 2,
        scratch_shapes=[scratch(*pair)] * 2 + [pltpu.SemaphoreType.DMA((parts,))],
        compiler_params=params(),
        cost_estimate=cost(2 * rows * width * inner, 2 * inner * (width + rows)),
        name="products",
    )(who, left, right)


def middle_kernel(count, blocks, offs, who, c_ref, gain_ref, *refs):
    out_pieces, gate_pieces, lift_pieces = (refs[i * count : (i + 1) * count] for i in range(3))
    mix_refs, refs = refs[3 * count : 3 * count + blocks], refs[3 * count + blocks :]
    dg_i, du_i, mid_i, dmid_o, fgain, dmix, *refs = refs
    outs, (wg, wu, wo, dg, du, mid, dhid, branch, mix), pair, sems = refs[:2], refs[2:11], refs[11:13], refs[13]
    mover = Mover(sems)
    in_dg = [mover.start(dg_i, dg)]
    in_wg = mover.pieces(offs, gate_pieces, wg)
    in_du = [mover.start(du_i, du)]
    in_wu = mover.pieces(offs, lift_pieces, wu, 2 * count)
    in_mid = [mover.start(mid_i, mid)]
    in_wo = mover.pieces(offs, out_pieces, wo)
    width = wg.shape[0]

    def back(which, j):
        at = pl.ds(pl.multiple_of(j * TILE, TILE), TILE)
        if which == 0:
            dhid[:, at] = mm(dg[...], wg[at, :], NT)
        else:
            dhid[:, at] += mm(du[...], wu[at, :], NT)
        return 0

    wait(in_dg + in_wg)
    lax.fori_loop(0, width // TILE, lambda j, _: back(0, j), 0, unroll=True)
    wait(in_du + in_wu)
    lax.fori_loop(0, width // TILE, lambda j, _: back(1, j), 0, unroll=True)
    wait(in_mid + in_wo)
    middle = mid[...]
    scale = lax.rsqrt(jnp.mean(middle * middle, axis=-1, keepdims=True) + EPS)
    gain_grad, part = norm_back(dhid[...], middle * scale, scale, gain_ref[...])
    fgain[...] = jnp.broadcast_to(gain_grad, fgain.shape)
    total = c_ref[...].astype(f32) + part
    dhid[...] = total
    branch[...] = total.astype(bf16)
    done = [mover.start(dhid, dmid_o)]
    for i, ref in enumerate(mix_refs):
        size = ref.shape[0]
        mix[i * size : (i + 1) * size, :] = ref[...]
    done += shard_products(who[0], mix, branch, pair, mover, outs)
    dmix[...] = mm(wo[...], branch[...], NT).astype(bf16)
    wait(done)


def middle_grads(offs, who, upstream, gain, mix, w_out, w_gate, w_up, dg, du, mid, parts):
    rows, width = upstream.shape
    pair = (parts // 2, width // parts, width)
    inner = dg.shape[1]
    count = len(w_gate)
    return pl.pallas_call(
        functools.partial(middle_kernel, count, len(mix)),
        out_shape=[
            like(rows, width, dtype=f32),
            like(8, width, dtype=f32),
            like(width, rows),
            like(*pair),
            like(*pair),
        ],
        in_specs=[smem()] * 2
        + [vmem()] * 2
        + [anywhere()] * (3 * count)
        + [vmem()] * len(mix)
        + [anywhere()] * 3,
        out_specs=[anywhere()] + [vmem()] * 2 + [anywhere()] * 2,
        scratch_shapes=[
            scratch(width, inner),
            scratch(width, inner),
            scratch(width, width),
            scratch(rows, inner),
            scratch(rows, inner),
            scratch(rows, width, dtype=f32),
            scratch(rows, width, dtype=f32),
            scratch(rows, width),
            scratch(width, rows),
            scratch(*pair),
            scratch(*pair),
            pltpu.SemaphoreType.DMA((3 * count + 4 + parts,)),
        ],
        compiler_params=params(),
        cost_estimate=cost(2 * rows * width * (2 * inner + width), 4 * inner * (width + rows)),
        name="middle_grads",
    )(offs, who, upstream, gain, *w_out, *w_gate, *w_up, *mix, dg, du, mid)


def output_kernel(count, offs, act_ref, mid_ref, *refs):
    pieces, (res, wd, sems) = refs[:count], refs[count:]
    wait(Mover(sems).pieces(offs, pieces, wd))

    def forth(j, _):
        at = pl.ds(pl.multiple_of(j * TILE, TILE), TILE)
        res[:, at] = (mid_ref[:, at] + mm(act_ref[...], wd[:, at])).astype(bf16)
        return 0

    lax.fori_loop(0, wd.shape[1] // TILE, forth, 0, unroll=True)


def output(offs, act, mid, w_down):
    rows, width = mid.shape
    count = len(w_down)
    inner = act.shape[1]
    return pl.pallas_call(
        functools.partial(output_kernel, count),
        out_shape=like(rows, width),
        in_specs=[smem()] + [vmem()] * 2 + [anywhere()] * count,
        out_specs=vmem(),
        scratch_shapes=[scratch(inner, width), pltpu.SemaphoreType.DMA((count,))],
        compiler_params=params(),
        cost_estimate=cost(2 * rows * width * inner, 2 * inner * (width + rows)),
        name="output",
    )(offs, act, mid, *w_down)


def tail_kernel(count, cols, offs, who, dq_ref, own_ref, cos_ref, sin_ref, hid_ref, x_ref, gain_ref, dmid_ref, fgain_ref, *refs):
    pieces = refs[:count]
    grad_ref, *outs = refs[count:]
    *outs, w, raw, gain_cols, sems = outs
    mover = Mover(sems)
    w_in = mover.columns(offs, pieces, w)
    cosine, sine = cos_ref[...], -sin_ref[...]
    raw[0:QCOLS, :] = dq_ref[...].astype(bf16)
    raw[QCOLS:cols, :] = own_ref[...]
    raw[cols:, :] = jnp.zeros((raw.shape[0] - cols, raw.shape[1]), bf16)
    for r in range(QRANK):
        at = BQ + r * HDIM
        one, two = turn(dq_ref[at : at + HDIM, :], cosine, sine)
        raw[at : at + HALF, :] = one.astype(bf16)
        raw[at + HALF : at + HDIM, :] = two.astype(bf16)
    for r in range(KRANK):
        at = BK + r * HDIM
        one, two = turn(own_ref[at : at + HDIM, :].astype(f32), cosine, sine)
        raw[QCOLS + at : QCOLS + at + HALF, :] = one.astype(bf16)
        raw[QCOLS + at + HALF : QCOLS + at + HDIM, :] = two.astype(bf16)
    draw = jnp.transpose(raw[...])
    wait(w_in)
    xf = x_ref[...].astype(f32)
    scale = lax.rsqrt(jnp.mean(xf * xf, axis=-1, keepdims=True) + EPS)
    dhid = mm(draw[:, 0:cols], w[...])
    gain_grad, part = norm_back(dhid, xf * scale, scale, gain_ref[...])
    grad_ref[...] = dmid_ref[...] + part
    line = lax.broadcasted_iota(jnp.int32, (128, gain_grad.shape[1]), 0)
    both = jnp.where(line == 0, gain_grad, jnp.where(line == 1, fgain_ref[0:1, :], 0.0))
    gain_cols[...] = jnp.transpose(both)
    count_out, wide, rows = outs[0].shape
    for flip in range(2 * count_out):
        at = pl.ds(pl.multiple_of((who[0] ^ flip) * rows, 16), rows)
        out = outs[flip % 2]
        out[flip // 2, 0:cols, :] = mm(raw[0:cols, :], hid_ref[at, :], NT).astype(bf16)
        out[flip // 2, cols:wide, :] = jnp.transpose(gain_cols[at, :])[0 : wide - cols].astype(bf16)


def tail(offs, who, dq, own, cosine, sine, hidT, x, gain, dmid, fgain, w_fac, cols, parts):
    rows, width = x.shape
    wide = (cols // 128 + 1) * 128
    count = len(w_fac)
    shard = (parts // 2, wide, width // parts)
    return pl.pallas_call(
        functools.partial(tail_kernel, count, cols),
        out_shape=[like(rows, width, dtype=f32)] + [like(*shard)] * 2,
        in_specs=[smem()] * 2 + [vmem()] * 9 + [anywhere()] * count,
        out_specs=[vmem()] * 3,
        scratch_shapes=[
            scratch(cols, width),
            scratch(wide, rows),
            scratch(width, 128, dtype=f32),
            pltpu.SemaphoreType.DMA((count,)),
        ],
        compiler_params=params(),
        cost_estimate=cost(4 * rows * width * cols, 4 * width * (cols + 3 * rows)),
        name="tail",
    )(offs, who, dq, own, cosine, sine, hidT, x, gain, dmid, fgain, *w_fac)


def partner(values, axis, flip):
    size = lax.axis_size(axis)
    return lax.ppermute(values, axis, [(i, i ^ flip) for i in range(size)])


def after(value, *earlier):
    if not earlier:
        return value
    return lax.optimization_barrier((value, *earlier))[0]


def places(pieces, rows, half):
    me = lax.axis_index("grp")
    at = []
    for flip, which in pieces:
        row = (me ^ flip) * rows
        at += [row if which is None else row + which * half, 0]
    return jnp.stack([jnp.asarray(v, jnp.int32) for v in at])


def total(*terms):
    got = terms[0].astype(f32)
    for term in terms[1:]:
        got = got + term.astype(f32)
    return got.astype(bf16)


def add_pairs_kernel(*refs):
    mine, other = refs[-2:]
    at = 0
    for keep, got in zip(refs[:-2:2], refs[1:-2:2]):
        cols = slice(at, at + keep.shape[2])
        mine[:, cols] = total(keep[0], got[0])
        other[:, cols] = total(keep[1], got[1])
        at += keep.shape[2]


def add_pairs(groups):
    rows = groups[0][0].shape[1]
    wide = sum(keep.shape[2] for keep, _ in groups)
    steps = next(n for n in (4, 2, 1) if n == 1 or (rows % (16 * n) == 0 and rows * wide > 2**19))
    out = pl.BlockSpec((rows // steps, wide), lambda i: (i, 0))
    terms = [term for group in groups for term in group]
    return pl.pallas_call(
        add_pairs_kernel,
        grid=(steps,),
        out_shape=[like(rows, wide)] * 2,
        in_specs=[pl.BlockSpec((2, rows // steps, v.shape[2]), lambda i: (0, i, 0)) for v in terms],
        out_specs=[out] * 2,
        compiler_params=params(),
        cost_estimate=cost(1, 1),
        name="add_pairs",
    )(*terms)


def halve_kernel(place, keep_one, keep_two, send_one, send_two, keep, send):
    keep[...] = total(keep_one[...], keep_two[...])
    send[...] = total(send_one[...], send_two[...])


def halve(place, one, two):
    rows, cols = one.shape[0] // 8, one.shape[1]
    one, two = (v.reshape(8, rows, cols) for v in (one, two))

    def piece(flip):
        def index(i, place):
            at = place[0] ^ ((i >> 1) * place[2]) ^ ((i & 1) * place[3])
            return (at ^ place[1] if flip else at, 0, 0)

        return pl.BlockSpec((1, rows, cols), index)

    out = pl.BlockSpec((1, rows, cols), lambda i, place: (i, 0, 0))
    return pl.pallas_call(
        halve_kernel,
        grid_spec=pltpu.PrefetchScalarGridSpec(
            num_scalar_prefetch=1,
            grid=(4,),
            in_specs=[piece(False)] * 2 + [piece(True)] * 2,
            out_specs=[out] * 2,
        ),
        out_shape=[like(4, rows, cols)] * 2,
        compiler_params=params(),
        cost_estimate=cost(1, 1),
        name="halve",
    )(place, one, two, one, two)


def batch_kernel(tasks, *refs):
    ins, outs = refs[: 2 * len(tasks)], list(refs[2 * len(tasks) :])
    for i, (kind, flip) in enumerate(tasks):
        one, two = ins[2 * i : 2 * i + 2]
        out = outs.pop(0)
        if kind == "split":
            half = out.shape[0]
            out[...] = total(one[:half], two[:half])
            outs.pop(0)[...] = total(one[half:], two[half:])
        elif kind == "pair":
            out[...] = total(one[0], two[0])
            outs.pop(0)[...] = total(one[1], two[1])
        elif kind == "join":
            half = one.shape[0]
            out[:half] = one[...]
            out[half:] = two[...]
        elif flip:
            for k in range(out.shape[0]):
                out[k] = total(one[k], two[k ^ flip])
        else:
            out[...] = total(one[...], two[...])


def batch(tasks):
    shapes, counts = [], []
    for kind, _, one, _ in tasks:
        first, rest = one.shape[0], one.shape[1:]
        got = {
            "split": [(first // 2,) + rest] * 2,
            "pair": [rest] * 2,
            "join": [(2 * first,) + rest],
            "sum": [one.shape],
        }[kind]
        shapes += got
        counts.append(len(got))
    outs = pl.pallas_call(
        functools.partial(batch_kernel, [task[:2] for task in tasks]),
        out_shape=[like(*shape) for shape in shapes],
        in_specs=[vmem()] * (2 * len(tasks)),
        out_specs=[vmem()] * len(shapes),
        compiler_params=params(),
        cost_estimate=cost(1, 1),
        name="batch",
    )(*[value for task in tasks for value in task[2:]])
    groups = []
    for count in counts:
        groups.append(outs[:count])
        outs = outs[count:]
    return groups


def finish_kernel(widths, place, near, far, *outs):
    _, rows, wide = near.shape
    for side, value in ((0, near), (1, far)):
        for k in range(4):
            at = place[0] ^ (side * place[1]) ^ ((k >> 1) * place[2]) ^ ((k & 1) * place[3])
            row = pl.ds(pl.multiple_of(at * rows, 8), rows)
            col = 0
            for out, cols in zip(outs, widths):
                out[row, :] = value[k, :, col : col + cols].astype(f32)
                col += cols


def finish(place, near, far, widths):
    rows = near.shape[1]
    return pl.pallas_call(
        functools.partial(finish_kernel, widths),
        out_shape=[like(8 * rows, cols, dtype=f32) for cols in widths],
        in_specs=[smem()] + [vmem()] * 2,
        out_specs=[vmem()] * len(widths),
        compiler_params=params(),
        cost_estimate=cost(1, 1),
        name="finish",
    )(place, near, far)


def scatter_all(keep, send):
    me = lax.axis_index("grp")
    both = jnp.stack([keep, send], axis=1)
    both = both.reshape((-1,) + both.shape[2:])
    both = jnp.take(both, jnp.arange(both.shape[0]) ^ me, axis=0)
    return lax.psum_scatter(both, "grp", scatter_dimension=0, tiled=False)


class Order:
    def __init__(self):
        self.last = None
        self.before = ()
        self.tasks = []

    def add(self, kind, flip, one, two, then):
        self.tasks.append(((kind, flip, self.free(one), two), then))

    def flush(self):
        groups = batch([task for task, _ in self.tasks])
        for (_, then), group in zip(self.tasks, groups):
            then(*group)
        self.tasks = []

    def __call__(self, value, *earlier):
        earlier = earlier if self.last is None else earlier + (self.last,)
        return after(value, *earlier) if earlier else value

    def phase(self, *results):
        self.before = results
        self.last = None

    def now(self, value, *earlier):
        last = () if self.last is None else (self.last,)
        return after(value, *self.before, *earlier, *last)

    def free(self, value):
        return after(value, *self.before)

    def ran(self, value):
        self.last = value
        return value


BITS = ((1, 2, 4), (2, 1, 4))


def along(values, step):
    reps, parts = lax.axis_size("rep"), lax.axis_size("grp")
    pairs = [
        (r * parts + g, (r ^ BITS[g % 2][step]) * parts + g)
        for r in range(reps)
        for g in range(parts)
    ]
    return lax.ppermute(values, ("rep", "grp"), pairs)


class Chunk:
    def __init__(self, order, place, *pairs):
        self.order, self.place, self.pairs = order, place, pairs

    def core(self):
        send = [after(pair[1], *self.order.before) for pair in self.pairs]
        self.got = [partner(value, "grp", 1) for value in send]

    def add_core(self):
        keep = [self.order.now(self.pairs[0][0])] + [pair[0] for pair in self.pairs[1:]]
        self.mine, self.other = add_pairs(list(zip(keep, self.got)))
        self.order.ran(self.other)

    def cross(self):
        self.got = partner(self.order.free(self.other), "grp", 2)

    def go(self, step):
        self.got = along(self.order.free(self.other), step)

    def fold(self, step, start=True):
        def then(mine, other):
            self.mine, self.other = mine, other
            if start:
                self.got = along(other, step)

        if step == 0:
            then(*halve(self.place, self.order.now(self.mine), self.got))
            self.order.ran(self.other)
        else:
            self.order.add("split", 0, self.mine, self.got, then)

    def pair(self):
        def then(mine, other):
            self.mine = mine
            self.got = partner(other, "grp", 2)

        self.order.add("pair", 0, self.pairs[0][0], self.got[0], then)

    def swap(self, step, flip=0):
        def then(mine):
            self.mine = mine
            self.got = along(mine, step)

        self.order.add("sum", flip, self.mine, self.got, then)

    def open(self, step):
        def then(mine):
            self.mine = mine
            self.got = along(mine, step)

        self.order.add("join", 0, self.mine, self.got, then)

    def finish(self, *widths):
        got = finish(self.place, self.order.now(self.mine), self.got, widths)
        self.order.ran(got[0])
        return got


def local(
    layer_input,
    branch,
    attention_gain,
    factor_weight,
    output_weight,
    feed_gain,
    gate_weight,
    up_weight,
    down_weight,
    cotangent,
):
    rows = layer_input.shape[1]
    parts = lax.axis_size("grp")
    me = lax.axis_index("grp")
    prompt_parts = parts // 2
    follows = me >= prompt_parts
    chosen = branch[0, jnp.maximum(me - prompt_parts, 0)]
    limit = jnp.where(follows, chosen, me * rows)
    npc = (limit + rows - 1) // rows
    position = jnp.where(follows, chosen, me * rows) + jnp.arange(rows, dtype=jnp.int32)
    info = jnp.stack([me, npc, limit]).astype(jnp.int32)
    freqs = 10000.0 ** (-jnp.arange(HALF).astype(f32) / HALF)
    phase = freqs[:, None] * position.astype(f32)[None, :]
    cosine, sine = jnp.cos(phase), jnp.sin(phase)

    x = layer_input[0]
    upstream = cotangent[0]
    shard_rows, cols = factor_weight.shape
    own_gains = jnp.stack([attention_gain, feed_gain])
    factor_turned = factor_weight.T
    gather = lambda value: lax.all_gather(value, "grp", axis=0, tiled=True)

    if parts != 4 or lax.axis_size("rep") != 8:
        whole = jnp.zeros((4,), jnp.int32)
        w_out, w_down = [gather(output_weight)], [gather(down_weight)]
        w_fac = [lax.all_gather(factor_turned, "grp", axis=1, tiled=True)]
        w_gate, w_up = [gather(gate_weight)], [gather(up_weight)]
        all_gains = lax.all_gather(own_gains, "grp", axis=1, tiled=True)
        fac, kv_own, hid_one, gains = front(whole, x, cosine, sine, w_fac, [all_gains])
        kv = [lax.all_gather(kv_own, "grp", axis=0, tiled=False)]
        mixed, lse = ([got] for got in attend(info, fac, kv, 0, HEADS))
        mid, hid_two, act, slope, lin, act_rows = feed(
            whole, mixed, x, gains[1:2], w_out, w_gate, w_up
        )
        down_pair = products(info, act_rows, upstream, parts)
        dgate, dup = slopes(whole, upstream, w_down, slope, lin)
        up_pair = products(info, hid_two, dup, parts)
        dmid, fgain, dmix, *out_pair = middle_grads(
            whole, info, upstream, gains[1:2], mixed, w_out, w_gate, w_up, dgate, dup, mid, parts
        )
        gate_pair = products(info, hid_two, dgate, parts)
        result = output(whole, act, mid, w_down)
        dq, *dkv = attend_back(info, fac, kv, dmix, lse, 0, HEADS, ())
        input_grad, *fac_pair = tail(
            whole, info, dq, scatter_all(*dkv), cosine, sine, hid_one, x, gains[0:1], dmid, fgain,
            w_fac, cols, parts,
        )
        pairs = (fac_pair, out_pair, gate_pair, up_pair, down_pair)
        shards = [scatter_all(*pair) for pair in pairs]
        sums = [lax.psum(shard, "rep").astype(f32) for shard in shards]
        fac_grad, out_grad, gate_grad, up_grad, down_grad = sums
    else:
        order = Order()
        low = lax.axis_index("rep") % 2
        even = (lax.axis_index("rep") // 2) % 2
        take = lambda v, which: lax.dynamic_slice_in_dim(v, which * (v.shape[0] // 2), v.shape[0] // 2, 0)
        quarter = places([(k, None) for k in range(4)], shard_rows, 0)
        halves = lambda v, rows: places(
            [(0, None), (1, None), (2, v), (2, 1 - v), (3, v), (3, 1 - v)], rows, rows // 2
        )
        by_side, by_line = halves(low, shard_rows), halves(even, shard_rows)
        by_down = halves(low, down_weight.shape[0])
        grp = lambda value, flip: partner(order.free(value), "grp", flip)
        rep = lambda value, flip: partner(order.free(value), "rep", flip)
        fac_x = partner(factor_turned, "grp", 2)
        fac_c = partner(factor_turned, "grp", 1)
        gains_x = partner(own_gains, "grp", 2)
        gains_c = partner(own_gains, "grp", 1)
        gate_c = partner(gate_weight, "grp", 1)
        gate_half, up_half = take(gate_weight, low), take(up_weight, even)
        out_half, down_half = take(output_weight, low), take(down_weight, low)
        order.phase(
            fac_x, fac_c, gains_x, gains_c, gate_c, gate_half, up_half, out_half, down_half
        )
        fac_xc = grp(fac_x, 1)
        gains_xc = grp(gains_x, 1)
        gate_x = grp(gate_half, 2)
        up_c = grp(up_weight, 1)
        out_c = grp(output_weight, 1)
        w_fac = [factor_turned, fac_c, fac_x, fac_xc]
        all_gains = [own_gains, gains_c, gains_x, gains_xc]
        fac, kv_own, hid_one, gains = front(
            quarter, order.now(x), cosine, sine, w_fac, all_gains
        )
        kv_x = partner(kv_own, "grp", 2)
        kv_c = partner(kv_own, "grp", 1)
        kv_xc = partner(kv_x, "grp", 1)
        kv = [kv_own, kv_c, kv_x, kv_xc]

        order.phase(gate_x, kv_x, kv_c, kv_xc, up_c, out_c)
        up_x = grp(up_half, 2)
        out_x = grp(out_half, 2)
        gate_y = rep(gate_x, 1)
        gate_xc = grp(gate_x, 1)
        down_c = grp(down_weight, 1)
        part = HEADS // 2
        heads = [attend(info, order.now(fac), kv, 0, part)]

        order.phase(up_x, out_x, gate_y, gate_xc, down_c, heads[0][0])
        down_x = grp(down_half, 2)
        up_z = rep(up_x, 2)
        up_xc = grp(up_x, 1)
        out_y = rep(out_x, 1)
        gate_yc = grp(gate_y, 1)
        heads.append(attend(info, order.now(fac), kv, part, part))
        mixed, lse = ([got[i] for got in heads] for i in range(2))

        order.phase(down_x, up_z, up_xc, out_y, gate_yc, heads[1][0])
        up_zc = grp(up_z, 1)
        out_xc = grp(out_x, 1)
        out_yc = grp(out_y, 1)
        w_out = [output_weight, out_c, out_x, out_y, out_xc, out_yc]
        w_gate = [gate_weight, gate_c, gate_x, gate_y, gate_xc, gate_yc]
        w_up = [up_weight, up_c, up_x, up_z, up_xc, up_zc]
        offs_feed = jnp.concatenate([by_side, by_line])

        order.phase(up_zc, out_xc, out_yc)
        odd = me % 2
        place = jnp.stack([lax.axis_index("rep"), 1 + odd, 2 - odd, jnp.full_like(odd, 4)])
        place = place.astype(jnp.int32)
        chunk = functools.partial(Chunk, order, place)
        down_y = rep(down_x, 1)
        down_xc = grp(down_x, 1)
        mid, hid_two, act, slope, lin, act_rows = feed(
            offs_feed, mixed, order.now(x), gains[1:2], w_out, w_gate, w_up
        )

        order.phase(down_y, down_xc, mid)
        down_yc = grp(down_y, 1)
        w_down = [down_weight, down_c, down_x, down_y, down_xc, down_yc]
        down = chunk(products(info, order.now(act_rows), upstream, parts))

        order.phase(down_yc, down.pairs[0][0])
        down.core()
        dgate, dup = slopes(by_down, order.now(upstream), w_down, slope, lin)
        up = chunk(products(info, hid_two, dup, parts))

        order.phase(*down.got, up.pairs[0][0])
        down.add_core()
        down.cross()
        up.core()
        dmid, fgain, dmix, *out_pair = middle_grads(
            offs_feed, info, order.free(upstream), gains[1:2], mixed, w_out, w_gate, w_up,
            dgate, dup, mid, parts,
        )
        out = chunk(out_pair)
        out.core()
        gate = chunk(products(info, after(hid_two, dmix), dgate, parts))
        part = 3
        state = attend_back(info, fac, kv, after(dmix, gate.pairs[0][0]), lse, 0, part, ())

        order.phase(down.got, *up.got, *out.got, state[0])
        both = chunk(*up.pairs, *out.pairs)
        both.got = up.got + out.got
        both.add_core()
        both.cross()
        down.fold(0)
        gate.core()
        dq, *terms = attend_back(info, fac, kv, order.free(dmix), lse, part, HEADS - part, state)

        order.phase(both.got, down.got, *gate.got, dq)
        dkv = chunk(terms)
        dkv.core()
        down.fold(1)
        order.flush()
        both.fold(0, start=False)

        order.phase(*dkv.got, down.got, both.other)
        both.go(0)
        dkv.pair()
        down.fold(2)
        order.flush()
        gate.add_core()

        order.phase(dkv.got, down.got, gate.other)
        gate.cross()
        sums = []
        order.add("sum", 0, dkv.mine, dkv.got, sums.append)
        down.swap(2)
        order.flush()
        input_grad, *terms = tail(
            quarter, info, dq, sums[0], cosine, sine, hid_one, x, gains[0:1], dmid, fgain,
            w_fac, cols, parts,
        )

        order.phase(both.got, down.got, input_grad)
        factor = chunk(terms)
        factor.core()
        both.fold(1)
        down.open(1)
        order.flush()

        order.phase(*factor.got, both.got, down.got)
        factor.pair()
        both.fold(2)
        down.open(0)
        order.flush()
        gate.got = after(gate.got, factor.mine)
        gate.fold(0)

        order.phase(factor.got, both.got, down.got, gate.got)
        factor.fold(0)
        gate.fold(1)
        both.swap(2)
        order.flush()
        (down_grad,) = down.finish(down_weight.shape[1])

        order.phase(factor.got, both.got, gate.got, down_grad)
        factor.swap(1)
        gate.fold(2)
        both.open(1)
        order.flush()

        order.phase(factor.got, both.got, gate.got)
        factor.swap(2, 2)
        gate.swap(2)
        both.open(0)
        order.flush()
        result = output(by_down, order.free(act), mid, w_down)

        order.phase(factor.got, both.got, gate.got, result)
        factor.swap(0, 1)
        gate.open(1)
        order.flush()
        up_grad, out_grad = both.finish(up_weight.shape[1], output_weight.shape[1])

        order.phase(factor.got, gate.got, up_grad)
        gate.open(0)
        order.flush()
        (fac_grad,) = factor.finish(shard_rows)

        order.phase(gate.got, fac_grad)
        (gate_grad,) = gate.finish(gate_weight.shape[1])
    return (
        result[None],
        input_grad[None],
        fac_grad[cols],
        fac_grad[:cols].T,
        out_grad,
        fac_grad[cols + 1],
        gate_grad,
        up_grad,
        down_grad,
    )


def solution(mesh):
    in_specs = (
        P("rep", "grp", None),
        P("rep", None),
        P("grp"),
        P("grp", None),
        P("grp", None),
        P("grp"),
        P("grp", None),
        P("grp", None),
        P("grp", None),
        P("rep", "grp", None),
    )
    out_specs = (
        P("rep", "grp", None),
        P("rep", "grp", None),
        P("grp"),
        P("grp", None),
        P("grp", None),
        P("grp"),
        P("grp", None),
        P("grp", None),
        P("grp", None),
    )
    return jax.shard_map(local, mesh=mesh, in_specs=in_specs, out_specs=out_specs, check_vma=False)
```

```python
import functools

import jax
import jax.numpy as jnp
import numpy as np
from jax import lax
from jax.experimental import pallas as pl
from jax.experimental.pallas import tpu as pltpu
from jax.sharding import PartitionSpec as P

HEADS = 16
HDIM = 64
QRANK = 6
KRANK = 2
HALF = HDIM // 2
QCOLS = QRANK * HEADS + QRANK * HDIM
KVCOLS = 2 * (KRANK * HEADS + KRANK * HDIM)
AQ, BQ = 0, QRANK * HEADS
AK, BK = 0, KRANK * HEADS
AV = BK + KRANK * HDIM
BV = AV + KRANK * HEADS
SCALE = HDIM**-0.5
EXP_SCALE = SCALE * float(np.log2(np.e))
NEG = -1e30
DEPTH = 128
EPS = 1e-05
VMEM_LIMIT = 60 * 2**20

f32 = jnp.float32
bf16 = jnp.bfloat16
NN = (((1,), (0,)), ((), ()))
NT = (((1,), (1,)), ((), ()))
TN = (((0,), (0,)), ((), ()))


def mm(left, right, dims=NN):
    return lax.dot_general(left, right, dims, preferred_element_type=f32)


def vmem():
    return pl.BlockSpec(memory_space=pltpu.VMEM)


def smem():
    return pl.BlockSpec(memory_space=pltpu.SMEM)


def params():
    return pltpu.CompilerParams(vmem_limit_bytes=VMEM_LIMIT)


def cost(flops, nbytes):
    return pl.CostEstimate(flops=int(flops) // 10**5, bytes_accessed=int(nbytes) // 10**5, transcendentals=0)


def weighty(micros):
    return pl.CostEstimate(flops=int(micros * 1.1e9), bytes_accessed=0, transcendentals=0)


def turn(part, cosine, sine):
    first, second = part[:HALF], part[HALF:]
    return first * cosine - second * sine, second * cosine + first * sine


def front_kernel(count, offs, x_ref, cos_ref, sin_ref, *refs):
    pieces, gain_refs = refs[:count], refs[count : 2 * count]
    fac_ref, kv_ref, hid_ref, gains_ref, w, sems = refs[2 * count :]
    w_in = Mover(sems).columns(offs, pieces, w)
    for i, ref in enumerate(gain_refs):
        size = ref.shape[1]
        at = offs[2 * i] if size % 128 == 0 else 0
        gains_ref[0:2, pl.ds(pl.multiple_of(at, 128), size)] = ref[...].astype(f32)
    xf = x_ref[...].astype(f32)
    normed = xf * lax.rsqrt(jnp.mean(xf * xf, axis=-1, keepdims=True) + EPS)
    hidden = (normed * gains_ref[0:1, :]).astype(bf16)
    turned = jnp.transpose(hidden)
    hid_ref[...] = turned
    wait(w_in)
    raw = mm(w[...], turned)
    cosine, sine = cos_ref[...], sin_ref[...]
    fac_ref[...] = raw[:QCOLS].astype(bf16)
    kv_ref[...] = raw[QCOLS:].astype(bf16)
    for ref, first, at in [(fac_ref, 0, BQ + r * HDIM) for r in range(QRANK)] + [
        (kv_ref, QCOLS, BK + r * HDIM) for r in range(KRANK)
    ]:
        one, two = turn(raw[first + at : first + at + HDIM], cosine, sine)
        ref[at : at + HALF, :] = one.astype(bf16)
        ref[at + HALF : at + HDIM, :] = two.astype(bf16)


def front(offs, x, cosine, sine, w_fac, gains):
    rows, width = x.shape
    cols = w_fac[0].shape[0]
    count = len(w_fac)
    return pl.pallas_call(
        functools.partial(front_kernel, count),
        out_shape=[
            like(QCOLS, rows),
            like(cols - QCOLS, rows),
            like(width, rows),
            like(8, width, dtype=f32),
        ],
        in_specs=[smem()] + [vmem()] * 3 + [anywhere()] * count + [vmem()] * count,
        out_specs=[vmem()] * 4,
        scratch_shapes=[scratch(cols, width), pltpu.SemaphoreType.DMA((count,))],
        compiler_params=params(),
        cost_estimate=cost(2 * rows * width * cols, 4 * width * (cols + rows)),
        name="front",
    )(offs, x, cosine, sine, *w_fac, *gains)


def load_factors(fac_ref, kv_refs, facf, kvf, qT, me):
    facf[...] = fac_ref[...].astype(f32)
    if len(kv_refs) == 1:

        def load(j, _):
            kvf[j] = kv_refs[0][j].astype(f32)
            return 0

        lax.fori_loop(0, kvf.shape[0], load, 0)
    else:
        for flip, ref in enumerate(kv_refs):
            kvf[me ^ flip] = ref[...].astype(f32)
    row = lax.broadcasted_iota(jnp.int32, (DEPTH - HDIM, qT.shape[1]), 0)
    qT[HDIM:DEPTH, :] = jnp.where(row == 0, 1.0, 0.0).astype(bf16)


def build_query(facf, qT, h):
    total = facf[pl.ds(AQ + h, 1), :] * facf[BQ : BQ + HDIM, :]
    for r in range(1, QRANK):
        total += facf[pl.ds(AQ + r * HEADS + h, 1), :] * facf[BQ + r * HDIM : BQ + (r + 1) * HDIM, :]
    qT[0:HDIM, :] = (total * (1.0 / QRANK)).astype(bf16)


def build_pair(kvf, j, h, a_at, b_at):
    total = kvf[j, pl.ds(a_at + h, 1), :] * kvf[j, b_at : b_at + HDIM, :]
    for r in range(1, KRANK):
        total += (
            kvf[j, pl.ds(a_at + r * HEADS + h, 1), :]
            * kvf[j, b_at + r * HDIM : b_at + (r + 1) * HDIM, :]
        )
    return (total * (1.0 / KRANK)).astype(bf16)


def build_key(kvf, kT, j, h, limit):
    span = kT.shape[1]
    kT[0:HDIM, :] = build_pair(kvf, j, h, AK, BK)
    if limit is None:
        kT[HDIM:DEPTH, :] = jnp.zeros((DEPTH - HDIM, span), bf16)
    else:
        row = lax.broadcasted_iota(jnp.int32, (DEPTH - HDIM, span), 0)
        key = j * span + lax.broadcasted_iota(jnp.int32, (DEPTH - HDIM, span), 1)
        kT[HDIM:DEPTH, :] = jnp.where((row == 0) & (key >= limit), NEG, 0.0).astype(bf16)


def causal(scores):
    key = lax.broadcasted_iota(jnp.int32, scores.shape, 0)
    query = lax.broadcasted_iota(jnp.int32, scores.shape, 1)
    return jnp.where(key <= query, scores, NEG)


def attend_kernel(first, heads, count, info_ref, fac_ref, *refs):
    kv_refs, (out_ref, lse_ref, facf, kvf, qT, kT, s_ref) = refs[:count], refs[count:]
    me, npc, limit = info_ref[0], info_ref[1], info_ref[2]
    rows = fac_ref.shape[1]
    load_factors(fac_ref, kv_refs, facf, kvf, qT, me)

    def head(step, _):
        h = first + step
        build_query(facf, qT, h)

        def chunk(j, top):
            build_key(kvf, kT, j, h, limit)
            scores = mm(kT[...], qT[...], TN)
            s_ref[j] = scores
            return jnp.maximum(top, jnp.max(scores, axis=0, keepdims=True))

        top = lax.fori_loop(0, npc, chunk, jnp.full((1, rows), NEG, f32))
        build_key(kvf, kT, me, h, None)
        scores = causal(mm(kT[...], qT[...], TN))
        s_ref[npc] = scores
        top = jnp.maximum(top, jnp.max(scores, axis=0, keepdims=True)) * EXP_SCALE

        def weigh(j, mass):
            probs = jnp.exp2(s_ref[j] * EXP_SCALE - top)
            s_ref[j] = probs
            return mass + jnp.sum(probs, axis=0, keepdims=True)

        mass = lax.fori_loop(0, npc + 1, weigh, jnp.zeros((1, rows), f32))
        lse_ref[pl.ds(step, 1), :] = top + jnp.log2(mass)
        share = 1.0 / mass

        def gather(j, total):
            at = jnp.where(j == npc, me, j)
            return total + mm(build_pair(kvf, at, h, AV, BV), (s_ref[j] * share).astype(bf16))

        total = lax.fori_loop(0, npc + 1, gather, jnp.zeros((HDIM, rows), f32))
        out_ref[pl.ds(pl.multiple_of(step * HDIM, HDIM), HDIM), :] = total.astype(bf16)
        return 0

    lax.fori_loop(0, heads, head, 0)


def kv_sizes(kv):
    return kv[0].shape if len(kv) == 1 else (len(kv),) + kv[0].shape


def attend(info, fac, kv, first, heads):
    parts, cols, rows = kv_sizes(kv)
    seen = min(parts, parts // 2 + 1)
    return pl.pallas_call(
        functools.partial(attend_kernel, first, heads, len(kv)),
        out_shape=[
            jax.ShapeDtypeStruct((heads * HDIM, rows), bf16),
            jax.ShapeDtypeStruct((heads, rows), f32),
        ],
        in_specs=[smem(), vmem()] + [vmem()] * len(kv),
        out_specs=[vmem()] * 2,
        scratch_shapes=[
            pltpu.VMEM((QCOLS, rows), f32),
            pltpu.VMEM((parts, cols, rows), f32),
            pltpu.VMEM((DEPTH, rows), bf16),
            pltpu.VMEM((DEPTH, rows), bf16),
            pltpu.VMEM((seen, rows, rows), f32),
        ],
        compiler_params=params(),
        cost_estimate=cost(16 * 2 * heads * 256 * rows * rows * seen, 4 * cols * rows * parts),
        name="attend",
    )(info, fac, *kv)


def attend_back_kernel(
    first, heads, final, count, count_out, blocks, info_ref, fac_ref, grad_ref, *refs
):
    kv_refs, lse_refs, refs = refs[:count], refs[count : count + blocks], refs[count + blocks :]
    if first:
        dq_in, dkv_in, *refs = refs
    dq_ref, *refs = refs
    if final:
        outs, refs = refs[:count_out], refs[count_out:]
        dkvf, *refs = refs
    else:
        dkvf, *refs = refs
    facf, kvf, qT, kTs, p_ref, dp_ref, lse_ref = refs
    for i, ref in enumerate(lse_refs):
        lse_ref[i * ref.shape[0] : (i + 1) * ref.shape[0], :] = ref[...]
    me, npc, limit = info_ref[0], info_ref[1], info_ref[2]
    parts, _, rows = kvf.shape
    load_factors(fac_ref, kv_refs, facf, kvf, qT, me)

    def begin(j, _):
        dkvf[j] = dkv_in[j] if first else jnp.zeros(dkvf.shape[1:], f32)
        return 0

    lax.fori_loop(0, parts, begin, 0)
    dq_ref[...] = dq_in[...] if first else jnp.zeros(dq_ref.shape, f32)

    def head(step, _):
        h = first + step
        build_query(facf, qT, h)
        grad = grad_ref[pl.ds(pl.multiple_of(h * HDIM, HDIM), HDIM), :]
        lse = lse_ref[pl.ds(h, 1), :]

        def probe(slot, at, scores, delta):
            probs = jnp.exp2(scores * EXP_SCALE - lse)
            p_ref[slot] = probs
            prob_grad = mm(build_pair(kvf, at, h, AV, BV), grad, TN)
            dp_ref[slot] = prob_grad
            return delta + jnp.sum(probs * prob_grad, axis=0, keepdims=True)

        def chunk(j, delta):
            build_key(kvf, kTs.at[j], j, h, limit)
            return probe(j, j, mm(kTs[j], qT[...], TN), delta)

        delta = lax.fori_loop(0, npc, chunk, jnp.zeros((1, rows), f32))
        build_key(kvf, kTs.at[npc], me, h, None)
        delta = probe(npc, me, causal(mm(kTs[npc], qT[...], TN)), delta)

        def pull(j, total):
            at = jnp.where(j == npc, me, j)
            probs = p_ref[j]
            score_grad = (probs * (dp_ref[j] - delta)).astype(bf16)
            key_grad = mm(qT[0:HDIM, :], score_grad, NT) * (SCALE / KRANK)
            value_grad = mm(grad, probs.astype(bf16), NT) * (1.0 / KRANK)
            for a_at, b_at, got in ((AK, BK, key_grad), (AV, BV, value_grad)):
                for r in range(KRANK):
                    a_row = pl.ds(a_at + r * HEADS + h, 1)
                    b_rows = slice(b_at + r * HDIM, b_at + (r + 1) * HDIM)
                    dkvf[at, a_row, :] = jnp.sum(got * kvf[at, b_rows, :], axis=0, keepdims=True)
                    dkvf[at, b_rows, :] += got * kvf[at, a_row, :]
            return total + mm(kTs[j, 0:HDIM, :], score_grad)

        query_grad = lax.fori_loop(0, npc + 1, pull, jnp.zeros((HDIM, rows), f32)) * (SCALE / QRANK)
        for r in range(QRANK):
            a_row = pl.ds(AQ + r * HEADS + h, 1)
            b_rows = slice(BQ + r * HDIM, BQ + (r + 1) * HDIM)
            dq_ref[a_row, :] = jnp.sum(query_grad * facf[b_rows, :], axis=0, keepdims=True)
            dq_ref[b_rows, :] += query_grad * facf[a_row, :]
        return 0

    lax.fori_loop(0, heads, head, 0)
    if final:
        for flip in range(parts):
            outs[flip % 2][flip // 2] = dkvf[me ^ flip].astype(bf16)


def attend_back(info, fac, kv, grad, lse, first, heads, so_far, declared=None):
    parts, cols, rows = kv_sizes(kv)
    seen = min(parts, parts // 2 + 1)
    final = first + heads == HEADS
    gathered = [like(parts // 2, cols, rows)] * 2 if final else [like(parts, cols, rows, dtype=f32)]
    return pl.pallas_call(
        functools.partial(
            attend_back_kernel, first, heads, final, len(kv), len(gathered), len(lse)
        ),
        out_shape=[like(QCOLS, rows, dtype=f32)] + gathered,
        in_specs=[smem()] + [vmem()] * (2 + len(kv) + len(lse) + len(so_far)),
        out_specs=[vmem()] * (1 + len(gathered)),
        scratch_shapes=([pltpu.VMEM((parts, cols, rows), f32)] if final else [])
        + [
            pltpu.VMEM((QCOLS, rows), f32),
            pltpu.VMEM((parts, cols, rows), f32),
            pltpu.VMEM((DEPTH, rows), bf16),
            pltpu.VMEM((seen, DEPTH, rows), bf16),
            pltpu.VMEM((seen, rows, rows), f32),
            pltpu.VMEM((seen, rows, rows), f32),
            pltpu.VMEM((HEADS, rows), f32),
        ],
        compiler_params=params(),
        cost_estimate=declared or cost(heads * rows * rows, 8 * cols * rows * parts),
        name="attend_back",
    )(info, fac, grad, *kv, *lse, *so_far)


class Mover:
    def __init__(self, sems):
        self.sems = sems
        self.used = 0

    def start(self, src, dst):
        copy = pltpu.make_async_copy(src, dst, self.sems.at[self.used])
        self.used += 1
        copy.start()
        return copy

    def pieces(self, offsets, refs, dst, first=0):
        copies = []
        for i, piece in enumerate(refs):
            rows, cols = piece.shape
            at = pl.ds(pl.multiple_of(offsets[first + 2 * i], 16), rows)
            if cols == dst.shape[1]:
                where = dst.at[at]
            else:
                where = dst.at[at, pl.ds(pl.multiple_of(offsets[first + 2 * i + 1], 128), cols)]
            copies.append(self.start(piece, where))
        return copies


    def columns(self, offsets, refs, dst):
        copies = []
        for i, piece in enumerate(refs):
            cols = piece.shape[1]
            if cols == dst.shape[1]:
                copies.append(self.start(piece, dst))
            else:
                at = pl.ds(pl.multiple_of(offsets[2 * i], 128), cols)
                copies.append(self.start(piece, dst.at[:, at]))
        return copies


def wait(copies):
    for copy in copies:
        copy.wait()


def anywhere():
    return pl.BlockSpec(memory_space=pl.ANY)


def like(*shape, dtype=bf16):
    return jax.ShapeDtypeStruct(shape, dtype)


def scratch(*shape, dtype=bf16):
    return pltpu.VMEM(shape, dtype)


TILE = 256


def norm_back(grad_hidden, normed, scale, gain):
    grad_normed = grad_hidden * gain
    gain_grad = jnp.sum(grad_hidden * normed, axis=0, keepdims=True)
    mean = jnp.mean(grad_normed * normed, axis=-1, keepdims=True)
    return gain_grad, scale * (grad_normed - normed * mean)


def shard_products(me, left, right, pair, mover, pair_out, base=0):
    copies = []
    count, rows, cols = pair[0].shape
    step = rows if rows <= 352 else rows // 2
    width = cols // 2 if cols % 256 == 0 and cols > 2048 else cols
    for odd in (1, 0):
        for j in range(count):
            row = (me ^ (2 * j + odd)) * rows
            for low in range(0, rows, step):
                lhs = left[pl.ds(pl.multiple_of(row + low, 16), step), :]
                for at in range(0, cols, width):
                    pair[odd][j, low : low + step, at : at + width] = mm(
                        lhs, right[:, base + at : base + at + width]
                    ).astype(bf16)
            copies.append(mover.start(pair[odd].at[j], pair_out[odd].at[j]))
    return copies


def feed_kernel(count, blocks, offs, x_ref, gain_ref, *refs):
    mix_refs, refs = refs[:blocks], refs[blocks:]
    out_pieces, gate_pieces, lift_pieces = (refs[i * count : (i + 1) * count] for i in range(3))
    refs = refs[3 * count :]
    (mid_o, hid_o, act_o, slope_o, lin_o, actT_o) = refs[:6]
    (wo, wg, wu, mid, hid, hidT, act, slope, lin, actT, sems) = refs[6:]
    mover = Mover(sems)
    wo_in = mover.pieces(offs, out_pieces, wo)
    wg_in = mover.pieces(offs, gate_pieces, wg)
    wu_in = mover.pieces(offs, lift_pieces, wu, 2 * count)
    mix = jnp.concatenate([jnp.transpose(ref[...]) for ref in mix_refs], axis=1)
    wait(wo_in)
    middle = x_ref[...].astype(f32) + mm(mix, wo[...])
    mid[...] = middle
    scale = lax.rsqrt(jnp.mean(middle * middle, axis=-1, keepdims=True) + EPS)
    hidden = (middle * scale * gain_ref[...]).astype(bf16)
    hid[...] = hidden
    hidT[...] = jnp.transpose(hidden)
    done = [mover.start(mid, mid_o), mover.start(hidT, hid_o)]
    wait(wg_in)
    wait(wu_in)

    def tile(j, _):
        cols = pl.ds(pl.multiple_of(j * TILE, TILE), TILE)
        gate = mm(hid[...], wg[:, cols])
        up = mm(hid[...], wu[:, cols])
        sig = jax.nn.sigmoid(gate)
        line = gate * sig
        active = (line * up).astype(bf16)
        act[:, cols] = active
        lin[:, cols] = line.astype(bf16)
        slope[:, cols] = (up * sig * (1.0 + gate * (1.0 - sig))).astype(bf16)
        actT[cols, :] = jnp.transpose(active)
        return 0

    lax.fori_loop(0, wg.shape[1] // TILE, tile, 0, unroll=True)
    done += [mover.start(act, act_o), mover.start(lin, lin_o), mover.start(slope, slope_o)]
    done.append(mover.start(actT, actT_o))
    wait(done)


def feed(offs, mix, x, gain, w_out, w_gate, w_up):
    rows, width = x.shape
    inner = w_gate[0].shape[1]
    count = len(w_gate)
    return pl.pallas_call(
        functools.partial(feed_kernel, count, len(mix)),
        out_shape=[
            like(rows, width, dtype=f32),
            like(width, rows),
            like(rows, inner),
            like(rows, inner),
            like(rows, inner),
        ]
        + [like(inner, rows)],
        in_specs=[smem()] + [vmem()] * (2 + len(mix)) + [anywhere()] * (3 * count),
        out_specs=[anywhere()] * 6,
        scratch_shapes=[
            scratch(width, width),
            scratch(width, inner),
            scratch(width, inner),
            scratch(rows, width, dtype=f32),
            scratch(rows, width),
            scratch(width, rows),
            scratch(rows, inner),
            scratch(rows, inner),
            scratch(rows, inner),
            scratch(inner, rows),
            pltpu.SemaphoreType.DMA((3 * count + 6,)),
        ],
        compiler_params=params(),
        cost_estimate=cost(2 * rows * width * (width + 3 * inner), 2 * inner * (3 * width + 3 * rows)),
        name="feed",
    )(offs, x, gain, *mix, *w_out, *w_gate, *w_up)


def slopes_kernel(count, offs, slope_ref, lin_ref, c_ref, *refs):
    pieces, (dg_o, du_o, wd, dg, du, sems) = refs[:count], refs[count:]
    mover = Mover(sems)
    wait(mover.pieces(offs, pieces, wd))

    def tile(j, _):
        cols = pl.ds(pl.multiple_of(j * TILE, 128), TILE)
        grad = mm(c_ref[...], wd[cols, :], NT)
        dg[:, cols] = (grad * slope_ref[:, cols].astype(f32)).astype(bf16)
        du[:, cols] = (grad * lin_ref[:, cols].astype(f32)).astype(bf16)
        return 0

    lax.fori_loop(0, wd.shape[0] // TILE, tile, 0, unroll=True)
    wait([mover.start(dg, dg_o), mover.start(du, du_o)])


def slopes(offs, upstream, w_down, slope, lin):
    rows, width = upstream.shape
    inner = slope.shape[1]
    count = len(w_down)
    return pl.pallas_call(
        functools.partial(slopes_kernel, count),
        out_shape=[like(rows, inner)] * 2,
        in_specs=[smem()] + [vmem()] * 3 + [anywhere()] * count,
        out_specs=[anywhere()] * 2,
        scratch_shapes=[
            scratch(inner, width),
            scratch(rows, inner),
            scratch(rows, inner),
            pltpu.SemaphoreType.DMA((count + 2,)),
        ],
        compiler_params=params(),
        cost_estimate=cost(2 * rows * width * inner, 2 * inner * (width + 4 * rows)),
        name="slopes",
    )(offs, slope, lin, upstream, *w_down)


def products_kernel(cuts, who, left, right, *refs):
    outs, pairs, sems = refs[: 2 * len(cuts)], refs[2 * len(cuts) : -1], refs[-1]
    mover = Mover(sems)
    done, base = [], 0
    for i, cut in enumerate(cuts):
        mine = slice(2 * i, 2 * i + 2)
        done += shard_products(who[0], left, right, pairs[mine], mover, outs[mine], base)
        base += cut
    wait(done)


def products(who, left, right, parts, cuts=None):
    width, rows = left.shape
    cuts = cuts or (right.shape[1],)
    shapes = [(parts // 2, width // parts, cut) for cut in cuts for _ in range(2)]
    return pl.pallas_call(
        functools.partial(products_kernel, cuts),
        out_shape=[like(*shape) for shape in shapes],
        in_specs=[smem()] + [vmem()] * 2,
        out_specs=[anywhere()] * len(shapes),
        scratch_shapes=[scratch(*shape) for shape in shapes]
        + [pltpu.SemaphoreType.DMA((parts * len(cuts),))],
        compiler_params=params(),
        cost_estimate=cost(1, 1),
        name="products",
    )(who, left, right)


def middle_kernel(count, blocks, offs, who, c_ref, gain_ref, *refs):
    out_pieces, gate_pieces, lift_pieces = (refs[i * count : (i + 1) * count] for i in range(3))
    mix_refs, refs = refs[3 * count : 3 * count + blocks], refs[3 * count + blocks :]
    dg_i, du_i, mid_i, dmid_o, fgain, dmix, *refs = refs
    outs, (wg, wu, wo, dg, du, mid, dhid, branch, mix), pair, sems = refs[:2], refs[2:11], refs[11:13], refs[13]
    mover = Mover(sems)
    in_dg = [mover.start(dg_i, dg)]
    in_wg = mover.pieces(offs, gate_pieces, wg)
    in_du = [mover.start(du_i, du)]
    in_wu = mover.pieces(offs, lift_pieces, wu, 2 * count)
    in_mid = [mover.start(mid_i, mid)]
    in_wo = mover.pieces(offs, out_pieces, wo)
    width = wg.shape[0]

    def back(which, j):
        at = pl.ds(pl.multiple_of(j * TILE, TILE), TILE)
        if which == 0:
            dhid[:, at] = mm(dg[...], wg[at, :], NT)
        else:
            dhid[:, at] += mm(du[...], wu[at, :], NT)
        return 0

    wait(in_dg + in_wg)
    lax.fori_loop(0, width // TILE, lambda j, _: back(0, j), 0, unroll=True)
    wait(in_du + in_wu)
    lax.fori_loop(0, width // TILE, lambda j, _: back(1, j), 0, unroll=True)
    wait(in_mid + in_wo)
    middle = mid[...]
    scale = lax.rsqrt(jnp.mean(middle * middle, axis=-1, keepdims=True) + EPS)
    gain_grad, part = norm_back(dhid[...], middle * scale, scale, gain_ref[...])
    fgain[...] = jnp.broadcast_to(gain_grad, fgain.shape)
    total = c_ref[...].astype(f32) + part
    dhid[...] = total
    branch[...] = total.astype(bf16)
    done = [mover.start(dhid, dmid_o)]
    for i, ref in enumerate(mix_refs):
        size = ref.shape[0]
        mix[i * size : (i + 1) * size, :] = ref[...]
    done += shard_products(who[0], mix, branch, pair, mover, outs)
    dmix[...] = mm(wo[...], branch[...], NT).astype(bf16)
    wait(done)


def middle_grads(offs, who, upstream, gain, mix, w_out, w_gate, w_up, dg, du, mid, parts):
    rows, width = upstream.shape
    pair = (parts // 2, width // parts, width)
    inner = dg.shape[1]
    count = len(w_gate)
    return pl.pallas_call(
        functools.partial(middle_kernel, count, len(mix)),
        out_shape=[
            like(rows, width, dtype=f32),
            like(8, width, dtype=f32),
            like(width, rows),
            like(*pair),
            like(*pair),
        ],
        in_specs=[smem()] * 2
        + [vmem()] * 2
        + [anywhere()] * (3 * count)
        + [vmem()] * len(mix)
        + [anywhere()] * 3,
        out_specs=[anywhere()] + [vmem()] * 2 + [anywhere()] * 2,
        scratch_shapes=[
            scratch(width, inner),
            scratch(width, inner),
            scratch(width, width),
            scratch(rows, inner),
            scratch(rows, inner),
            scratch(rows, width, dtype=f32),
            scratch(rows, width, dtype=f32),
            scratch(rows, width),
            scratch(width, rows),
            scratch(*pair),
            scratch(*pair),
            pltpu.SemaphoreType.DMA((3 * count + 4 + parts,)),
        ],
        compiler_params=params(),
        cost_estimate=cost(2 * rows * width * (2 * inner + width), 4 * inner * (width + rows)),
        name="middle_grads",
    )(offs, who, upstream, gain, *w_out, *w_gate, *w_up, *mix, dg, du, mid)


def output_kernel(count, offs, act_ref, mid_ref, *refs):
    pieces, (res, wd, sems) = refs[:count], refs[count:]
    wait(Mover(sems).pieces(offs, pieces, wd))

    def forth(j, _):
        at = pl.ds(pl.multiple_of(j * TILE, TILE), TILE)
        res[:, at] = (mid_ref[:, at] + mm(act_ref[...], wd[:, at])).astype(bf16)
        return 0

    lax.fori_loop(0, wd.shape[1] // TILE, forth, 0, unroll=True)


def output(offs, act, mid, w_down):
    rows, width = mid.shape
    count = len(w_down)
    inner = act.shape[1]
    return pl.pallas_call(
        functools.partial(output_kernel, count),
        out_shape=like(rows, width),
        in_specs=[smem()] + [vmem()] * 2 + [anywhere()] * count,
        out_specs=vmem(),
        scratch_shapes=[scratch(inner, width), pltpu.SemaphoreType.DMA((count,))],
        compiler_params=params(),
        cost_estimate=cost(2 * rows * width * inner, 2 * inner * (width + rows)),
        name="output",
    )(offs, act, mid, *w_down)


def tail_kernel(count, cols, offs, who, dq_ref, own_ref, cos_ref, sin_ref, hid_ref, x_ref, gain_ref, dmid_ref, fgain_ref, *refs):
    pieces = refs[:count]
    grad_ref, *outs = refs[count:]
    *outs, w, raw, gain_cols, sems = outs
    mover = Mover(sems)
    w_in = mover.columns(offs, pieces, w)
    cosine, sine = cos_ref[...], -sin_ref[...]
    raw[0:QCOLS, :] = dq_ref[...].astype(bf16)
    raw[QCOLS:cols, :] = own_ref[...]
    raw[cols:, :] = jnp.zeros((raw.shape[0] - cols, raw.shape[1]), bf16)
    for r in range(QRANK):
        at = BQ + r * HDIM
        one, two = turn(dq_ref[at : at + HDIM, :], cosine, sine)
        raw[at : at + HALF, :] = one.astype(bf16)
        raw[at + HALF : at + HDIM, :] = two.astype(bf16)
    for r in range(KRANK):
        at = BK + r * HDIM
        one, two = turn(own_ref[at : at + HDIM, :].astype(f32), cosine, sine)
        raw[QCOLS + at : QCOLS + at + HALF, :] = one.astype(bf16)
        raw[QCOLS + at + HALF : QCOLS + at + HDIM, :] = two.astype(bf16)
    draw = jnp.transpose(raw[...])
    wait(w_in)
    xf = x_ref[...].astype(f32)
    scale = lax.rsqrt(jnp.mean(xf * xf, axis=-1, keepdims=True) + EPS)
    dhid = mm(draw[:, 0:cols], w[...])
    gain_grad, part = norm_back(dhid, xf * scale, scale, gain_ref[...])
    grad_ref[...] = dmid_ref[...] + part
    line = lax.broadcasted_iota(jnp.int32, (128, gain_grad.shape[1]), 0)
    both = jnp.where(line == 0, gain_grad, jnp.where(line == 1, fgain_ref[0:1, :], 0.0))
    gain_cols[...] = jnp.transpose(both)
    count_out, wide, rows = outs[0].shape
    for flip in range(2 * count_out):
        at = pl.ds(pl.multiple_of((who[0] ^ flip) * rows, 16), rows)
        out = outs[flip % 2]
        out[flip // 2, 0:cols, :] = mm(raw[0:cols, :], hid_ref[at, :], NT).astype(bf16)
        out[flip // 2, cols:wide, :] = jnp.transpose(gain_cols[at, :])[0 : wide - cols].astype(bf16)


def tail(offs, who, dq, own, cosine, sine, hidT, x, gain, dmid, fgain, w_fac, cols, parts):
    rows, width = x.shape
    wide = (cols // 128 + 1) * 128
    count = len(w_fac)
    shard = (parts // 2, wide, width // parts)
    return pl.pallas_call(
        functools.partial(tail_kernel, count, cols),
        out_shape=[like(rows, width, dtype=f32)] + [like(*shard)] * 2,
        in_specs=[smem()] * 2 + [vmem()] * 9 + [anywhere()] * count,
        out_specs=[vmem()] * 3,
        scratch_shapes=[
            scratch(cols, width),
            scratch(wide, rows),
            scratch(width, 128, dtype=f32),
            pltpu.SemaphoreType.DMA((count,)),
        ],
        compiler_params=params(),
        cost_estimate=cost(4 * rows * width * cols, 4 * width * (cols + 3 * rows)),
        name="tail",
    )(offs, who, dq, own, cosine, sine, hidT, x, gain, dmid, fgain, *w_fac)


def partner(values, axis, flip):
    size = lax.axis_size(axis)
    return lax.ppermute(values, axis, [(i, i ^ flip) for i in range(size)])


def after(value, *earlier):
    if not earlier:
        return value
    return lax.optimization_barrier((value, *earlier))[0]


def places(pieces, rows, half):
    me = lax.axis_index("grp")
    at = []
    for flip, which in pieces:
        row = (me ^ flip) * rows
        at += [row if which is None else row + which * half, 0]
    return jnp.stack([jnp.asarray(v, jnp.int32) for v in at])


def total(*terms):
    got = terms[0].astype(f32)
    for term in terms[1:]:
        got = got + term.astype(f32)
    return got.astype(bf16)


def add_pairs_kernel(*refs):
    mine, other = refs[-2:]
    at = 0
    for keep, got in zip(refs[:-2:2], refs[1:-2:2]):
        cols = slice(at, at + keep.shape[2])
        mine[:, cols] = total(keep[0], got[0])
        other[:, cols] = total(keep[1], got[1])
        at += keep.shape[2]


def add_pairs(groups):
    rows = groups[0][0].shape[1]
    wide = sum(keep.shape[2] for keep, _ in groups)
    steps = next(n for n in (4, 2, 1) if n == 1 or (rows % (16 * n) == 0 and rows * wide > 2**19))
    out = pl.BlockSpec((rows // steps, wide), lambda i: (i, 0))
    terms = [term for group in groups for term in group]
    return pl.pallas_call(
        add_pairs_kernel,
        grid=(steps,),
        out_shape=[like(rows, wide)] * 2,
        in_specs=[pl.BlockSpec((2, rows // steps, v.shape[2]), lambda i: (0, i, 0)) for v in terms],
        out_specs=[out] * 2,
        compiler_params=params(),
        cost_estimate=cost(1, 1),
        name="add_pairs",
    )(*terms)


def eighths(value):
    return value.reshape(8, value.shape[0] // 8, value.shape[1])


def halve_body(place, one, two, keep, send):
    for i in range(4):
        at = place[0] ^ ((i >> 1) * place[2]) ^ ((i & 1) * place[3])
        keep[i] = total(one[at], two[at])
        send[i] = total(one[at ^ place[1]], two[at ^ place[1]])


def halve(place, one, two):
    one, two = eighths(one), eighths(two)
    return pl.pallas_call(
        halve_body,
        out_shape=[like(4, *one.shape[1:])] * 2,
        in_specs=[smem()] + [vmem()] * 2,
        out_specs=[vmem()] * 2,
        compiler_params=params(),
        cost_estimate=cost(1, 1),
        name="halve",
    )(place, one, two)


def batch_kernel(tasks, place, *refs):
    ins, outs = refs[: 2 * len(tasks)], list(refs[2 * len(tasks) :])
    for i, (kind, flip) in enumerate(tasks):
        one, two = ins[2 * i : 2 * i + 2]
        out = outs.pop(0)
        if kind == "halve":
            halve_body(place, one, two, out, outs.pop(0))
        elif kind == "split":
            half = out.shape[0]
            out[...] = total(one[:half], two[:half])
            outs.pop(0)[...] = total(one[half:], two[half:])
        elif kind == "pair":
            out[...] = total(one[0], two[0])
            outs.pop(0)[...] = total(one[1], two[1])
        elif kind == "join":
            half = one.shape[0]
            out[:half] = one[...]
            out[half:] = two[...]
        elif flip:
            for k in range(out.shape[0]):
                out[k] = total(one[k], two[k ^ flip])
        else:
            out[...] = total(one[...], two[...])


def batch(place, tasks):
    shapes, counts = [], []
    for kind, _, one, _ in tasks:
        first, rest = one.shape[0], one.shape[1:]
        got = {
            "halve": [(first // 2,) + rest] * 2,
            "split": [(first // 2,) + rest] * 2,
            "pair": [rest] * 2,
            "join": [(2 * first,) + rest],
            "sum": [one.shape],
        }[kind]
        shapes += got
        counts.append(len(got))
    outs = pl.pallas_call(
        functools.partial(batch_kernel, [task[:2] for task in tasks]),
        out_shape=[like(*shape) for shape in shapes],
        in_specs=[smem()] + [vmem()] * (2 * len(tasks)),
        out_specs=[vmem()] * len(shapes),
        compiler_params=params(),
        cost_estimate=cost(1, 1),
        name="batch",
    )(place, *[value for task in tasks for value in task[2:]])
    groups = []
    for count in counts:
        groups.append(outs[:count])
        outs = outs[count:]
    return groups


def finish_kernel(widths, place, near, far, *outs):
    _, rows, wide = near.shape
    for side, value in ((0, near), (1, far)):
        for k in range(4):
            at = place[0] ^ (side * place[1]) ^ ((k >> 1) * place[2]) ^ ((k & 1) * place[3])
            row = pl.ds(pl.multiple_of(at * rows, 8), rows)
            col = 0
            for out, cols in zip(outs, widths):
                out[row, :] = value[k, :, col : col + cols].astype(f32)
                col += cols


def finish(place, near, far, widths):
    rows = near.shape[1]
    return pl.pallas_call(
        functools.partial(finish_kernel, widths),
        out_shape=[like(8 * rows, cols, dtype=f32) for cols in widths],
        in_specs=[smem()] + [vmem()] * 2,
        out_specs=[vmem()] * len(widths),
        compiler_params=params(),
        cost_estimate=cost(1, 1),
        name="finish",
    )(place, near, far)


def scatter_all(keep, send):
    me = lax.axis_index("grp")
    both = jnp.stack([keep, send], axis=1)
    both = both.reshape((-1,) + both.shape[2:])
    both = jnp.take(both, jnp.arange(both.shape[0]) ^ me, axis=0)
    return lax.psum_scatter(both, "grp", scatter_dimension=0, tiled=False)


class Order:
    def __init__(self):
        self.last = None
        self.before = ()
        self.tasks = []

    def add(self, kind, flip, one, two, then):
        self.tasks.append(((kind, flip, self.free(one), two), then))

    def flush(self):
        groups = batch(self.place, [task for task, _ in self.tasks])
        for (_, then), group in zip(self.tasks, groups):
            then(*group)
        self.tasks = []

    def __call__(self, value, *earlier):
        earlier = earlier if self.last is None else earlier + (self.last,)
        return after(value, *earlier) if earlier else value

    def phase(self, *results):
        self.before = results
        self.last = None

    def now(self, value, *earlier):
        last = () if self.last is None else (self.last,)
        return after(value, *self.before, *earlier, *last)

    def free(self, value):
        return after(value, *self.before)

    def ran(self, value):
        self.last = value
        return value


BITS = ((1, 2, 4), (2, 1, 4))


def along(values, step):
    reps, parts = lax.axis_size("rep"), lax.axis_size("grp")
    pairs = [
        (r * parts + g, (r ^ BITS[g % 2][step]) * parts + g)
        for r in range(reps)
        for g in range(parts)
    ]
    return lax.ppermute(values, ("rep", "grp"), pairs)


class Chunk:
    def __init__(self, order, place, *pairs):
        self.order, self.place, self.pairs = order, place, pairs

    def core(self):
        send = [pair[1] if len(self.pairs) > 1 else after(pair[1], *self.order.before) for pair in self.pairs]
        self.got = [partner(value, "grp", 1) for value in send]

    def add_core(self):
        keep = [self.order.now(self.pairs[0][0])] + [pair[0] for pair in self.pairs[1:]]
        self.mine, self.other = add_pairs(list(zip(keep, self.got)))
        self.order.ran(self.other)

    def cross(self):
        self.got = partner(self.order.free(self.other), "grp", 2)

    def go(self, step):
        self.got = along(self.order.free(self.other), step)

    def fold(self, step, start=True, alone=True):
        def then(mine, other):
            self.mine, self.other = mine, other
            if start:
                self.got = along(other, step)

        if step == 0 and not alone:
            self.order.add("halve", 0, eighths(self.mine), eighths(self.got), then)
        elif step == 0:
            then(*halve(self.place, self.order.now(self.mine), self.got))
            self.order.ran(self.other)
        else:
            self.order.add("split", 0, self.mine, self.got, then)

    def pair(self):
        def then(mine, other):
            self.mine = mine
            self.got = partner(other, "grp", 2)

        self.order.add("pair", 0, self.pairs[0][0], self.got[0], then)

    def swap(self, step, flip=0):
        def then(mine):
            self.mine = mine
            self.got = along(mine, step)

        self.order.add("sum", flip, self.mine, self.got, then)

    def open(self, step):
        def then(mine):
            self.mine = mine
            self.got = along(mine, step)

        self.order.add("join", 0, self.mine, self.got, then)

    def finish(self, *widths):
        got = finish(self.place, self.order.now(self.mine), self.got, widths)
        self.order.ran(got[0])
        return got


def local(
    layer_input,
    branch,
    attention_gain,
    factor_weight,
    output_weight,
    feed_gain,
    gate_weight,
    up_weight,
    down_weight,
    cotangent,
):
    rows = layer_input.shape[1]
    parts = lax.axis_size("grp")
    me = lax.axis_index("grp")
    prompt_parts = parts // 2
    follows = me >= prompt_parts
    chosen = branch[0, jnp.maximum(me - prompt_parts, 0)]
    limit = jnp.where(follows, chosen, me * rows)
    npc = (limit + rows - 1) // rows
    position = jnp.where(follows, chosen, me * rows) + jnp.arange(rows, dtype=jnp.int32)
    info = jnp.stack([me, npc, limit]).astype(jnp.int32)
    freqs = 10000.0 ** (-jnp.arange(HALF).astype(f32) / HALF)
    phase = freqs[:, None] * position.astype(f32)[None, :]
    cosine, sine = jnp.cos(phase), jnp.sin(phase)

    x = layer_input[0]
    upstream = cotangent[0]
    shard_rows, cols = factor_weight.shape
    own_gains = jnp.stack([attention_gain, feed_gain])
    factor_turned = factor_weight.T
    gather = lambda value: lax.all_gather(value, "grp", axis=0, tiled=True)

    if parts != 4 or lax.axis_size("rep") != 8:
        whole = jnp.zeros((4,), jnp.int32)
        w_out, w_down = [gather(output_weight)], [gather(down_weight)]
        w_fac = [lax.all_gather(factor_turned, "grp", axis=1, tiled=True)]
        w_gate, w_up = [gather(gate_weight)], [gather(up_weight)]
        all_gains = lax.all_gather(own_gains, "grp", axis=1, tiled=True)
        fac, kv_own, hid_one, gains = front(whole, x, cosine, sine, w_fac, [all_gains])
        kv = [lax.all_gather(kv_own, "grp", axis=0, tiled=False)]
        mixed, lse = ([got] for got in attend(info, fac, kv, 0, HEADS))
        mid, hid_two, act, slope, lin, act_rows = feed(
            whole, mixed, x, gains[1:2], w_out, w_gate, w_up
        )
        down_pair = products(info, act_rows, upstream, parts)
        dgate, dup = slopes(whole, upstream, w_down, slope, lin)
        up_pair = products(info, hid_two, dup, parts)
        dmid, fgain, dmix, *out_pair = middle_grads(
            whole, info, upstream, gains[1:2], mixed, w_out, w_gate, w_up, dgate, dup, mid, parts
        )
        gate_pair = products(info, hid_two, dgate, parts)
        result = output(whole, act, mid, w_down)
        dq, *dkv = attend_back(info, fac, kv, dmix, lse, 0, HEADS, ())
        input_grad, *fac_pair = tail(
            whole, info, dq, scatter_all(*dkv), cosine, sine, hid_one, x, gains[0:1], dmid, fgain,
            w_fac, cols, parts,
        )
        pairs = (fac_pair, out_pair, gate_pair, up_pair, down_pair)
        shards = [scatter_all(*pair) for pair in pairs]
        sums = [lax.psum(shard, "rep").astype(f32) for shard in shards]
        fac_grad, out_grad, gate_grad, up_grad, down_grad = sums
    else:
        order = Order()
        low = lax.axis_index("rep") % 2
        even = (lax.axis_index("rep") // 2) % 2
        take = lambda v, which: lax.dynamic_slice_in_dim(v, which * (v.shape[0] // 2), v.shape[0] // 2, 0)
        quarter = places([(k, None) for k in range(4)], shard_rows, 0)
        halves = lambda v, rows: places(
            [(0, None), (1, None), (2, v), (2, 1 - v), (3, v), (3, 1 - v)], rows, rows // 2
        )
        by_side, by_line = halves(low, shard_rows), halves(even, shard_rows)
        by_down = halves(low, down_weight.shape[0])
        grp = lambda value, flip: partner(order.free(value), "grp", flip)
        rep = lambda value, flip: partner(order.free(value), "rep", flip)
        fac_x = partner(factor_turned, "grp", 2)
        fac_c = partner(factor_turned, "grp", 1)
        gains_x = partner(own_gains, "grp", 2)
        gains_c = partner(own_gains, "grp", 1)
        gate_c = partner(gate_weight, "grp", 1)
        gate_half, up_half = take(gate_weight, low), take(up_weight, even)
        out_half, down_half = take(output_weight, low), take(down_weight, low)
        order.phase(
            fac_x, fac_c, gains_x, gains_c, gate_c, gate_half, up_half, out_half, down_half
        )
        fac_xc = grp(fac_x, 1)
        gains_xc = grp(gains_x, 1)
        gate_x = grp(gate_half, 2)
        up_c = grp(up_weight, 1)
        out_c = grp(output_weight, 1)
        w_fac = [factor_turned, fac_c, fac_x, fac_xc]
        all_gains = [own_gains, gains_c, gains_x, gains_xc]
        fac, kv_own, hid_one, gains = front(
            quarter, order.now(x), cosine, sine, w_fac, all_gains
        )
        kv_x = partner(kv_own, "grp", 2)
        kv_c = partner(kv_own, "grp", 1)
        kv_xc = partner(kv_x, "grp", 1)
        kv = [kv_own, kv_c, kv_x, kv_xc]

        order.phase(gate_x, kv_x, kv_c, kv_xc, up_c, out_c)
        up_x = grp(up_half, 2)
        out_x = grp(out_half, 2)
        gate_y = rep(gate_x, 1)
        gate_xc = grp(gate_x, 1)
        down_c = grp(down_weight, 1)
        part = HEADS // 2
        heads = [attend(info, order.now(fac), kv, 0, part)]

        order.phase(up_x, out_x, gate_y, gate_xc, down_c, heads[0][0])
        down_x = grp(down_half, 2)
        up_z = rep(up_x, 2)
        up_xc = grp(up_x, 1)
        out_y = rep(out_x, 1)
        gate_yc = grp(gate_y, 1)
        heads.append(attend(info, order.now(fac), kv, part, part))
        mixed, lse = ([got[i] for got in heads] for i in range(2))

        order.phase(down_x, up_z, up_xc, out_y, gate_yc, heads[1][0])
        up_zc = grp(up_z, 1)
        out_xc = grp(out_x, 1)
        out_yc = grp(out_y, 1)
        w_out = [output_weight, out_c, out_x, out_y, out_xc, out_yc]
        w_gate = [gate_weight, gate_c, gate_x, gate_y, gate_xc, gate_yc]
        w_up = [up_weight, up_c, up_x, up_z, up_xc, up_zc]
        offs_feed = jnp.concatenate([by_side, by_line])

        order.phase(up_zc, out_xc, out_yc)
        odd = me % 2
        place = jnp.stack([lax.axis_index("rep"), 1 + odd, 2 - odd, jnp.full_like(odd, 4)])
        place = place.astype(jnp.int32)
        order.place = place
        chunk = functools.partial(Chunk, order, place)
        down_y = rep(down_x, 1)
        down_xc = grp(down_x, 1)
        mid, hid_two, act, slope, lin, act_rows = feed(
            offs_feed, mixed, order.now(x), gains[1:2], w_out, w_gate, w_up
        )

        order.phase(down_y, down_xc, mid)
        down_yc = grp(down_y, 1)
        w_down = [down_weight, down_c, down_x, down_y, down_xc, down_yc]
        down = chunk(products(info, order.now(act_rows), upstream, parts))

        order.phase(down_yc, down.pairs[0][0])
        down.core()
        dgate, dup = slopes(by_down, order.now(upstream), w_down, slope, lin)

        order.phase(*down.got, dgate)
        down.add_core()
        down.cross()
        third = 1024
        cuts = (third, third, up_weight.shape[1] - 2 * third)
        terms = products(info, order.free(hid_two), dup, parts, cuts)
        up = chunk(*[terms[i : i + 2] for i in range(0, 6, 2)])
        up.core()
        dmid, fgain, dmix, *out_pair = middle_grads(
            offs_feed, info, order.free(upstream), gains[1:2], mixed, w_out, w_gate, w_up,
            dgate, dup, mid, parts,
        )
        out = chunk(out_pair)
        out.core()
        gate = chunk(products(info, after(hid_two, dmix), dgate, parts))
        part = 1
        state = attend_back(info, fac, kv, after(dmix, gate.pairs[0][0]), lse, 0, part, ())

        order.phase(down.got, *up.got, *out.got, state[0])
        both = chunk(*up.pairs, *out.pairs)
        both.got = up.got + out.got
        both.add_core()
        both.cross()
        down.fold(0)
        gate.core()
        dq, *terms = attend_back(info, fac, kv, order.free(dmix), lse, part, HEADS - part, state)

        order.phase(both.got, down.got, *gate.got, dq)
        dkv = chunk(terms)
        dkv.core()
        down.fold(1)
        order.flush()
        both.fold(0, start=False)

        order.phase(*dkv.got, down.got, both.other)
        both.go(0)
        dkv.pair()
        down.fold(2)
        order.flush()
        gate.add_core()

        order.phase(dkv.got, down.got, gate.other)
        gate.cross()
        sums = []
        order.add("sum", 0, dkv.mine, dkv.got, sums.append)
        down.swap(2)
        order.flush()
        input_grad, *terms = tail(
            quarter, info, dq, sums[0], cosine, sine, hid_one, x, gains[0:1], dmid, fgain,
            w_fac, cols, parts,
        )

        order.phase(both.got, down.got, input_grad)
        factor = chunk(terms)
        factor.core()
        both.fold(1)
        down.open(1)
        order.flush()

        order.phase(*factor.got, both.got, down.got)
        factor.pair()
        both.fold(2)
        down.open(0)
        order.flush()
        gate.got = after(gate.got, factor.mine)
        gate.fold(0)

        order.phase(factor.got, both.got, down.got, gate.got)
        factor.fold(0, alone=False)
        gate.fold(1)
        both.swap(2)
        order.flush()
        (down_grad,) = down.finish(down_weight.shape[1])

        order.phase(factor.got, both.got, gate.got, down_grad)
        factor.swap(1)
        gate.fold(2)
        both.open(1)
        order.flush()

        order.phase(factor.got, both.got, gate.got)
        factor.swap(2, 2)
        gate.swap(2)
        both.open(0)
        order.flush()
        result = output(by_down, order.free(act), mid, w_down)

        order.phase(factor.got, both.got, gate.got, result)
        factor.swap(0, 1)
        gate.open(1)
        order.flush()
        up_grad, out_grad = both.finish(up_weight.shape[1], output_weight.shape[1])

        order.phase(factor.got, gate.got, up_grad)
        gate.open(0)
        order.flush()
        (fac_grad,) = factor.finish(shard_rows)

        order.phase(gate.got, fac_grad)
        (gate_grad,) = gate.finish(gate_weight.shape[1])
    return (
        result[None],
        input_grad[None],
        fac_grad[cols],
        fac_grad[:cols].T,
        out_grad,
        fac_grad[cols + 1],
        gate_grad,
        up_grad,
        down_grad,
    )


def solution(mesh):
    in_specs = (
        P("rep", "grp", None),
        P("rep", None),
        P("grp"),
        P("grp", None),
        P("grp", None),
        P("grp"),
        P("grp", None),
        P("grp", None),
        P("grp", None),
        P("rep", "grp", None),
    )
    out_specs = (
        P("rep", "grp", None),
        P("rep", "grp", None),
        P("grp"),
        P("grp", None),
        P("grp", None),
        P("grp"),
        P("grp", None),
        P("grp", None),
        P("grp", None),
    )
    return jax.shard_map(local, mesh=mesh, in_specs=in_specs, out_specs=out_specs, check_vma=False)
```

```python
import functools

import jax
import jax.numpy as jnp
import numpy as np
from jax import lax
from jax.experimental import pallas as pl
from jax.experimental.pallas import tpu as pltpu
from jax.sharding import PartitionSpec as P

HEADS = 16
HDIM = 64
QRANK = 6
KRANK = 2
HALF = HDIM // 2
QCOLS = QRANK * HEADS + QRANK * HDIM
KVCOLS = 2 * (KRANK * HEADS + KRANK * HDIM)
AQ, BQ = 0, QRANK * HEADS
AK, BK = 0, KRANK * HEADS
AV = BK + KRANK * HDIM
BV = AV + KRANK * HEADS
SCALE = HDIM**-0.5
EXP_SCALE = SCALE * float(np.log2(np.e))
NEG = -1e30
DEPTH = 128
EPS = 1e-05
VMEM_LIMIT = 60 * 2**20

f32 = jnp.float32
bf16 = jnp.bfloat16
NN = (((1,), (0,)), ((), ()))
NT = (((1,), (1,)), ((), ()))
TN = (((0,), (0,)), ((), ()))


def mm(left, right, dims=NN):
    return lax.dot_general(left, right, dims, preferred_element_type=f32)


def vmem():
    return pl.BlockSpec(memory_space=pltpu.VMEM)


def smem():
    return pl.BlockSpec(memory_space=pltpu.SMEM)


def params():
    return pltpu.CompilerParams(vmem_limit_bytes=VMEM_LIMIT)


def cost(flops, nbytes):
    return pl.CostEstimate(flops=int(flops) // 10**5, bytes_accessed=int(nbytes) // 10**5, transcendentals=0)


def weighty(micros):
    return pl.CostEstimate(flops=int(micros * 1.1e9), bytes_accessed=0, transcendentals=0)


def turn(part, cosine, sine):
    first, second = part[:HALF], part[HALF:]
    return first * cosine - second * sine, second * cosine + first * sine


def front_kernel(count, offs, x_ref, cos_ref, sin_ref, *refs):
    pieces, gain_refs = refs[:count], refs[count : 2 * count]
    fac_ref, kv_ref, hid_ref, gains_ref, w, sems = refs[2 * count :]
    w_in = Mover(sems).columns(offs, pieces, w)
    for i, ref in enumerate(gain_refs):
        size = ref.shape[1]
        at = offs[2 * i] if size % 128 == 0 else 0
        gains_ref[0:2, pl.ds(pl.multiple_of(at, 128), size)] = ref[...].astype(f32)
    xf = x_ref[...].astype(f32)
    normed = xf * lax.rsqrt(jnp.mean(xf * xf, axis=-1, keepdims=True) + EPS)
    hidden = (normed * gains_ref[0:1, :]).astype(bf16)
    turned = jnp.transpose(hidden)
    hid_ref[...] = turned
    wait(w_in)
    raw = mm(w[...], turned)
    cosine, sine = cos_ref[...], sin_ref[...]
    fac_ref[...] = raw[:QCOLS].astype(bf16)
    kv_ref[...] = raw[QCOLS:].astype(bf16)
    for ref, first, at in [(fac_ref, 0, BQ + r * HDIM) for r in range(QRANK)] + [
        (kv_ref, QCOLS, BK + r * HDIM) for r in range(KRANK)
    ]:
        one, two = turn(raw[first + at : first + at + HDIM], cosine, sine)
        ref[at : at + HALF, :] = one.astype(bf16)
        ref[at + HALF : at + HDIM, :] = two.astype(bf16)


def front(offs, x, cosine, sine, w_fac, gains):
    rows, width = x.shape
    cols = w_fac[0].shape[0]
    count = len(w_fac)
    return pl.pallas_call(
        functools.partial(front_kernel, count),
        out_shape=[
            like(QCOLS, rows),
            like(cols - QCOLS, rows),
            like(width, rows),
            like(8, width, dtype=f32),
        ],
        in_specs=[smem()] + [vmem()] * 3 + [anywhere()] * count + [vmem()] * count,
        out_specs=[vmem()] * 4,
        scratch_shapes=[scratch(cols, width), pltpu.SemaphoreType.DMA((count,))],
        compiler_params=params(),
        cost_estimate=cost(2 * rows * width * cols, 4 * width * (cols + rows)),
        name="front",
    )(offs, x, cosine, sine, *w_fac, *gains)


def load_factors(fac_ref, kv_refs, facf, kvf, qT, me):
    facf[...] = fac_ref[...].astype(f32)
    if len(kv_refs) == 1:

        def load(j, _):
            kvf[j] = kv_refs[0][j].astype(f32)
            return 0

        lax.fori_loop(0, kvf.shape[0], load, 0)
    else:
        for flip, ref in enumerate(kv_refs):
            kvf[me ^ flip] = ref[...].astype(f32)
    row = lax.broadcasted_iota(jnp.int32, (DEPTH - HDIM, qT.shape[1]), 0)
    qT[HDIM:DEPTH, :] = jnp.where(row == 0, 1.0, 0.0).astype(bf16)


def build_query(facf, qT, h):
    total = facf[pl.ds(AQ + h, 1), :] * facf[BQ : BQ + HDIM, :]
    for r in range(1, QRANK):
        total += facf[pl.ds(AQ + r * HEADS + h, 1), :] * facf[BQ + r * HDIM : BQ + (r + 1) * HDIM, :]
    qT[0:HDIM, :] = (total * (1.0 / QRANK)).astype(bf16)


def build_pair(kvf, j, h, a_at, b_at):
    total = kvf[j, pl.ds(a_at + h, 1), :] * kvf[j, b_at : b_at + HDIM, :]
    for r in range(1, KRANK):
        total += (
            kvf[j, pl.ds(a_at + r * HEADS + h, 1), :]
            * kvf[j, b_at + r * HDIM : b_at + (r + 1) * HDIM, :]
        )
    return (total * (1.0 / KRANK)).astype(bf16)


def build_key(kvf, kT, j, h, limit):
    span = kT.shape[1]
    kT[0:HDIM, :] = build_pair(kvf, j, h, AK, BK)
    if limit is None:
        kT[HDIM:DEPTH, :] = jnp.zeros((DEPTH - HDIM, span), bf16)
    else:
        row = lax.broadcasted_iota(jnp.int32, (DEPTH - HDIM, span), 0)
        key = j * span + lax.broadcasted_iota(jnp.int32, (DEPTH - HDIM, span), 1)
        kT[HDIM:DEPTH, :] = jnp.where((row == 0) & (key >= limit), NEG, 0.0).astype(bf16)


def causal(scores):
    key = lax.broadcasted_iota(jnp.int32, scores.shape, 0)
    query = lax.broadcasted_iota(jnp.int32, scores.shape, 1)
    return jnp.where(key <= query, scores, NEG)


def attend_kernel(first, heads, count, info_ref, fac_ref, *refs):
    kv_refs, (out_ref, lse_ref, facf, kvf, qT, kT, s_ref) = refs[:count], refs[count:]
    me, npc, limit = info_ref[0], info_ref[1], info_ref[2]
    rows = fac_ref.shape[1]
    load_factors(fac_ref, kv_refs, facf, kvf, qT, me)

    def head(step, _):
        h = first + step
        build_query(facf, qT, h)

        def chunk(j, top):
            build_key(kvf, kT, j, h, limit)
            scores = mm(kT[...], qT[...], TN)
            s_ref[j] = scores
            return jnp.maximum(top, jnp.max(scores, axis=0, keepdims=True))

        top = lax.fori_loop(0, npc, chunk, jnp.full((1, rows), NEG, f32))
        build_key(kvf, kT, me, h, None)
        scores = causal(mm(kT[...], qT[...], TN))
        s_ref[npc] = scores
        top = jnp.maximum(top, jnp.max(scores, axis=0, keepdims=True)) * EXP_SCALE

        def weigh(j, mass):
            probs = jnp.exp2(s_ref[j] * EXP_SCALE - top)
            s_ref[j] = probs
            return mass + jnp.sum(probs, axis=0, keepdims=True)

        mass = lax.fori_loop(0, npc + 1, weigh, jnp.zeros((1, rows), f32))
        lse_ref[pl.ds(step, 1), :] = top + jnp.log2(mass)
        share = 1.0 / mass

        def gather(j, total):
            at = jnp.where(j == npc, me, j)
            return total + mm(build_pair(kvf, at, h, AV, BV), (s_ref[j] * share).astype(bf16))

        total = lax.fori_loop(0, npc + 1, gather, jnp.zeros((HDIM, rows), f32))
        out_ref[pl.ds(pl.multiple_of(step * HDIM, HDIM), HDIM), :] = total.astype(bf16)
        return 0

    lax.fori_loop(0, heads, head, 0)


def kv_sizes(kv):
    return kv[0].shape if len(kv) == 1 else (len(kv),) + kv[0].shape


def attend(info, fac, kv, first, heads):
    parts, cols, rows = kv_sizes(kv)
    seen = min(parts, parts // 2 + 1)
    return pl.pallas_call(
        functools.partial(attend_kernel, first, heads, len(kv)),
        out_shape=[
            jax.ShapeDtypeStruct((heads * HDIM, rows), bf16),
            jax.ShapeDtypeStruct((heads, rows), f32),
        ],
        in_specs=[smem(), vmem()] + [vmem()] * len(kv),
        out_specs=[vmem()] * 2,
        scratch_shapes=[
            pltpu.VMEM((QCOLS, rows), f32),
            pltpu.VMEM((parts, cols, rows), f32),
            pltpu.VMEM((DEPTH, rows), bf16),
            pltpu.VMEM((DEPTH, rows), bf16),
            pltpu.VMEM((seen, rows, rows), f32),
        ],
        compiler_params=params(),
        cost_estimate=cost(16 * 2 * heads * 256 * rows * rows * seen, 4 * cols * rows * parts),
        name="attend",
    )(info, fac, *kv)


def attend_back_kernel(
    first, heads, final, count, count_out, blocks, info_ref, fac_ref, grad_ref, *refs
):
    kv_refs, lse_refs, refs = refs[:count], refs[count : count + blocks], refs[count + blocks :]
    if first:
        dq_in, dkv_in, *refs = refs
    dq_ref, *refs = refs
    if final:
        outs, refs = refs[:count_out], refs[count_out:]
        dkvf, *refs = refs
    else:
        dkvf, *refs = refs
    facf, kvf, qT, kTs, p_ref, dp_ref, lse_ref = refs
    for i, ref in enumerate(lse_refs):
        lse_ref[i * ref.shape[0] : (i + 1) * ref.shape[0], :] = ref[...]
    me, npc, limit = info_ref[0], info_ref[1], info_ref[2]
    parts, _, rows = kvf.shape
    load_factors(fac_ref, kv_refs, facf, kvf, qT, me)

    def begin(j, _):
        dkvf[j] = dkv_in[j] if first else jnp.zeros(dkvf.shape[1:], f32)
        return 0

    lax.fori_loop(0, parts, begin, 0)
    dq_ref[...] = dq_in[...] if first else jnp.zeros(dq_ref.shape, f32)

    def head(step, _):
        h = first + step
        build_query(facf, qT, h)
        grad = grad_ref[pl.ds(pl.multiple_of(h * HDIM, HDIM), HDIM), :]
        lse = lse_ref[pl.ds(h, 1), :]

        def probe(slot, at, scores, delta):
            probs = jnp.exp2(scores * EXP_SCALE - lse)
            p_ref[slot] = probs
            prob_grad = mm(build_pair(kvf, at, h, AV, BV), grad, TN)
            dp_ref[slot] = prob_grad
            return delta + jnp.sum(probs * prob_grad, axis=0, keepdims=True)

        def chunk(j, delta):
            build_key(kvf, kTs.at[j], j, h, limit)
            return probe(j, j, mm(kTs[j], qT[...], TN), delta)

        delta = lax.fori_loop(0, npc, chunk, jnp.zeros((1, rows), f32))
        build_key(kvf, kTs.at[npc], me, h, None)
        delta = probe(npc, me, causal(mm(kTs[npc], qT[...], TN)), delta)

        def pull(j, total):
            at = jnp.where(j == npc, me, j)
            probs = p_ref[j]
            score_grad = (probs * (dp_ref[j] - delta)).astype(bf16)
            key_grad = mm(qT[0:HDIM, :], score_grad, NT) * (SCALE / KRANK)
            value_grad = mm(grad, probs.astype(bf16), NT) * (1.0 / KRANK)
            for a_at, b_at, got in ((AK, BK, key_grad), (AV, BV, value_grad)):
                for r in range(KRANK):
                    a_row = pl.ds(a_at + r * HEADS + h, 1)
                    b_rows = slice(b_at + r * HDIM, b_at + (r + 1) * HDIM)
                    dkvf[at, a_row, :] = jnp.sum(got * kvf[at, b_rows, :], axis=0, keepdims=True)
                    dkvf[at, b_rows, :] += got * kvf[at, a_row, :]
            return total + mm(kTs[j, 0:HDIM, :], score_grad)

        query_grad = lax.fori_loop(0, npc + 1, pull, jnp.zeros((HDIM, rows), f32)) * (SCALE / QRANK)
        for r in range(QRANK):
            a_row = pl.ds(AQ + r * HEADS + h, 1)
            b_rows = slice(BQ + r * HDIM, BQ + (r + 1) * HDIM)
            dq_ref[a_row, :] = jnp.sum(query_grad * facf[b_rows, :], axis=0, keepdims=True)
            dq_ref[b_rows, :] += query_grad * facf[a_row, :]
        return 0

    lax.fori_loop(0, heads, head, 0)
    if final:
        for flip in range(parts):
            outs[flip % 2][flip // 2] = dkvf[me ^ flip].astype(bf16)


def attend_back(info, fac, kv, grad, lse, first, heads, so_far, declared=None):
    parts, cols, rows = kv_sizes(kv)
    seen = min(parts, parts // 2 + 1)
    final = first + heads == HEADS
    gathered = [like(parts // 2, cols, rows)] * 2 if final else [like(parts, cols, rows, dtype=f32)]
    return pl.pallas_call(
        functools.partial(
            attend_back_kernel, first, heads, final, len(kv), len(gathered), len(lse)
        ),
        out_shape=[like(QCOLS, rows, dtype=f32)] + gathered,
        in_specs=[smem()] + [vmem()] * (2 + len(kv) + len(lse) + len(so_far)),
        out_specs=[vmem()] * (1 + len(gathered)),
        scratch_shapes=([pltpu.VMEM((parts, cols, rows), f32)] if final else [])
        + [
            pltpu.VMEM((QCOLS, rows), f32),
            pltpu.VMEM((parts, cols, rows), f32),
            pltpu.VMEM((DEPTH, rows), bf16),
            pltpu.VMEM((seen, DEPTH, rows), bf16),
            pltpu.VMEM((seen, rows, rows), f32),
            pltpu.VMEM((seen, rows, rows), f32),
            pltpu.VMEM((HEADS, rows), f32),
        ],
        compiler_params=params(),
        cost_estimate=declared or cost(heads * rows * rows, 8 * cols * rows * parts),
        name="attend_back",
    )(info, fac, grad, *kv, *lse, *so_far)


class Mover:
    def __init__(self, sems):
        self.sems = sems
        self.used = 0

    def start(self, src, dst):
        copy = pltpu.make_async_copy(src, dst, self.sems.at[self.used])
        self.used += 1
        copy.start()
        return copy

    def pieces(self, offsets, refs, dst, first=0):
        copies = []
        for i, piece in enumerate(refs):
            rows, cols = piece.shape
            at = pl.ds(pl.multiple_of(offsets[first + 2 * i], 16), rows)
            if cols == dst.shape[1]:
                where = dst.at[at]
            else:
                where = dst.at[at, pl.ds(pl.multiple_of(offsets[first + 2 * i + 1], 128), cols)]
            copies.append(self.start(piece, where))
        return copies


    def columns(self, offsets, refs, dst):
        copies = []
        for i, piece in enumerate(refs):
            cols = piece.shape[1]
            if cols == dst.shape[1]:
                copies.append(self.start(piece, dst))
            else:
                at = pl.ds(pl.multiple_of(offsets[2 * i], 128), cols)
                copies.append(self.start(piece, dst.at[:, at]))
        return copies


def wait(copies):
    for copy in copies:
        copy.wait()


def anywhere():
    return pl.BlockSpec(memory_space=pl.ANY)


def like(*shape, dtype=bf16):
    return jax.ShapeDtypeStruct(shape, dtype)


def scratch(*shape, dtype=bf16):
    return pltpu.VMEM(shape, dtype)


TILE = 256


def norm_back(grad_hidden, normed, scale, gain):
    grad_normed = grad_hidden * gain
    gain_grad = jnp.sum(grad_hidden * normed, axis=0, keepdims=True)
    mean = jnp.mean(grad_normed * normed, axis=-1, keepdims=True)
    return gain_grad, scale * (grad_normed - normed * mean)


def shard_products(me, left, right, pair, mover, pair_out, base=0):
    copies = []
    count, rows, cols = pair[0].shape
    step = rows if rows <= 352 else rows // 2
    width = cols // 2 if cols % 256 == 0 and cols > 2048 else cols
    for odd in (1, 0):
        for j in range(count):
            row = (me ^ (2 * j + odd)) * rows
            for low in range(0, rows, step):
                lhs = left[pl.ds(pl.multiple_of(row + low, 16), step), :]
                for at in range(0, cols, width):
                    pair[odd][j, low : low + step, at : at + width] = mm(
                        lhs, right[:, base + at : base + at + width]
                    ).astype(bf16)
            copies.append(mover.start(pair[odd].at[j], pair_out[odd].at[j]))
    return copies


def feed_kernel(count, blocks, offs, x_ref, gain_ref, *refs):
    mix_refs, refs = refs[:blocks], refs[blocks:]
    out_pieces, gate_pieces, lift_pieces = (refs[i * count : (i + 1) * count] for i in range(3))
    refs = refs[3 * count :]
    (mid_o, hid_o, act_o, slope_o, lin_o, actT_o) = refs[:6]
    (wo, wg, wu, mid, hid, hidT, act, slope, lin, actT, sems) = refs[6:]
    mover = Mover(sems)
    wo_in = mover.pieces(offs, out_pieces, wo)
    wg_in = mover.pieces(offs, gate_pieces, wg)
    wu_in = mover.pieces(offs, lift_pieces, wu, 2 * count)
    mix = jnp.concatenate([jnp.transpose(ref[...]) for ref in mix_refs], axis=1)
    wait(wo_in)
    middle = x_ref[...].astype(f32) + mm(mix, wo[...])
    mid[...] = middle
    scale = lax.rsqrt(jnp.mean(middle * middle, axis=-1, keepdims=True) + EPS)
    hidden = (middle * scale * gain_ref[...]).astype(bf16)
    hid[...] = hidden
    hidT[...] = jnp.transpose(hidden)
    done = [mover.start(mid, mid_o), mover.start(hidT, hid_o)]
    wait(wg_in)
    wait(wu_in)

    def tile(j, _):
        cols = pl.ds(pl.multiple_of(j * TILE, TILE), TILE)
        gate = mm(hid[...], wg[:, cols])
        up = mm(hid[...], wu[:, cols])
        sig = jax.nn.sigmoid(gate)
        line = gate * sig
        active = (line * up).astype(bf16)
        act[:, cols] = active
        lin[:, cols] = line.astype(bf16)
        slope[:, cols] = (up * sig * (1.0 + gate * (1.0 - sig))).astype(bf16)
        actT[cols, :] = jnp.transpose(active)
        return 0

    lax.fori_loop(0, wg.shape[1] // TILE, tile, 0, unroll=True)
    done += [mover.start(act, act_o), mover.start(lin, lin_o), mover.start(slope, slope_o)]
    done.append(mover.start(actT, actT_o))
    wait(done)


def feed(offs, mix, x, gain, w_out, w_gate, w_up):
    rows, width = x.shape
    inner = w_gate[0].shape[1]
    count = len(w_gate)
    return pl.pallas_call(
        functools.partial(feed_kernel, count, len(mix)),
        out_shape=[
            like(rows, width, dtype=f32),
            like(width, rows),
            like(rows, inner),
            like(rows, inner),
            like(rows, inner),
        ]
        + [like(inner, rows)],
        in_specs=[smem()] + [vmem()] * (2 + len(mix)) + [anywhere()] * (3 * count),
        out_specs=[anywhere()] * 6,
        scratch_shapes=[
            scratch(width, width),
            scratch(width, inner),
            scratch(width, inner),
            scratch(rows, width, dtype=f32),
            scratch(rows, width),
            scratch(width, rows),
            scratch(rows, inner),
            scratch(rows, inner),
            scratch(rows, inner),
            scratch(inner, rows),
            pltpu.SemaphoreType.DMA((3 * count + 6,)),
        ],
        compiler_params=params(),
        cost_estimate=cost(2 * rows * width * (width + 3 * inner), 2 * inner * (3 * width + 3 * rows)),
        name="feed",
    )(offs, x, gain, *mix, *w_out, *w_gate, *w_up)


def slopes_kernel(count, offs, slope_ref, lin_ref, c_ref, *refs):
    pieces, (dg_o, du_o, wd, dg, du, sems) = refs[:count], refs[count:]
    mover = Mover(sems)
    wait(mover.pieces(offs, pieces, wd))

    def tile(j, _):
        cols = pl.ds(pl.multiple_of(j * TILE, 128), TILE)
        grad = mm(c_ref[...], wd[cols, :], NT)
        dg[:, cols] = (grad * slope_ref[:, cols].astype(f32)).astype(bf16)
        du[:, cols] = (grad * lin_ref[:, cols].astype(f32)).astype(bf16)
        return 0

    lax.fori_loop(0, wd.shape[0] // TILE, tile, 0, unroll=True)
    wait([mover.start(dg, dg_o), mover.start(du, du_o)])


def slopes(offs, upstream, w_down, slope, lin):
    rows, width = upstream.shape
    inner = slope.shape[1]
    count = len(w_down)
    return pl.pallas_call(
        functools.partial(slopes_kernel, count),
        out_shape=[like(rows, inner)] * 2,
        in_specs=[smem()] + [vmem()] * 3 + [anywhere()] * count,
        out_specs=[anywhere()] * 2,
        scratch_shapes=[
            scratch(inner, width),
            scratch(rows, inner),
            scratch(rows, inner),
            pltpu.SemaphoreType.DMA((count + 2,)),
        ],
        compiler_params=params(),
        cost_estimate=cost(2 * rows * width * inner, 2 * inner * (width + 4 * rows)),
        name="slopes",
    )(offs, slope, lin, upstream, *w_down)


def products_kernel(cuts, who, left, right, *refs):
    outs, pairs, sems = refs[: 2 * len(cuts)], refs[2 * len(cuts) : -1], refs[-1]
    mover = Mover(sems)
    done, base = [], 0
    for i, cut in enumerate(cuts):
        mine = slice(2 * i, 2 * i + 2)
        done += shard_products(who[0], left, right, pairs[mine], mover, outs[mine], base)
        base += cut
    wait(done)


def products(who, left, right, parts, cuts=None):
    width, rows = left.shape
    cuts = cuts or (right.shape[1],)
    shapes = [(parts // 2, width // parts, cut) for cut in cuts for _ in range(2)]
    return pl.pallas_call(
        functools.partial(products_kernel, cuts),
        out_shape=[like(*shape) for shape in shapes],
        in_specs=[smem()] + [vmem()] * 2,
        out_specs=[anywhere()] * len(shapes),
        scratch_shapes=[scratch(*shape) for shape in shapes]
        + [pltpu.SemaphoreType.DMA((parts * len(cuts),))],
        compiler_params=params(),
        cost_estimate=cost(1, 1),
        name="products",
    )(who, left, right)


def middle_kernel(count, blocks, offs, who, c_ref, gain_ref, *refs):
    out_pieces, gate_pieces, lift_pieces = (refs[i * count : (i + 1) * count] for i in range(3))
    mix_refs, refs = refs[3 * count : 3 * count + blocks], refs[3 * count + blocks :]
    dg_i, du_i, mid_i, dmid_o, fgain, dmix, *refs = refs
    outs, (wg, wu, wo, dg, du, mid, dhid, branch, mix), pair, sems = refs[:2], refs[2:11], refs[11:13], refs[13]
    mover = Mover(sems)
    in_dg = [mover.start(dg_i, dg)]
    in_wg = mover.pieces(offs, gate_pieces, wg)
    in_du = [mover.start(du_i, du)]
    in_wu = mover.pieces(offs, lift_pieces, wu, 2 * count)
    in_mid = [mover.start(mid_i, mid)]
    in_wo = mover.pieces(offs, out_pieces, wo)
    width = wg.shape[0]

    def back(which, j):
        at = pl.ds(pl.multiple_of(j * TILE, TILE), TILE)
        if which == 0:
            dhid[:, at] = mm(dg[...], wg[at, :], NT)
        else:
            dhid[:, at] += mm(du[...], wu[at, :], NT)
        return 0

    wait(in_dg + in_wg)
    lax.fori_loop(0, width // TILE, lambda j, _: back(0, j), 0, unroll=True)
    wait(in_du + in_wu)
    lax.fori_loop(0, width // TILE, lambda j, _: back(1, j), 0, unroll=True)
    wait(in_mid + in_wo)
    middle = mid[...]
    scale = lax.rsqrt(jnp.mean(middle * middle, axis=-1, keepdims=True) + EPS)
    gain_grad, part = norm_back(dhid[...], middle * scale, scale, gain_ref[...])
    fgain[...] = jnp.broadcast_to(gain_grad, fgain.shape)
    total = c_ref[...].astype(f32) + part
    dhid[...] = total
    branch[...] = total.astype(bf16)
    done = [mover.start(dhid, dmid_o)]
    for i, ref in enumerate(mix_refs):
        size = ref.shape[0]
        mix[i * size : (i + 1) * size, :] = ref[...]
    done += shard_products(who[0], mix, branch, pair, mover, outs)
    dmix[...] = mm(wo[...], branch[...], NT).astype(bf16)
    wait(done)


def middle_grads(offs, who, upstream, gain, mix, w_out, w_gate, w_up, dg, du, mid, parts):
    rows, width = upstream.shape
    pair = (parts // 2, width // parts, width)
    inner = dg.shape[1]
    count = len(w_gate)
    return pl.pallas_call(
        functools.partial(middle_kernel, count, len(mix)),
        out_shape=[
            like(rows, width, dtype=f32),
            like(8, width, dtype=f32),
            like(width, rows),
            like(*pair),
            like(*pair),
        ],
        in_specs=[smem()] * 2
        + [vmem()] * 2
        + [anywhere()] * (3 * count)
        + [vmem()] * len(mix)
        + [anywhere()] * 3,
        out_specs=[anywhere()] + [vmem()] * 2 + [anywhere()] * 2,
        scratch_shapes=[
            scratch(width, inner),
            scratch(width, inner),
            scratch(width, width),
            scratch(rows, inner),
            scratch(rows, inner),
            scratch(rows, width, dtype=f32),
            scratch(rows, width, dtype=f32),
            scratch(rows, width),
            scratch(width, rows),
            scratch(*pair),
            scratch(*pair),
            pltpu.SemaphoreType.DMA((3 * count + 4 + parts,)),
        ],
        compiler_params=params(),
        cost_estimate=cost(2 * rows * width * (2 * inner + width), 4 * inner * (width + rows)),
        name="middle_grads",
    )(offs, who, upstream, gain, *w_out, *w_gate, *w_up, *mix, dg, du, mid)


def output_kernel(count, offs, act_ref, mid_ref, *refs):
    pieces, (res, wd, sems) = refs[:count], refs[count:]
    wait(Mover(sems).pieces(offs, pieces, wd))

    def forth(j, _):
        at = pl.ds(pl.multiple_of(j * TILE, TILE), TILE)
        res[:, at] = (mid_ref[:, at] + mm(act_ref[...], wd[:, at])).astype(bf16)
        return 0

    lax.fori_loop(0, wd.shape[1] // TILE, forth, 0, unroll=True)


def output(offs, act, mid, w_down):
    rows, width = mid.shape
    count = len(w_down)
    inner = act.shape[1]
    return pl.pallas_call(
        functools.partial(output_kernel, count),
        out_shape=like(rows, width),
        in_specs=[smem()] + [vmem()] * 2 + [anywhere()] * count,
        out_specs=vmem(),
        scratch_shapes=[scratch(inner, width), pltpu.SemaphoreType.DMA((count,))],
        compiler_params=params(),
        cost_estimate=cost(2 * rows * width * inner, 2 * inner * (width + rows)),
        name="output",
    )(offs, act, mid, *w_down)


def tail_kernel(count, cols, offs, who, dq_ref, own_ref, cos_ref, sin_ref, hid_ref, x_ref, gain_ref, dmid_ref, fgain_ref, *refs):
    pieces = refs[:count]
    grad_ref, *outs = refs[count:]
    *outs, w, raw, gain_cols, sems = outs
    mover = Mover(sems)
    w_in = mover.columns(offs, pieces, w)
    cosine, sine = cos_ref[...], -sin_ref[...]
    raw[0:QCOLS, :] = dq_ref[...].astype(bf16)
    raw[QCOLS:cols, :] = own_ref[...]
    raw[cols:, :] = jnp.zeros((raw.shape[0] - cols, raw.shape[1]), bf16)
    for r in range(QRANK):
        at = BQ + r * HDIM
        one, two = turn(dq_ref[at : at + HDIM, :], cosine, sine)
        raw[at : at + HALF, :] = one.astype(bf16)
        raw[at + HALF : at + HDIM, :] = two.astype(bf16)
    for r in range(KRANK):
        at = BK + r * HDIM
        one, two = turn(own_ref[at : at + HDIM, :].astype(f32), cosine, sine)
        raw[QCOLS + at : QCOLS + at + HALF, :] = one.astype(bf16)
        raw[QCOLS + at + HALF : QCOLS + at + HDIM, :] = two.astype(bf16)
    draw = jnp.transpose(raw[...])
    wait(w_in)
    xf = x_ref[...].astype(f32)
    scale = lax.rsqrt(jnp.mean(xf * xf, axis=-1, keepdims=True) + EPS)
    dhid = mm(draw[:, 0:cols], w[...])
    gain_grad, part = norm_back(dhid, xf * scale, scale, gain_ref[...])
    grad_ref[...] = dmid_ref[...] + part
    line = lax.broadcasted_iota(jnp.int32, (128, gain_grad.shape[1]), 0)
    both = jnp.where(line == 0, gain_grad, jnp.where(line == 1, fgain_ref[0:1, :], 0.0))
    gain_cols[...] = jnp.transpose(both)
    count_out, wide, rows = outs[0].shape
    for flip in range(2 * count_out):
        at = pl.ds(pl.multiple_of((who[0] ^ flip) * rows, 16), rows)
        out = outs[flip % 2]
        out[flip // 2, 0:cols, :] = mm(raw[0:cols, :], hid_ref[at, :], NT).astype(bf16)
        out[flip // 2, cols:wide, :] = jnp.transpose(gain_cols[at, :])[0 : wide - cols].astype(bf16)


def tail(offs, who, dq, own, cosine, sine, hidT, x, gain, dmid, fgain, w_fac, cols, parts):
    rows, width = x.shape
    wide = (cols // 128 + 1) * 128
    count = len(w_fac)
    shard = (parts // 2, wide, width // parts)
    return pl.pallas_call(
        functools.partial(tail_kernel, count, cols),
        out_shape=[like(rows, width, dtype=f32)] + [like(*shard)] * 2,
        in_specs=[smem()] * 2 + [vmem()] * 9 + [anywhere()] * count,
        out_specs=[vmem()] * 3,
        scratch_shapes=[
            scratch(cols, width),
            scratch(wide, rows),
            scratch(width, 128, dtype=f32),
            pltpu.SemaphoreType.DMA((count,)),
        ],
        compiler_params=params(),
        cost_estimate=cost(4 * rows * width * cols, 4 * width * (cols + 3 * rows)),
        name="tail",
    )(offs, who, dq, own, cosine, sine, hidT, x, gain, dmid, fgain, *w_fac)


def partner(values, axis, flip):
    size = lax.axis_size(axis)
    return lax.ppermute(values, axis, [(i, i ^ flip) for i in range(size)])


def after(value, *earlier):
    if not earlier:
        return value
    return lax.optimization_barrier((value, *earlier))[0]


def places(pieces, rows, half):
    me = lax.axis_index("grp")
    at = []
    for flip, which in pieces:
        row = (me ^ flip) * rows
        at += [row if which is None else row + which * half, 0]
    return jnp.stack([jnp.asarray(v, jnp.int32) for v in at])


def total(*terms):
    got = terms[0].astype(f32)
    for term in terms[1:]:
        got = got + term.astype(f32)
    return got.astype(bf16)


def add_pairs_kernel(*refs):
    mine, other = refs[-2:]
    at = 0
    for keep, got in zip(refs[:-2:2], refs[1:-2:2]):
        cols = slice(at, at + keep.shape[2])
        mine[:, cols] = total(keep[0], got[0])
        other[:, cols] = total(keep[1], got[1])
        at += keep.shape[2]


def add_pairs(groups):
    rows = groups[0][0].shape[1]
    wide = sum(keep.shape[2] for keep, _ in groups)
    steps = next(n for n in (4, 2, 1) if n == 1 or (rows % (16 * n) == 0 and rows * wide > 2**19))
    out = pl.BlockSpec((rows // steps, wide), lambda i: (i, 0))
    terms = [term for group in groups for term in group]
    return pl.pallas_call(
        add_pairs_kernel,
        grid=(steps,),
        out_shape=[like(rows, wide)] * 2,
        in_specs=[pl.BlockSpec((2, rows // steps, v.shape[2]), lambda i: (0, i, 0)) for v in terms],
        out_specs=[out] * 2,
        compiler_params=params(),
        cost_estimate=cost(1, 1),
        name="add_pairs",
    )(*terms)


def eighths(value):
    return value.reshape(8, value.shape[0] // 8, value.shape[1])


def halve_body(place, one, two, keep, send):
    for i in range(4):
        at = place[0] ^ ((i >> 1) * place[2]) ^ ((i & 1) * place[3])
        keep[i] = total(one[at], two[at])
        send[i] = total(one[at ^ place[1]], two[at ^ place[1]])


def halve(place, one, two):
    one, two = eighths(one), eighths(two)
    return pl.pallas_call(
        halve_body,
        out_shape=[like(4, *one.shape[1:])] * 2,
        in_specs=[smem()] + [vmem()] * 2,
        out_specs=[vmem()] * 2,
        compiler_params=params(),
        cost_estimate=cost(1, 1),
        name="halve",
    )(place, one, two)


def batch_kernel(tasks, place, *refs):
    ins, outs = refs[: 2 * len(tasks)], list(refs[2 * len(tasks) :])
    for i, (kind, flip) in enumerate(tasks):
        one, two = ins[2 * i : 2 * i + 2]
        out = outs.pop(0)
        if kind == "halve":
            halve_body(place, one, two, out, outs.pop(0))
        elif kind == "split":
            half = out.shape[0]
            out[...] = total(one[:half], two[:half])
            outs.pop(0)[...] = total(one[half:], two[half:])
        elif kind == "pair":
            out[...] = total(one[0], two[0])
            outs.pop(0)[...] = total(one[1], two[1])
        elif kind == "join":
            half = one.shape[0]
            out[:half] = one[...]
            out[half:] = two[...]
        elif flip:
            for k in range(out.shape[0]):
                out[k] = total(one[k], two[k ^ flip])
        else:
            out[...] = total(one[...], two[...])


def batch(place, tasks):
    shapes, counts = [], []
    for kind, _, one, _ in tasks:
        first, rest = one.shape[0], one.shape[1:]
        got = {
            "halve": [(first // 2,) + rest] * 2,
            "split": [(first // 2,) + rest] * 2,
            "pair": [rest] * 2,
            "join": [(2 * first,) + rest],
            "sum": [one.shape],
        }[kind]
        shapes += got
        counts.append(len(got))
    outs = pl.pallas_call(
        functools.partial(batch_kernel, [task[:2] for task in tasks]),
        out_shape=[like(*shape) for shape in shapes],
        in_specs=[smem()] + [vmem()] * (2 * len(tasks)),
        out_specs=[vmem()] * len(shapes),
        compiler_params=params(),
        cost_estimate=cost(1, 1),
        name="batch",
    )(place, *[value for task in tasks for value in task[2:]])
    groups = []
    for count in counts:
        groups.append(outs[:count])
        outs = outs[count:]
    return groups


def finish_kernel(widths, place, near, far, *outs):
    _, rows, wide = near.shape
    for side, value in ((0, near), (1, far)):
        for k in range(4):
            at = place[0] ^ (side * place[1]) ^ ((k >> 1) * place[2]) ^ ((k & 1) * place[3])
            row = pl.ds(pl.multiple_of(at * rows, 8), rows)
            col = 0
            for out, cols in zip(outs, widths):
                out[row, :] = value[k, :, col : col + cols].astype(f32)
                col += cols


def finish(place, near, far, widths):
    rows = near.shape[1]
    return pl.pallas_call(
        functools.partial(finish_kernel, widths),
        out_shape=[like(8 * rows, cols, dtype=f32) for cols in widths],
        in_specs=[smem()] + [vmem()] * 2,
        out_specs=[vmem()] * len(widths),
        compiler_params=params(),
        cost_estimate=cost(1, 1),
        name="finish",
    )(place, near, far)


def scatter_all(keep, send):
    me = lax.axis_index("grp")
    both = jnp.stack([keep, send], axis=1)
    both = both.reshape((-1,) + both.shape[2:])
    both = jnp.take(both, jnp.arange(both.shape[0]) ^ me, axis=0)
    return lax.psum_scatter(both, "grp", scatter_dimension=0, tiled=False)


class Order:
    def __init__(self):
        self.last = None
        self.before = ()
        self.tasks = []

    def add(self, kind, flip, one, two, then):
        self.tasks.append(((kind, flip, self.free(one), two), then))

    def flush(self):
        groups = batch(self.place, [task for task, _ in self.tasks])
        for (_, then), group in zip(self.tasks, groups):
            then(*group)
        self.tasks = []

    def __call__(self, value, *earlier):
        earlier = earlier if self.last is None else earlier + (self.last,)
        return after(value, *earlier) if earlier else value

    def phase(self, *results):
        self.before = results
        self.last = None

    def now(self, value, *earlier):
        last = () if self.last is None else (self.last,)
        return after(value, *self.before, *earlier, *last)

    def free(self, value):
        return after(value, *self.before)

    def ran(self, value):
        self.last = value
        return value


BITS = ((1, 2, 4), (2, 1, 4))


def along(values, step):
    reps, parts = lax.axis_size("rep"), lax.axis_size("grp")
    pairs = [
        (r * parts + g, (r ^ BITS[g % 2][step]) * parts + g)
        for r in range(reps)
        for g in range(parts)
    ]
    return lax.ppermute(values, ("rep", "grp"), pairs)


class Chunk:
    def __init__(self, order, place, *pairs):
        self.order, self.place, self.pairs = order, place, pairs

    def core(self):
        send = [pair[1] if len(self.pairs) > 1 else after(pair[1], *self.order.before) for pair in self.pairs]
        self.got = [partner(value, "grp", 1) for value in send]

    def add_core(self):
        keep = [self.order.now(self.pairs[0][0])] + [pair[0] for pair in self.pairs[1:]]
        self.mine, self.other = add_pairs(list(zip(keep, self.got)))
        self.order.ran(self.other)

    def cross(self):
        self.got = partner(self.order.free(self.other), "grp", 2)

    def go(self, step):
        self.got = along(self.order.free(self.other), step)

    def fold(self, step, start=True, alone=True):
        def then(mine, other):
            self.mine, self.other = mine, other
            if start:
                self.got = along(other, step)

        if step == 0 and not alone:
            self.order.add("halve", 0, eighths(self.mine), eighths(self.got), then)
        elif step == 0:
            then(*halve(self.place, self.order.now(self.mine), self.got))
            self.order.ran(self.other)
        else:
            self.order.add("split", 0, self.mine, self.got, then)

    def pair(self):
        def then(mine, other):
            self.mine = mine
            self.got = partner(other, "grp", 2)

        self.order.add("pair", 0, self.pairs[0][0], self.got[0], then)

    def swap(self, step, flip=0):
        def then(mine):
            self.mine = mine
            self.got = along(mine, step)

        self.order.add("sum", flip, self.mine, self.got, then)

    def open(self, step):
        def then(mine):
            self.mine = mine
            self.got = along(mine, step)

        self.order.add("join", 0, self.mine, self.got, then)

    def finish(self, *widths):
        got = finish(self.place, self.order.now(self.mine), self.got, widths)
        self.order.ran(got[0])
        return got


def local(
    layer_input,
    branch,
    attention_gain,
    factor_weight,
    output_weight,
    feed_gain,
    gate_weight,
    up_weight,
    down_weight,
    cotangent,
):
    rows = layer_input.shape[1]
    parts = lax.axis_size("grp")
    me = lax.axis_index("grp")
    prompt_parts = parts // 2
    follows = me >= prompt_parts
    chosen = branch[0, jnp.maximum(me - prompt_parts, 0)]
    limit = jnp.where(follows, chosen, me * rows)
    npc = (limit + rows - 1) // rows
    position = jnp.where(follows, chosen, me * rows) + jnp.arange(rows, dtype=jnp.int32)
    info = jnp.stack([me, npc, limit]).astype(jnp.int32)
    freqs = 10000.0 ** (-jnp.arange(HALF).astype(f32) / HALF)
    phase = freqs[:, None] * position.astype(f32)[None, :]
    cosine, sine = jnp.cos(phase), jnp.sin(phase)

    x = layer_input[0]
    upstream = cotangent[0]
    shard_rows, cols = factor_weight.shape
    own_gains = jnp.stack([attention_gain, feed_gain])
    factor_turned = factor_weight.T
    gather = lambda value: lax.all_gather(value, "grp", axis=0, tiled=True)

    if parts != 4 or lax.axis_size("rep") != 8:
        whole = jnp.zeros((4,), jnp.int32)
        w_out, w_down = [gather(output_weight)], [gather(down_weight)]
        w_fac = [lax.all_gather(factor_turned, "grp", axis=1, tiled=True)]
        w_gate, w_up = [gather(gate_weight)], [gather(up_weight)]
        all_gains = lax.all_gather(own_gains, "grp", axis=1, tiled=True)
        fac, kv_own, hid_one, gains = front(whole, x, cosine, sine, w_fac, [all_gains])
        kv = [lax.all_gather(kv_own, "grp", axis=0, tiled=False)]
        mixed, lse = ([got] for got in attend(info, fac, kv, 0, HEADS))
        mid, hid_two, act, slope, lin, act_rows = feed(
            whole, mixed, x, gains[1:2], w_out, w_gate, w_up
        )
        down_pair = products(info, act_rows, upstream, parts)
        dgate, dup = slopes(whole, upstream, w_down, slope, lin)
        up_pair = products(info, hid_two, dup, parts)
        dmid, fgain, dmix, *out_pair = middle_grads(
            whole, info, upstream, gains[1:2], mixed, w_out, w_gate, w_up, dgate, dup, mid, parts
        )
        gate_pair = products(info, hid_two, dgate, parts)
        result = output(whole, act, mid, w_down)
        dq, *dkv = attend_back(info, fac, kv, dmix, lse, 0, HEADS, ())
        input_grad, *fac_pair = tail(
            whole, info, dq, scatter_all(*dkv), cosine, sine, hid_one, x, gains[0:1], dmid, fgain,
            w_fac, cols, parts,
        )
        pairs = (fac_pair, out_pair, gate_pair, up_pair, down_pair)
        shards = [scatter_all(*pair) for pair in pairs]
        sums = [lax.psum(shard, "rep").astype(f32) for shard in shards]
        fac_grad, out_grad, gate_grad, up_grad, down_grad = sums
    else:
        order = Order()
        low = lax.axis_index("rep") % 2
        even = (lax.axis_index("rep") // 2) % 2
        take = lambda v, which: lax.dynamic_slice_in_dim(v, which * (v.shape[0] // 2), v.shape[0] // 2, 0)
        quarter = places([(k, None) for k in range(4)], shard_rows, 0)
        halves = lambda v, rows: places(
            [(0, None), (1, None), (2, v), (2, 1 - v), (3, v), (3, 1 - v)], rows, rows // 2
        )
        by_side, by_line = halves(low, shard_rows), halves(even, shard_rows)
        by_down = halves(low, down_weight.shape[0])
        grp = lambda value, flip: partner(order.free(value), "grp", flip)
        rep = lambda value, flip: partner(order.free(value), "rep", flip)
        fac_x = partner(factor_turned, "grp", 2)
        fac_c = partner(factor_turned, "grp", 1)
        gains_x = partner(own_gains, "grp", 2)
        gains_c = partner(own_gains, "grp", 1)
        gate_half, up_half = take(gate_weight, low), take(up_weight, even)
        out_half, down_half = take(output_weight, low), take(down_weight, low)
        order.phase(
            fac_x, fac_c, gains_x, gains_c, gate_half, up_half, out_half, down_half
        )
        fac_xc = grp(fac_x, 1)
        gains_xc = grp(gains_x, 1)
        gate_x = grp(gate_half, 2)
        up_c = grp(up_weight, 1)
        gate_c = grp(gate_weight, 1)
        w_fac = [factor_turned, fac_c, fac_x, fac_xc]
        all_gains = [own_gains, gains_c, gains_x, gains_xc]
        fac, kv_own, hid_one, gains = front(
            quarter, order.now(x), cosine, sine, w_fac, all_gains
        )
        kv_x = partner(kv_own, "grp", 2)
        kv_c = partner(kv_own, "grp", 1)
        kv_xc = partner(kv_x, "grp", 1)
        kv = [kv_own, kv_c, kv_x, kv_xc]

        order.phase(gate_x, kv_x, kv_c, kv_xc, up_c, gate_c)
        up_x = grp(up_half, 2)
        out_x = grp(out_half, 2)
        gate_y = rep(gate_x, 1)
        gate_xc = grp(gate_x, 1)
        down_c = grp(down_weight, 1)
        part = HEADS // 2
        heads = [attend(info, order.now(fac), kv, 0, part)]

        order.phase(up_x, out_x, gate_y, gate_xc, down_c, heads[0][0])
        down_x = grp(down_half, 2)
        up_z = rep(up_x, 2)
        up_xc = grp(up_x, 1)
        out_y = rep(out_x, 1)
        gate_yc = grp(gate_y, 1)
        heads.append(attend(info, order.now(fac), kv, part, part))
        mixed, lse = ([got[i] for got in heads] for i in range(2))

        order.phase(down_x, up_z, up_xc, out_y, gate_yc, heads[1][0])
        up_zc = grp(up_z, 1)
        out_c = grp(output_weight, 1)
        out_xc = grp(out_x, 1)
        out_yc = grp(out_y, 1)
        w_out = [output_weight, out_c, out_x, out_y, out_xc, out_yc]
        w_gate = [gate_weight, gate_c, gate_x, gate_y, gate_xc, gate_yc]
        w_up = [up_weight, up_c, up_x, up_z, up_xc, up_zc]
        offs_feed = jnp.concatenate([by_side, by_line])

        order.phase(up_zc, out_c, out_xc, out_yc)
        odd = me % 2
        place = jnp.stack([lax.axis_index("rep"), 1 + odd, 2 - odd, jnp.full_like(odd, 4)])
        place = place.astype(jnp.int32)
        order.place = place
        chunk = functools.partial(Chunk, order, place)
        down_y = rep(down_x, 1)
        down_xc = grp(down_x, 1)
        mid, hid_two, act, slope, lin, act_rows = feed(
            offs_feed, mixed, order.now(x), gains[1:2], w_out, w_gate, w_up
        )

        order.phase(down_y, down_xc, mid)
        down_yc = grp(down_y, 1)
        w_down = [down_weight, down_c, down_x, down_y, down_xc, down_yc]
        down = chunk(products(info, order.now(act_rows), upstream, parts))

        order.phase(down_yc, down.pairs[0][0])
        down.core()
        dgate, dup = slopes(by_down, order.now(upstream), w_down, slope, lin)

        order.phase(*down.got, dgate)
        down.add_core()
        down.cross()
        third = 1024
        cuts = (third, third, up_weight.shape[1] - 2 * third)
        terms = products(info, order.free(hid_two), dup, parts, cuts)
        up = chunk(*[terms[i : i + 2] for i in range(0, 6, 2)])
        up.core()
        dmid, fgain, dmix, *out_pair = middle_grads(
            offs_feed, info, order.free(upstream), gains[1:2], mixed, w_out, w_gate, w_up,
            dgate, dup, mid, parts,
        )
        out = chunk(out_pair)
        out.core()
        gate = chunk(products(info, after(hid_two, dmix), dgate, parts))
        part = 1
        state = attend_back(info, fac, kv, after(dmix, gate.pairs[0][0]), lse, 0, part, ())

        order.phase(down.got, *up.got, *out.got, state[0])
        both = chunk(*up.pairs, *out.pairs)
        both.got = up.got + out.got
        both.add_core()
        both.cross()
        down.fold(0)
        gate.core()
        dq, *terms = attend_back(info, fac, kv, order.free(dmix), lse, part, HEADS - part, state)

        order.phase(both.got, down.got, *gate.got, dq)
        dkv = chunk(terms)
        dkv.core()
        down.fold(1)
        order.flush()
        both.fold(0, start=False)

        order.phase(*dkv.got, down.got, both.other)
        both.go(0)
        dkv.pair()
        down.fold(2)
        order.flush()
        gate.add_core()

        order.phase(dkv.got, down.got, gate.other)
        gate.cross()
        sums = []
        order.add("sum", 0, dkv.mine, dkv.got, sums.append)
        down.swap(2)
        order.flush()
        input_grad, *terms = tail(
            quarter, info, dq, sums[0], cosine, sine, hid_one, x, gains[0:1], dmid, fgain,
            w_fac, cols, parts,
        )

        order.phase(both.got, down.got, input_grad)
        factor = chunk(terms)
        factor.core()
        both.fold(1)
        down.open(1)
        order.flush()

        order.phase(*factor.got, both.got, down.got)
        factor.pair()
        both.fold(2)
        down.open(0)
        order.flush()
        gate.got = after(gate.got, factor.mine)
        gate.fold(0)

        order.phase(factor.got, both.got, down.got, gate.got)
        factor.fold(0, alone=False)
        gate.fold(1)
        both.swap(2)
        order.flush()
        (down_grad,) = down.finish(down_weight.shape[1])

        order.phase(factor.got, both.got, gate.got, down_grad)
        factor.swap(1)
        gate.fold(2)
        both.open(1)
        order.flush()

        order.phase(factor.got, both.got, gate.got)
        factor.swap(2, 2)
        gate.swap(2)
        both.open(0)
        order.flush()
        result = output(by_down, order.free(act), mid, w_down)

        order.phase(factor.got, both.got, gate.got, result)
        factor.swap(0, 1)
        gate.open(1)
        order.flush()
        up_grad, out_grad = both.finish(up_weight.shape[1], output_weight.shape[1])

        order.phase(factor.got, gate.got, up_grad)
        gate.open(0)
        order.flush()
        (fac_grad,) = factor.finish(shard_rows)

        order.phase(gate.got, fac_grad)
        (gate_grad,) = gate.finish(gate_weight.shape[1])
    return (
        result[None],
        input_grad[None],
        fac_grad[cols],
        fac_grad[:cols].T,
        out_grad,
        fac_grad[cols + 1],
        gate_grad,
        up_grad,
        down_grad,
    )


def solution(mesh):
    in_specs = (
        P("rep", "grp", None),
        P("rep", None),
        P("grp"),
        P("grp", None),
        P("grp", None),
        P("grp"),
        P("grp", None),
        P("grp", None),
        P("grp", None),
        P("rep", "grp", None),
    )
    out_specs = (
        P("rep", "grp", None),
        P("rep", "grp", None),
        P("grp"),
        P("grp", None),
        P("grp", None),
        P("grp"),
        P("grp", None),
        P("grp", None),
        P("grp", None),
    )
    return jax.shard_map(local, mesh=mesh, in_specs=in_specs, out_specs=out_specs, check_vma=False)
```
